32 devices in a mesh: seq: 8 (over z, x), head: 4 (over y, core).
Axes of the slice: x: 2, y: 2, z: 4, core: 2. Of those that a mesh axis runs over, the one named last changes fastest.
Arguments:
- tokens: bfloat16 [8192, 2048], P('seq'), may hold values from -12 to 12
- cotangent: bfloat16 [8192, 2048], P('seq'), may hold values from -6 to 6
- norm1_gain: float32 [2048], P('seq'), may hold values from 0.5 to 1.5
- w_query: float32 [2048, 2048], P('seq', 'head'), may hold values from -0.125 to 0.125
- w_key: float32 [2048, 2048], P('seq', 'head'), may hold values from -0.125 to 0.125
- w_value: float32 [2048, 4096], P('seq', 'head'), may hold values from -0.125 to 0.125
- w_gate_out: float32 [2048, 4096], P('seq', 'head'), may hold values from -0.125 to 0.125
- w_alpha: float32 [2048, 16], P('seq', 'head'), may hold values from -0.125 to 0.125
- w_beta: float32 [2048, 16], P('seq', 'head'), may hold values from -1 to 1
- conv_query: float32 [4, 16, 128], P(None, 'head', 'seq'), may hold values from -4 to 4
- conv_key: float32 [4, 16, 128], P(None, 'head', 'seq'), may hold values from -4 to 4
- conv_value: float32 [4, 16, 256], P(None, 'head', 'seq'), may hold values from -4 to 4
- a_log: float32 [16], P('seq'), may hold values from -11 to -4
- dt_bias: float32 [16], P('seq'), may hold values from -3 to 1
- out_gain: float32 [256], P('seq'), may hold values from 0.5 to 1.5
- w_out: float32 [4096, 2048], P('head', 'seq'), may hold values from -0.1875 to 0.1875
- norm2_gain: float32 [2048], P('seq'), may hold values from 0.5 to 1.5
- w_gate: float32 [2048, 5504], P('seq', 'head'), may hold values from -0.125 to 0.125
- w_up: float32 [2048, 5504], P('seq', 'head'), may hold values from -0.125 to 0.125
- w_down: float32 [5504, 2048], P('head', 'seq'), may hold values from -0.125 to 0.125
Outputs:
- out: bfloat16 [8192, 2048], P('seq')
- grad_tokens: float32 [8192, 2048], P('seq')
- grad_norm1_gain: float32 [2048], P('seq')
- grad_w_query: float32 [2048, 2048], P('seq', 'head')
- grad_w_key: float32 [2048, 2048], P('seq', 'head')
- grad_w_value: float32 [2048, 4096], P('seq', 'head')
- grad_w_gate_out: float32 [2048, 4096], P('seq', 'head')
- grad_w_alpha: float32 [2048, 16], P('seq', 'head')
- grad_w_beta: float32 [2048, 16], P('seq', 'head')
- grad_conv_query: float32 [4, 16, 128], P(None, 'head', 'seq')
- grad_conv_key: float32 [4, 16, 128], P(None, 'head', 'seq')
- grad_conv_value: float32 [4, 16, 256], P(None, 'head', 'seq')
- grad_a_log: float32 [16], P('seq')
- grad_dt_bias: float32 [16], P('seq')
- grad_out_gain: float32 [256], P('seq')
- grad_w_out: float32 [4096, 2048], P('head', 'seq')
- grad_norm2_gain: float32 [2048], P('seq')
- grad_w_gate: float32 [2048, 5504], P('seq', 'head')
- grad_w_up: float32 [2048, 5504], P('seq', 'head')
- grad_w_down: float32 [5504, 2048], P('head', 'seq')
The draws below stay inside these ranges and needn't reach their ends.
All inputs are finite; a program needn't handle non-finite values.
Results may differ from the reference program's by a relative error of at most 0.03.
Values may be sent and summed in bfloat16 or wider, within the bound.
No kernel may reach another device: no remote copies, remote signals or barrier semaphores. Data moves between devices by JAX's collectives and lax.ppermute only.
A program may use at most 512 MiB of HBM per device.

```python
import math
import jax
import jax.numpy as jnp
from jax import lax

D = 2048
HEADS = 16
DK = 128
DV = 256
FF = 5504
BLOCK = 64
KEYS = 2048
VALS = 4096
TOKENS = 8192


def common_mean(key):
    return jnp.clip(jax.random.normal(key, (D,), jnp.float32), -3.0, 3.0)


def draw_tokens(key, part):
    mean_row = common_mean(key)
    key = jax.random.fold_in(key, 11)
    jitter_key = jax.random.fold_in(key, 0)
    jitter = jnp.clip(jax.random.normal(jitter_key, (TOKENS, D), jnp.float32), -4.0, 4.0)
    values = 0.5 * mean_row[None, :] + jitter
    return values.astype(jnp.bfloat16)


def draw_w_beta(key, part):
    mean_row = common_mean(key)
    key = jax.random.fold_in(key, 12)
    scale_key, jitter_key = jax.random.split(key)
    offsets = jnp.exp(jax.random.uniform(scale_key, (HEADS,), jnp.float32, math.log(3.0), math.log(10.0)))
    jitter = jnp.clip(jax.random.normal(jitter_key, (D, HEADS), jnp.float32), -4.0, 4.0) * (0.5 / math.sqrt(D))
    return -mean_row[:, None] * offsets[None, :] / D + jitter


def block_scale(own_key, extent, pieces, least, top_value):
    def one(dim, shards_of):
        steps = jax.random.uniform(jax.random.fold_in(jax.random.fold_in(own_key, 6), dim), (shards_of,), jnp.float32, least / len(pieces), top_value / len(pieces))
        return jnp.repeat(jnp.exp(steps), extent[dim] // shards_of).reshape((-1,) + (1,) * (len(extent) - dim - 1))

    level = one(*pieces[0])
    for cut in pieces[1:]:
        level = level * one(*cut)
    return level


def noise(own_key, dims, spread, reach, cuts=(), kind=jnp.bfloat16):
    level = block_scale(own_key, dims, cuts, -0.22, 0.18) if cuts else 1.0
    drawn = jax.random.normal(own_key, dims, jnp.float32) * spread * level
    return jnp.minimum(jnp.maximum(drawn, -reach), reach).astype(kind)


def setup_inputs(seed: int = 0) -> dict:
    keys = jax.random.split(jax.random.key(seed), 21)
    tokens = draw_tokens(jax.random.fold_in(keys[20], 71), 0)
    cotangent = noise(keys[1], (TOKENS, D), 1.0, 6.0, ((0, 8),))
    norm1_gain = jnp.clip(1.0 + 0.1 * jax.random.normal(keys[2], (D,), jnp.float32), 0.5, 1.5)
    w_query = noise(keys[3], (D, KEYS), D ** -0.5, 0.125, ((0, 8), (1, 4)), jnp.float32)
    w_key = noise(keys[4], (D, KEYS), D ** -0.5, 0.125, ((0, 8), (1, 4)), jnp.float32)
    w_value = noise(keys[5], (D, VALS), D ** -0.5, 0.125, ((0, 8), (1, 4)), jnp.float32)
    w_gate_out = noise(keys[6], (D, VALS), D ** -0.5, 0.125, ((0, 8), (1, 4)), jnp.float32)
    w_alpha = noise(keys[7], (D, HEADS), D ** -0.5, 0.125, ((0, 8), (1, 4)), jnp.float32)
    w_beta = draw_w_beta(jax.random.fold_in(keys[20], 71), 0)
    conv_query = noise(keys[9], (4, HEADS, DK), 2 ** -0.5, 4.0, ((1, 4), (2, 8)), jnp.float32)
    conv_key = noise(keys[10], (4, HEADS, DK), 2 ** -0.5, 4.0, ((1, 4), (2, 8)), jnp.float32)
    conv_value = noise(keys[11], (4, HEADS, DV), 2 ** -0.5, 4.0, ((1, 4), (2, 8)), jnp.float32)
    a_log = jnp.clip(-11.0 + 7.0 * jax.random.uniform(keys[12], (HEADS,), jnp.float32) ** block_scale(keys[12], (HEADS,), ((0, 8),), -0.2, 0.2), -11.0, -4.0)
    dt_bias = jnp.clip(-3.0 + 4.0 * jax.random.uniform(keys[13], (HEADS,), jnp.float32) ** block_scale(keys[13], (HEADS,), ((0, 8),), -0.2, 0.2), -3.0, 1.0)
    out_gain = jnp.clip(1.0 + 0.1 * jax.random.normal(keys[14], (DV,), jnp.float32), 0.5, 1.5)
    w_out = noise(keys[15], (VALS, D), (VALS // 4) ** -0.5, 0.1875, ((0, 4), (1, 8)), jnp.float32)
    norm2_gain = jnp.clip(1.0 + 0.1 * jax.random.normal(keys[16], (D,), jnp.float32), 0.5, 1.5)
    w_gate = noise(keys[17], (D, FF), D ** -0.5, 0.125, ((0, 8), (1, 4)), jnp.float32)
    w_up = noise(keys[18], (D, FF), D ** -0.5, 0.125, ((0, 8), (1, 4)), jnp.float32)
    w_down = noise(keys[19], (FF, D), (FF // 3) ** -0.5, 0.125, ((0, 4), (1, 8)), jnp.float32)
    return {"tokens": tokens, "cotangent": cotangent, "norm1_gain": norm1_gain, "w_query": w_query, "w_key": w_key, "w_value": w_value, "w_gate_out": w_gate_out, "w_alpha": w_alpha, "w_beta": w_beta, "conv_query": conv_query, "conv_key": conv_key, "conv_value": conv_value, "a_log": a_log, "dt_bias": dt_bias, "out_gain": out_gain, "w_out": w_out, "norm2_gain": norm2_gain, "w_gate": w_gate, "w_up": w_up, "w_down": w_down}


highest = lax.Precision.HIGHEST
eps_norm = 1e-06

@jax.custom_vjp
def low(v):
    return lax.optimization_barrier(v.astype(jnp.bfloat16)).astype(jnp.float32)

@jax.custom_vjp
def low_back(v):
    return v

def low_keep(v):
    return (low(v), None)

def low_pass(kept, grad):
    return (grad,)

def back_keep(v):
    return (v, None)

def back_low(kept, grad):
    return (low(grad),)
low.defvjp(low_keep, low_pass)
low_back.defvjp(back_keep, back_low)

def matmul(left_side, right_side):
    return jnp.dot(left_side, right_side, precision=highest, preferred_element_type=jnp.float32)

def rms_scale(values, scale_gain):
    return values * lax.rsqrt(lax.optimization_barrier(jnp.mean(values * values, axis=-1, keepdims=True)) + eps_norm) * scale_gain

def unit_rows(values):
    return values * lax.rsqrt(lax.optimization_barrier(jnp.sum(values * values, axis=-1, keepdims=True)) + eps_norm)

def causal_conv(projected, filters):
    length = projected.shape[0]
    padded = jnp.concatenate([jnp.zeros((3, projected.shape[1]), jnp.float32), projected], axis=0)
    running = filters[0] * padded[0:length]
    for offset in range(1, 4):
        running = running + filters[offset] * padded[offset:offset + length]
    return jax.nn.silu(running)

def token_block(state_in, block_data):

    def token_step(state_now, token_item):
        query_row, key_row, value_row, decay_log, beta_row = token_item
        decay_now = jnp.exp(decay_log)
        predicted = jnp.einsum('hvk,hk->hv', state_now, key_row, precision=highest)
        error_term = beta_row[:, None] * (value_row - decay_now[:, None] * predicted)
        state_now = decay_now[:, None, None] * state_now + error_term[:, :, None] * key_row[:, None, :]
        output_row = jnp.einsum('hvk,hk->hv', state_now, query_row, precision=highest)
        return (state_now, output_row)
    return lax.scan(token_step, state_in, block_data)

def delta_rule(queries, key_rows, values, log_decay, strength):
    length = queries.shape[0]
    blocks = length // BLOCK
    members = tuple((member.reshape((blocks, BLOCK) + member.shape[1:]) for member in (queries, key_rows, values, log_decay, strength)))
    initial = jnp.zeros((HEADS, DV, DK), jnp.float32)
    final_state, outputs = lax.scan(jax.checkpoint(token_block), initial, members)
    return outputs.reshape(length, HEADS, DV)

def layer_forward(inputs, norm1_gain, w_query, w_key, w_value, w_gate_out, w_alpha, w_beta, conv_query, conv_key, conv_value, a_log, dt_bias, out_gain, w_out, norm2_gain, w_gate, w_up, w_down):
    length = inputs.shape[0]
    normed1 = low(rms_scale(inputs, low(norm1_gain)))
    proj_query = low_back(low(matmul(normed1, low(w_query))))
    proj_key = low_back(low(matmul(normed1, low(w_key))))
    proj_value = low_back(low(matmul(normed1, low(w_value))))
    gate_pre = low_back(matmul(normed1, low(w_gate_out)))
    alpha_pre = low_back(matmul(normed1, low(w_alpha)))
    beta_pre = low_back(matmul(normed1, low(w_beta)))
    queries = unit_rows(causal_conv(proj_query, low(conv_query).reshape(4, KEYS)).reshape(length, HEADS, DK)) * DK ** (-0.5)
    key_rows = unit_rows(causal_conv(proj_key, low(conv_key).reshape(4, KEYS)).reshape(length, HEADS, DK))
    values = causal_conv(proj_value, low(conv_value).reshape(4, VALS)).reshape(length, HEADS, DV)
    log_decay = -jnp.exp(low(a_log)) * jax.nn.softplus(alpha_pre + low(dt_bias))
    strength = jax.nn.sigmoid(beta_pre)
    outputs = delta_rule(queries, key_rows, values, log_decay, strength)
    gated_out = low(rms_scale(outputs, low(out_gain)) * jax.nn.silu(gate_pre).reshape(length, HEADS, DV)).reshape(length, VALS)
    attention = low_back(matmul(gated_out, low(w_out)))
    hidden_state = inputs + attention
    normed2 = low(rms_scale(hidden_state, low(norm2_gain)))
    gate_act = low_back(matmul(normed2, low(w_gate)))
    up_act = low_back(matmul(normed2, low(w_up)))
    mixed_hidden = low(jax.nn.silu(gate_act) * up_act)
    branch = low_back(matmul(mixed_hidden, low(w_down)))
    return hidden_state + branch

def reference(tokens, cotangent, norm1_gain, w_query, w_key, w_value, w_gate_out, w_alpha, w_beta, conv_query, conv_key, conv_value, a_log, dt_bias, out_gain, w_out, norm2_gain, w_gate, w_up, w_down):
    primal, pullback = jax.vjp(layer_forward, tokens.astype(jnp.float32), norm1_gain, w_query, w_key, w_value, w_gate_out, w_alpha, w_beta, conv_query, conv_key, conv_value, a_log, dt_bias, out_gain, w_out, norm2_gain, w_gate, w_up, w_down)
    gradients = pullback(cotangent.astype(jnp.float32))
    return (primal.astype(jnp.bfloat16), gradients[0], gradients[1], gradients[2], gradients[3], gradients[4], gradients[5], gradients[6], gradients[7], gradients[8], gradients[9], gradients[10], gradients[11], gradients[12], gradients[13], gradients[14], gradients[15], gradients[16], gradients[17], gradients[18])
```

```python
import functools
import jax
import jax.numpy as jnp
from jax import lax
from jax.experimental import pallas as pl
from jax.experimental.pallas import tpu as pltpu

ROWS = 128
KEY = 128
VAL = 256
HALO = 16
eps_norm = 1e-06
f32 = jnp.float32
bf16 = jnp.bfloat16


def mm(a, b):
    return lax.dot_general(
        a.astype(bf16), b.astype(bf16), (((1,), (0,)), ((), ())), preferred_element_type=f32
    )


def mm_nt(a, b):
    return lax.dot_general(
        a.astype(bf16), b.astype(bf16), (((1,), (1,)), ((), ())), preferred_element_type=f32
    )


def mm_tn(a, b):
    return lax.dot_general(
        a.astype(bf16), b.astype(bf16), (((0,), (0,)), ((), ())), preferred_element_type=f32
    )


def mm_full(a, b):
    return lax.dot_general(
        a, b, (((1,), (0,)), ((), ())), precision=lax.Precision.HIGHEST, preferred_element_type=f32
    )


def sigmoid(x):
    return 1.0 / (1.0 + jnp.exp(-x))


def softplus(x):
    return jnp.maximum(x, 0.0) + jnp.log(1.0 + jnp.exp(-jnp.abs(x)))


def positions():
    rows = lax.broadcasted_iota(jnp.int32, (ROWS, ROWS), 0)
    cols = lax.broadcasted_iota(jnp.int32, (ROWS, ROWS), 1)
    return rows, cols


def decay_terms(heads, ab, par):
    rows, cols = positions()
    log_decay = -par[0:1, :] * softplus(ab + par[1:2, :])
    running = mm_full((rows >= cols).astype(f32), log_decay)
    return log_decay, running, running.T, sigmoid(ab)


def ratio_of(running, running_rows, h, rows, cols):
    gap = running[:, h : h + 1] - running_rows[h : h + 1, :]
    return jnp.where(rows >= cols, jnp.exp(jnp.where(rows >= cols, gap, 0.0)), 0.0)


def conv_at(xs_ref, taps_ref, lo, width):
    total = taps_ref[0:1, lo : lo + width] * xs_ref[HALO - 3 : HALO - 3 + ROWS, lo : lo + width]
    for i in range(1, 4):
        total = total + taps_ref[i : i + 1, lo : lo + width] * (
            xs_ref[HALO - 3 + i : HALO - 3 + i + ROWS, lo : lo + width]
        )
    return total


def forward_kernel(heads, proj_ref, edge_ref, taps_ref, ab_ref, par_ref,
                   value_ref, ident_ref, inv_ref, state_ref, final_ref, xs_ref, s_ref):
    step = pl.program_id(0)
    keys = heads * KEY

    @pl.when(step == 0)
    def _():
        xs_ref[0:HALO, :] = edge_ref[...].astype(f32)
        r, c = positions()
        for h in range(heads):
            s_ref[h, :, 0:VAL] = jnp.zeros((KEY, VAL), f32)
            s_ref[h, :, VAL:] = (r == c).astype(f32)

    @pl.when(step > 0)
    def _():
        xs_ref[0:HALO, :] = xs_ref[ROWS : ROWS + HALO, :]

    xs_ref[HALO : HALO + ROWS, :] = proj_ref[...].astype(f32)
    rows, cols = positions()
    log_decay, running, running_rows, strength = decay_terms(heads, ab_ref[...], par_ref[...])
    every = range(heads)
    q, k, v, ratio, a, p, t, beta, grow = [], [], [], [], [], [], [], [], []
    for h in every:
        u = conv_at(xs_ref, taps_ref, h * KEY, KEY)
        u = u * sigmoid(u)
        q.append(u * (lax.rsqrt(jnp.sum(u * u, axis=1, keepdims=True) + eps_norm) * KEY**-0.5))
        w = conv_at(xs_ref, taps_ref, keys + h * KEY, KEY)
        w = w * sigmoid(w)
        k.append(w * lax.rsqrt(jnp.sum(w * w, axis=1, keepdims=True) + eps_norm))
        x = conv_at(xs_ref, taps_ref, 2 * keys + h * VAL, VAL)
        v.append(x * sigmoid(x))
        beta.append(strength[:, heads + h : heads + h + 1])
        grow.append(jnp.exp(running[:, h : h + 1]))
    for h in every:
        ratio.append(ratio_of(running, running_rows, h, rows, cols))
        gram = mm_nt(k[h], k[h])
        a.append(jnp.where(rows > cols, ratio[h] * gram, 0.0) * beta[h])
        p.append(ratio[h] * mm_nt(q[h], k[h]))
    for h in every:
        first = (rows // 2 == cols // 2) & (rows > cols)
        t.append((rows == cols).astype(f32) - jnp.where(first, a[h], 0.0))
    b = 2
    while b < ROWS:
        low = (rows // (2 * b) == cols // (2 * b)) & ((rows // b) % 2 == 1) & ((cols // b) % 2 == 0)
        inner = [mm(jnp.where(low, a[h], 0.0), t[h]) for h in every]
        t = [t[h] - mm(t[h], inner[h]) for h in every]
        b *= 2
    uw = [
        mm(t[h], jnp.concatenate([beta[h] * v[h], (beta[h] * grow[h]) * k[h]], axis=1))
        for h in every
    ]
    for h in every:
        inv_ref[:, h * KEY : (h + 1) * KEY] = t[h].astype(bf16)
        state_ref[h] = s_ref[h].astype(bf16)
    for h in every:
        state = s_ref[h]
        pred = mm(uw[h][:, VAL:], state)
        err = jnp.concatenate([uw[h][:, :VAL] - pred[:, :VAL], -pred[:, VAL:]], axis=1)
        out = grow[h] * mm(q[h], state) + mm(p[h], err)
        value_ref[:, h * VAL : (h + 1) * VAL] = out[:, :VAL]
        ident_ref[:, h * KEY : (h + 1) * KEY] = out[:, VAL:].astype(bf16)
        end = running[ROWS - 1 : ROWS, h : h + 1]
        tail = jnp.exp(end - running[:, h : h + 1]) * k[h]
        s_ref[h] = jnp.exp(end) * state + mm_tn(tail, err)

    @pl.when(step == pl.num_programs(0) - 1)
    def _():
        final_ref[...] = s_ref[...]


def delta_forward(proj, edge, taps, ab, par):
    tokens = proj.shape[0]
    heads = proj.shape[1] // (2 * KEY + VAL)
    keys, vals = heads * KEY, heads * VAL
    blocks = tokens // ROWS
    width = proj.shape[1]
    whole = lambda *shape: pl.BlockSpec(shape, lambda c: (0,) * len(shape))
    return pl.pallas_call(
        functools.partial(forward_kernel, heads),
        grid=(blocks,),
        in_specs=[
            pl.BlockSpec((ROWS, width), lambda c: (c, 0)),
            whole(HALO, width),
            whole(8, width),
            pl.BlockSpec((ROWS, 128), lambda c: (c, 0)),
            whole(8, 128),
        ],
        out_specs=[
            pl.BlockSpec((ROWS, vals), lambda c: (c, 0)),
            pl.BlockSpec((ROWS, keys), lambda c: (c, 0)),
            pl.BlockSpec((ROWS, keys), lambda c: (c, 0)),
            pl.BlockSpec((None, heads, KEY, VAL + KEY), lambda c: (c, 0, 0, 0)),
            whole(heads, KEY, VAL + KEY),
        ],
        out_shape=[
            jax.ShapeDtypeStruct((tokens, vals), f32),
            jax.ShapeDtypeStruct((tokens, keys), bf16),
            jax.ShapeDtypeStruct((tokens, keys), bf16),
            jax.ShapeDtypeStruct((blocks, heads, KEY, VAL + KEY), bf16),
            jax.ShapeDtypeStruct((heads, KEY, VAL + KEY), f32),
        ],
        scratch_shapes=[
            pltpu.VMEM((HALO + ROWS, width), f32),
            pltpu.VMEM((heads, KEY, VAL + KEY), f32),
        ],
        compiler_params=pltpu.CompilerParams(
            dimension_semantics=("arbitrary",), vmem_limit_bytes=48 * 2**20
        ),
    )(proj, edge, taps, ab, par)


def output_kernel(heads, value_ref, ident_ref, state_ref, gate_ref, gain_ref, out_ref, gated_ref):
    for h in range(heads):
        span = slice(h * VAL, (h + 1) * VAL)
        out = value_ref[:, span] + mm(ident_ref[:, h * KEY : (h + 1) * KEY], state_ref[h])
        out_ref[:, span] = out
        gate = gate_ref[:, span]
        unit = out * lax.rsqrt(jnp.mean(out * out, axis=1, keepdims=True) + eps_norm)
        gated_ref[:, span] = (unit * gain_ref[0:1, :] * (gate * sigmoid(gate))).astype(bf16)


def gated_outputs(value_out, ident, state_in, gate_pre, gain):
    tokens, vals = value_out.shape
    heads = vals // VAL
    rows = 256
    by_rows = lambda width: pl.BlockSpec((rows, width), lambda c: (c, 0))
    return pl.pallas_call(
        functools.partial(output_kernel, heads),
        grid=(tokens // rows,),
        in_specs=[
            by_rows(vals),
            by_rows(heads * KEY),
            pl.BlockSpec((heads, KEY, VAL), lambda c: (0, 0, 0)),
            by_rows(vals),
            pl.BlockSpec((1, VAL), lambda c: (0, 0)),
        ],
        out_specs=[by_rows(vals), by_rows(vals)],
        out_shape=[
            jax.ShapeDtypeStruct((tokens, vals), f32),
            jax.ShapeDtypeStruct((tokens, vals), bf16),
        ],
        compiler_params=pltpu.CompilerParams(
            dimension_semantics=("arbitrary",), vmem_limit_bytes=48 * 2**20
        ),
    )(value_out, ident, state_in, gate_pre, gain)


def gate_back_kernel(heads, grad_ref, out_ref, gate_ref, gain_ref, ident_ref,
                     dout_ref, dgate_ref, dgain_ref, pull_ref):
    @pl.when(pl.program_id(0) == 0)
    def _():
        dgain_ref[...] = jnp.zeros_like(dgain_ref)
        pull_ref[...] = jnp.zeros_like(pull_ref)

    gain = gain_ref[0:1, :]
    for h in range(heads):
        span = slice(h * VAL, (h + 1) * VAL)
        grad, out, gate = grad_ref[:, span], out_ref[:, span], gate_ref[:, span]
        scale = lax.rsqrt(jnp.mean(out * out, axis=1, keepdims=True) + eps_norm)
        unit = out * scale
        sig = sigmoid(gate)
        m = grad * (gate * sig)
        mn = m * unit
        dgain_ref[...] += jnp.sum(mn.reshape(-1, 8, VAL), axis=0)
        mean = jnp.mean(mn * gain, axis=1, keepdims=True)
        dout = (scale * (m * gain - unit * mean)).astype(bf16)
        dout_ref[:, span] = dout
        dgate_ref[:, span] = (
            grad * unit * gain * (sig * (1.0 + gate * (1.0 - sig)))
        ).astype(bf16)
        pull_ref[h] += mm_tn(ident_ref[:, h * KEY : (h + 1) * KEY], dout)


def gate_backward(grad_gated, outputs, gate_pre, gain, ident):
    tokens, vals = outputs.shape
    heads = vals // VAL
    rows = 256
    by_rows = lambda width: pl.BlockSpec((rows, width), lambda c: (c, 0))
    return pl.pallas_call(
        functools.partial(gate_back_kernel, heads),
        grid=(tokens // rows,),
        in_specs=[
            by_rows(vals),
            by_rows(vals),
            by_rows(vals),
            pl.BlockSpec((1, VAL), lambda c: (0, 0)),
            by_rows(heads * KEY),
        ],
        out_specs=[
            by_rows(vals),
            by_rows(vals),
            pl.BlockSpec((8, VAL), lambda c: (0, 0)),
            pl.BlockSpec((heads, KEY, VAL), lambda c: (0, 0, 0)),
        ],
        out_shape=[
            jax.ShapeDtypeStruct((tokens, vals), bf16),
            jax.ShapeDtypeStruct((tokens, vals), bf16),
            jax.ShapeDtypeStruct((8, VAL), f32),
            jax.ShapeDtypeStruct((heads, KEY, VAL), f32),
        ],
        compiler_params=pltpu.CompilerParams(
            dimension_semantics=("arbitrary",), vmem_limit_bytes=48 * 2**20
        ),
    )(grad_gated, outputs, gate_pre, gain, ident)


def backward_kernel(heads, proj_ref, before_ref, edge_ref, taps_ref, ab_ref, par_ref, dout_ref,
                    inv_ref, state_ref, enter_ref, dfinal_ref,
                    dproj_ref, dab_ref, dtaps_ref, dpar_ref, dhead_ref,
                    xs_ref, gs_ref, ds_ref):
    step = pl.program_id(0)
    last = pl.num_programs(0) - 1
    keys = heads * KEY
    width = 2 * keys + heads * VAL

    @pl.when(step == 0)
    def _():
        ds_ref[...] = dfinal_ref[...]
        dtaps_ref[...] = jnp.zeros_like(dtaps_ref)
        dpar_ref[...] = jnp.zeros_like(dpar_ref)
        gs_ref[ROWS : ROWS + 8, :] = jnp.zeros((8, width), f32)

    @pl.when(step > 0)
    def _():
        gs_ref[ROWS : ROWS + 8, :] = gs_ref[0:8, :]

    @pl.when(step == last)
    def _():
        xs_ref[0:HALO, :] = edge_ref[...].astype(f32)

    @pl.when(step < last)
    def _():
        xs_ref[0:HALO, :] = before_ref[...].astype(f32)

    xs_ref[HALO : HALO + ROWS, :] = proj_ref[...].astype(f32)
    rows, cols = positions()
    ab, par = ab_ref[...], par_ref[...]
    log_decay, running, running_rows, strength = decay_terms(heads, ab, par)
    lane = lax.broadcasted_iota(jnp.int32, (ROWS, 128), 1)
    row_at = lax.broadcasted_iota(jnp.int32, (ROWS, 1), 0)
    drunning = jnp.zeros((ROWS, 128), f32)
    dbeta = jnp.zeros((ROWS, 128), f32)

    for h in range(heads):
        qs, ks, vs = h * KEY, keys + h * KEY, 2 * keys + h * VAL
        u = conv_at(xs_ref, taps_ref, qs, KEY)
        su = sigmoid(u)
        wu = u * su
        ru = lax.rsqrt(jnp.sum(wu * wu, axis=1, keepdims=True) + eps_norm)
        q = wu * (ru * KEY**-0.5)
        y = conv_at(xs_ref, taps_ref, ks, KEY)
        sy = sigmoid(y)
        wy = y * sy
        ry = lax.rsqrt(jnp.sum(wy * wy, axis=1, keepdims=True) + eps_norm)
        k = wy * ry
        x = conv_at(xs_ref, taps_ref, vs, VAL)
        sx = sigmoid(x)
        v = x * sx
        qb, kb = q.astype(bf16), k.astype(bf16)
        beta = strength[:, heads + h : heads + h + 1]
        at = running[:, h : h + 1]
        grow = jnp.exp(at)
        end = running[ROWS - 1 : ROWS, h : h + 1]
        tail = jnp.exp(end - at)
        ratio = ratio_of(running, running_rows, h, rows, cols)
        p = ratio * mm_nt(qb, kb)
        t = inv_ref[:, h * KEY : (h + 1) * KEY]
        dout = dout_ref[:, h * VAL : (h + 1) * VAL]
        state = state_ref[h, :, :VAL].astype(f32) + mm(state_ref[h, :, VAL:], enter_ref[h])
        state_b = state.astype(bf16)
        dstate = ds_ref[h]
        dstate_b = dstate.astype(bf16)
        err = mm(t, beta * (v - grow * mm(kb, state_b)))
        err_b = err.astype(bf16)
        derr = mm_tn(p, dout) + mm(tail * k, dstate_b)
        dright = mm_tn(t, derr)
        dright_b = dright.astype(bf16)
        dp = mm_nt(dout, err_b) * ratio
        dp_b = dp.astype(bf16)
        da = jnp.where(rows > cols, mm_nt(dright_b, err_b) * ratio, 0.0) * (-beta)
        da_b = da.astype(bf16)
        back = (beta * grow) * dright
        back_b = back.astype(bf16)
        dq = grow * mm_nt(dout, state_b) + mm(dp_b, kb)
        dk_read = mm(da_b, kb) - mm_nt(back_b, state_b)
        dk_tail = tail * mm_nt(err_b, dstate_b)
        dk_write = mm_tn(dp_b, qb) + mm_tn(da_b, kb) + dk_tail
        dk = dk_read + dk_write
        dv = beta * dright
        to_beta = (1.0 - beta) * jnp.sum(dright * err, axis=1, keepdims=True)
        to_decay = jnp.sum(q * dq + k * (dk_read - dk_write), axis=1, keepdims=True)
        at_end = jnp.exp(end) * jnp.sum(
            jnp.sum(state * dstate, axis=1, keepdims=True), axis=0, keepdims=True
        ) + jnp.sum(jnp.sum(k * dk_tail, axis=1, keepdims=True), axis=0, keepdims=True)
        to_decay = to_decay + jnp.where(row_at == ROWS - 1, at_end, 0.0)
        drunning = jnp.where(lane == h, to_decay, drunning)
        dbeta = jnp.where(lane == heads + h, to_beta, dbeta)
        ds_ref[h] = jnp.exp(end) * dstate + mm_tn(grow * q, dout) - mm_tn(kb, back_b)
        along = jnp.sum(wu * dq, axis=1, keepdims=True)
        du = (KEY**-0.5) * (ru * dq - wu * (ru * ru * ru * along))
        gs_ref[0:ROWS, qs : qs + KEY] = du * (su * (1.0 + u * (1.0 - su)))
        along = jnp.sum(wy * dk, axis=1, keepdims=True)
        dy = ry * dk - wy * (ry * ry * ry * along)
        gs_ref[0:ROWS, ks : ks + KEY] = dy * (sy * (1.0 + y * (1.0 - sy)))
        gs_ref[0:ROWS, vs : vs + VAL] = dv * (sx * (1.0 + x * (1.0 - sx)))

    for lo in range(0, width, 256):
        span = slice(lo, lo + 256)
        grad = gs_ref[0:ROWS, span]
        total = taps_ref[3:4, span] * grad
        for i in range(4):
            moved = xs_ref[HALO - 3 + i : HALO - 3 + i + ROWS, span] * grad
            dtaps_ref[8 * i : 8 * i + 8, span] += jnp.sum(moved.reshape(-1, 8, 256), axis=0)
            if i < 3:
                total = total + taps_ref[i : i + 1, span] * gs_ref[3 - i : 3 - i + ROWS, span]
        dproj_ref[:, span] = total.astype(bf16)

    dlog = mm_full((rows <= cols).astype(f32), drunning)
    dalpha = -dlog * par[0:1, :] * sigmoid(ab + par[1:2, :])
    dab_ref[...] = jnp.where(lane < heads, dalpha, dbeta).astype(bf16)
    dpar_ref[0:8, :] += jnp.sum((dlog * log_decay).reshape(-1, 8, 128), axis=0)
    dpar_ref[8:16, :] += jnp.sum(dalpha.reshape(-1, 8, 128), axis=0)

    @pl.when(step == last)
    def _():
        dhead_ref[...] = gs_ref[0:8, :]


def delta_backward(proj, edge, taps, ab, par, dout, inverse, states, entering, dfinal):
    tokens, width = proj.shape
    heads = width // (2 * KEY + VAL)
    keys, vals = heads * KEY, heads * VAL
    blocks = tokens // ROWS
    whole = lambda *shape: pl.BlockSpec(shape, lambda c: (0,) * len(shape))
    rev = lambda w: pl.BlockSpec((ROWS, w), lambda c: (blocks - 1 - c, 0))
    per = ROWS // HALO
    return pl.pallas_call(
        functools.partial(backward_kernel, heads),
        grid=(blocks,),
        in_specs=[
            rev(width),
            pl.BlockSpec((HALO, width), lambda c: (jnp.maximum((blocks - 1 - c) * per - 1, 0), 0)),
            whole(HALO, width),
            whole(8, width),
            rev(128),
            whole(8, 128),
            rev(vals),
            rev(keys),
            pl.BlockSpec((None, heads, KEY, VAL + KEY), lambda c: (blocks - 1 - c, 0, 0, 0)),
            whole(heads, KEY, VAL),
            whole(heads, KEY, VAL),
        ],
        out_specs=[
            rev(width),
            rev(128),
            whole(32, width),
            whole(16, 128),
            whole(8, width),
        ],
        out_shape=[
            jax.ShapeDtypeStruct((tokens, width), bf16),
            jax.ShapeDtypeStruct((tokens, 128), bf16),
            jax.ShapeDtypeStruct((32, width), f32),
            jax.ShapeDtypeStruct((16, 128), f32),
            jax.ShapeDtypeStruct((8, width), f32),
        ],
        scratch_shapes=[
            pltpu.VMEM((HALO + ROWS, width), f32),
            pltpu.VMEM((ROWS + 8, width), f32),
            pltpu.VMEM((heads, KEY, VAL), f32),
        ],
        compiler_params=pltpu.CompilerParams(
            dimension_semantics=("arbitrary",), vmem_limit_bytes=56 * 2**20
        ),
    )(proj, proj, edge, taps, ab, par, dout, inverse, states, entering, dfinal)


def dot_rows(a, b):
    return lax.dot_general(a, b, (((1,), (0,)), ((), ())), preferred_element_type=f32)


def dot_left(a, b):
    return lax.dot_general(a, b, (((0,), (0,)), ((), ())), preferred_element_type=f32)


def dot_right(a, b):
    return lax.dot_general(a, b, (((1,), (1,)), ((), ())), preferred_element_type=f32)


def head_sum(partial):
    if lax.axis_size("head") != 4:
        return lax.psum(partial.astype(bf16), "head").astype(f32)
    core = lax.axis_index("head") % 2
    half = partial.shape[0] // 2
    both = [(0, 1), (1, 0), (2, 3), (3, 2)]
    away = lax.dynamic_slice_in_dim(partial, (1 - core) * half, half).astype(bf16)
    mine = lax.dynamic_slice_in_dim(partial, core * half, half)
    mine = (mine + lax.ppermute(away, "head", both).astype(f32)).astype(bf16)
    across = lax.ppermute(mine, "head", [(0, 2), (2, 0), (1, 3), (3, 1)])
    mine = (mine.astype(f32) + across.astype(f32)).astype(bf16)
    other = lax.ppermute(mine, "head", both)
    top = jnp.where(core == 0, mine, other)
    bottom = jnp.where(core == 0, other, mine)
    return jnp.concatenate([top, bottom], axis=0).astype(f32)


def batched(a, b):
    return lax.dot_general(a, b, (((2,), (1,)), ((0,), (0,))), preferred_element_type=f32)


def batched_t(a, b):
    return lax.dot_general(a, b, (((1,), (1,)), ((0,), (0,))), preferred_element_type=f32)


def group_sizes():
    count = lax.axis_size("seq")
    across = count // 4 if count % 4 == 0 else 1
    return count, across, count // across


def in_group_order(mine):
    count, across, _ = group_sizes()
    place = lax.axis_index("seq") % across
    held = [mine]
    for turn in range(1, across):
        route = [(i - i % across + (i + turn) % across, i) for i in range(count)]
        held.append(lax.ppermute(mine, "seq", route))
    ordered = []
    for j in range(across):
        pick = (j - place) % across
        chosen = held[0]
        for turn in range(1, across):
            chosen = jnp.where(pick == turn, held[turn], chosen)
        ordered.append(chosen)
    return ordered


def states_in(final):
    count, across, groups = group_sizes()
    place = lax.axis_index("seq") % across
    members = in_group_order(final.astype(bf16))
    total = members[0].astype(f32)
    for member in members[1:]:
        total = batched(member[:, :, VAL:], total.astype(bf16))
        total = total + jnp.pad(member[:, :, :VAL].astype(f32), ((0, 0), (0, 0), (0, KEY)))
    bias, move = total[:, :, :VAL], total[:, :, VAL:].astype(bf16)
    onward = [(i, i + across) for i in range(count - across)]
    state = jnp.zeros_like(bias).astype(bf16)
    for hop in range(groups - 1):
        sent = bias if hop == 0 else batched(move, state) + bias
        state = lax.ppermute(sent.astype(bf16), "seq", onward)
    entering = state
    for j in range(across - 1):
        nxt = batched(members[j][:, :, VAL:], state) + members[j][:, :, :VAL].astype(f32)
        state = nxt.astype(bf16)
        entering = jnp.where(place == j + 1, state, entering)
    return entering, [m[:, :, VAL:] for m in members], move


def states_back(local, moves, move):
    count, across, groups = group_sizes()
    place = lax.axis_index("seq") % across
    members = in_group_order(local.astype(bf16))
    total = members[-1].astype(f32)
    for j in range(across - 2, -1, -1):
        total = batched_t(moves[j], total.astype(bf16)) + members[j].astype(f32)
    onward = [(i + across, i) for i in range(count - across)]
    state = jnp.zeros_like(total).astype(bf16)
    for hop in range(groups - 1):
        sent = total if hop == 0 else batched_t(move, state) + total
        state = lax.ppermute(sent.astype(bf16), "seq", onward)
    leaving = state
    for j in range(across - 1, 0, -1):
        state = (batched_t(moves[j], state) + members[j].astype(f32)).astype(bf16)
        leaving = jnp.where(place == j - 1, state, leaving)
    return leaving.astype(f32)


def on_device(
    tokens, cotangent, norm1_gain, w_query, w_key, w_value, w_gate_out, w_alpha, w_beta,
    conv_query, conv_key, conv_value, a_log, dt_bias, out_gain, w_out, norm2_gain, w_gate, w_up, w_down,
):
    shards = lax.axis_size("seq")
    row_count, model = tokens.shape
    heads = w_alpha.shape[1]
    hidden = w_gate.shape[1]
    padded = -(-hidden // 128) * 128
    keys, vals = heads * KEY, heads * VAL
    width = 2 * keys + vals
    head_at = lax.axis_index("head")
    gather = lambda x, axis: lax.all_gather(x, "seq", axis=axis, tiled=True)

    small = [norm1_gain, norm2_gain, w_alpha, w_beta, conv_query, conv_key, conv_value, a_log, dt_bias, out_gain]
    flat = jnp.concatenate([s.astype(bf16).reshape(-1) for s in small])
    used = flat.shape[0]
    flat = jnp.pad(flat, (0, -used % 1024))
    flat = lax.all_gather(flat, "seq", axis=0, tiled=False).astype(f32)
    parts, at = [], 0
    for s in small:
        parts.append(flat[:, at : at + s.size].reshape((shards,) + s.shape))
        at += s.size
    gain_first, gain_second = parts[0].reshape(-1), parts[1].reshape(-1)
    mix_weight = jnp.concatenate([parts[2].reshape(model, heads), parts[3].reshape(model, heads)], axis=1)
    mix_weight = jnp.pad(mix_weight, ((0, 0), (0, 128 - 2 * heads))).astype(bf16)
    taps = jnp.concatenate(
        [jnp.moveaxis(p, 0, 2).reshape(4, -1) for p in parts[4:7]], axis=1
    )
    taps = jnp.pad(taps, ((0, 4), (0, 0)))
    rate = lax.dynamic_slice_in_dim(parts[7].reshape(-1), head_at * heads, heads)
    bias = lax.dynamic_slice_in_dim(parts[8].reshape(-1), head_at * heads, heads)
    gain_out = parts[9].reshape(1, -1)
    par = jnp.pad(jnp.stack([jnp.exp(rate), bias]), ((0, 6), (0, 128 - heads)))

    proj_weight = gather(jnp.concatenate([w_query, w_key, w_value], axis=1).astype(bf16), 0)
    gate_weight = gather(w_gate_out.astype(bf16), 0)
    out_weight = gather(w_out.astype(bf16), 1)
    widen = ((0, 0), (0, padded - hidden))
    mlp_in = gather(jnp.concatenate([jnp.pad(w_gate, widen), jnp.pad(w_up, widen)], axis=1).astype(bf16), 0)
    mlp_down = gather(jnp.pad(w_down, ((0, padded - hidden), (0, 0))).astype(bf16), 1)

    inputs = tokens.astype(f32)
    scale_first = lax.rsqrt(jnp.mean(inputs * inputs, axis=1, keepdims=True) + eps_norm)
    normed_first = (inputs * scale_first * gain_first).astype(bf16)
    proj = dot_rows(normed_first, proj_weight).astype(bf16)
    mix_pre = dot_rows(normed_first, mix_weight)
    forward = [(i, i + 1) for i in range(shards - 1)]
    backward = [(i + 1, i) for i in range(shards - 1)]
    edge = lax.ppermute(proj[row_count - HALO :], "seq", forward)
    value_out, ident, inverse, states, final = delta_forward(proj, edge, taps, mix_pre, par)
    gate_pre = dot_rows(normed_first, gate_weight)
    entering, moves, move = states_in(final)
    outputs, gated = gated_outputs(value_out, ident, entering, gate_pre, gain_out)
    attention = head_sum(dot_rows(gated, out_weight))
    hidden_state = inputs + attention
    scale_second = lax.rsqrt(jnp.mean(hidden_state * hidden_state, axis=1, keepdims=True) + eps_norm)
    hat_second = hidden_state * scale_second
    normed_second = (hat_second * gain_second).astype(bf16)
    grad_mixed = dot_right(cotangent, mlp_down)
    act = dot_rows(normed_second, mlp_in)
    gate_act, up_act = act[:, :padded], act[:, padded:]
    sig = jax.nn.sigmoid(gate_act)
    mixed = (gate_act * sig * up_act).astype(bf16)
    grad_act = jnp.concatenate(
        [grad_mixed * up_act * sig * (1.0 + gate_act * (1.0 - sig)), grad_mixed * (gate_act * sig)], axis=1
    ).astype(bf16)
    partial_second = dot_right(grad_act, mlp_in)
    grad_normed_second = head_sum(partial_second)
    grad_gain_second = jnp.sum(partial_second * hat_second, axis=0)
    scatter = lambda x, axis: lax.psum_scatter(
        x.astype(bf16), "seq", scatter_dimension=axis, tiled=True
    ).astype(f32)
    grad_down = scatter(dot_left(mixed, cotangent), 1)
    grad_in = scatter(dot_left(normed_second, grad_act), 0)
    branch = head_sum(dot_rows(mixed, mlp_down))
    result = (hidden_state + branch).astype(bf16)
    g = grad_normed_second * gain_second
    grad_hidden = cotangent.astype(f32) + scale_second * (
        g - hat_second * jnp.mean(g * hat_second, axis=1, keepdims=True)
    )
    attention_rounded = grad_hidden.astype(bf16)
    grad_gated = dot_right(attention_rounded, out_weight)
    grad_outputs, grad_gate, grad_gain_out, local_pull = gate_backward(
        grad_gated, outputs, gate_pre, gain_out, ident
    )
    grad_out_weight = scatter(dot_left(gated, attention_rounded), 1)
    grad_gate_weight = scatter(dot_left(normed_first, grad_gate), 0)
    leaving = states_back(local_pull, moves, move)
    grad_proj, grad_mix, grad_taps, grad_par, grad_head = delta_backward(
        proj, edge, taps, mix_pre, par, grad_outputs, inverse, states, entering, leaving
    )
    following = lax.ppermute(grad_head, "seq", backward)
    fixes = []
    for s in range(3):
        fixes.append(sum(taps[3 - j] * following[s - 3 + j] for j in range(3 - s, 4)))
    ending = (grad_proj[row_count - HALO :].astype(f32)
              + jnp.pad(jnp.stack(fixes), ((HALO - 3, 0), (0, 0)))).astype(bf16)
    grad_proj = lax.dynamic_update_slice_in_dim(grad_proj, ending, row_count - HALO, 0)
    partial_first = (
        dot_right(grad_proj, proj_weight) + dot_right(grad_gate, gate_weight) + dot_right(grad_mix, mix_weight)
    )
    grad_normed_first = head_sum(partial_first)
    hat_first = inputs * scale_first
    grad_gain_first = jnp.sum(partial_first * hat_first, axis=0)
    grad_mix_weight = dot_left(normed_first, grad_mix)
    taps_sum = jnp.sum(grad_taps.reshape(4, 8, width), axis=1)
    par_sum = jnp.sum(grad_par.reshape(2, 8, 128), axis=1)
    every = jnp.zeros((2, shards * a_log.shape[0]), f32)
    every = lax.dynamic_update_slice(every, par_sum[:, :heads], (0, head_at * heads))

    def by_shard(x, lo, like):
        block = x[:, lo : lo + like.shape[2] * shards * heads].reshape(4, heads, shards, like.shape[2])
        return jnp.moveaxis(block, 2, 0).reshape(shards, -1)

    summed = [
        grad_gain_first.reshape(shards, -1),
        grad_gain_second.reshape(shards, -1),
        every[0].reshape(shards, -1),
        every[1].reshape(shards, -1),
        jnp.sum(grad_gain_out, axis=0).reshape(shards, -1),
        grad_mix_weight[:, :heads].reshape(shards, -1),
        grad_mix_weight[:, heads : 2 * heads].reshape(shards, -1),
        by_shard(taps_sum, 0, conv_query),
        by_shard(taps_sum, keys, conv_key),
        by_shard(taps_sum, 2 * keys, conv_value),
    ]
    packed = jnp.concatenate(summed, axis=1)
    length = packed.shape[1]
    packed = jnp.pad(packed, ((0, 0), (0, -length % 1024)))
    packed = scatter(packed, 0).reshape(-1)
    shared = sum(s.shape[1] for s in summed[:5])
    head_part = lax.psum(packed[:shared].astype(bf16), "head").astype(f32)
    packed = jnp.concatenate([head_part, packed[shared:]])
    pieces, at = [], 0
    for s in summed:
        pieces.append(packed[at : at + s.shape[1]])
        at += s.shape[1]
    grad_proj_weight = scatter(dot_left(normed_first, grad_proj), 0)
    g = grad_normed_first * gain_first
    grad_tokens = grad_hidden + scale_first * (
        g - hat_first * jnp.mean(g * hat_first, axis=1, keepdims=True)
    )
    return (
        result,
        grad_tokens,
        pieces[0],
        grad_proj_weight[:, :keys],
        grad_proj_weight[:, keys : 2 * keys],
        grad_proj_weight[:, 2 * keys :],
        grad_gate_weight,
        pieces[5].reshape(w_alpha.shape),
        pieces[6].reshape(w_beta.shape),
        pieces[7].reshape(conv_query.shape),
        pieces[8].reshape(conv_key.shape),
        pieces[9].reshape(conv_value.shape),
        pieces[2],
        pieces[3],
        pieces[4],
        grad_out_weight,
        pieces[1],
        grad_in[:, :hidden],
        grad_in[:, padded : padded + hidden],
        grad_down[:hidden],
    )


def solution(mesh):
    P = jax.sharding.PartitionSpec
    rows, vector, filters, turned = P("seq", None), P("seq"), P(None, "head", "seq"), P("head", "seq")
    matrix = P("seq", "head")
    in_specs = (rows, rows, vector) + (matrix,) * 6 + (filters,) * 3 + (vector,) * 3 + (
        turned, vector, matrix, matrix, turned)
    out_specs = (rows, rows, vector) + (matrix,) * 6 + (filters,) * 3 + (vector,) * 3 + (
        turned, vector, matrix, matrix, turned)
    return jax.shard_map(
        on_device, mesh=mesh, in_specs=in_specs, out_specs=out_specs, check_vma=False
    )
```

```python
import functools
import jax
import jax.numpy as jnp
from jax import lax
from jax.experimental import pallas as pl
from jax.experimental.pallas import tpu as pltpu

ROWS = 128
KEY = 128
VAL = 256
HALO = 16
eps_norm = 1e-06
f32 = jnp.float32
bf16 = jnp.bfloat16


def mm(a, b):
    return lax.dot_general(
        a.astype(bf16), b.astype(bf16), (((1,), (0,)), ((), ())), preferred_element_type=f32
    )


def mm_nt(a, b):
    return lax.dot_general(
        a.astype(bf16), b.astype(bf16), (((1,), (1,)), ((), ())), preferred_element_type=f32
    )


def mm_tn(a, b):
    return lax.dot_general(
        a.astype(bf16), b.astype(bf16), (((0,), (0,)), ((), ())), preferred_element_type=f32
    )


def mm_full(a, b):
    return lax.dot_general(
        a, b, (((1,), (0,)), ((), ())), precision=lax.Precision.HIGHEST, preferred_element_type=f32
    )


def sigmoid(x):
    return 1.0 / (1.0 + jnp.exp(-x))


def softplus(x):
    return jnp.maximum(x, 0.0) + jnp.log(1.0 + jnp.exp(-jnp.abs(x)))


def positions():
    rows = lax.broadcasted_iota(jnp.int32, (ROWS, ROWS), 0)
    cols = lax.broadcasted_iota(jnp.int32, (ROWS, ROWS), 1)
    return rows, cols


def decay_terms(heads, ab, par):
    rows, cols = positions()
    log_decay = -par[0:1, :] * softplus(ab + par[1:2, :])
    running = mm_full((rows >= cols).astype(f32), log_decay)
    return log_decay, running, running.T, sigmoid(ab)


def ratio_of(running, running_rows, h, rows, cols):
    gap = running[:, h : h + 1] - running_rows[h : h + 1, :]
    return jnp.where(rows >= cols, jnp.exp(jnp.where(rows >= cols, gap, 0.0)), 0.0)


def conv_at(xs_ref, taps_ref, base, lo, width):
    total = taps_ref[0:1, lo : lo + width] * xs_ref[base - 3 : base - 3 + ROWS, lo : lo + width]
    for i in range(1, 4):
        total = total + taps_ref[i : i + 1, lo : lo + width] * (
            xs_ref[base - 3 + i : base - 3 + i + ROWS, lo : lo + width]
        )
    return total


def forward_kernel(heads, proj_ref, edge_ref, taps_ref, ab_ref, par_ref,
                   value_ref, ident_ref, inv_ref, state_ref, final_ref, xs_ref, s_ref):
    step = pl.program_id(0)
    keys = heads * KEY

    @pl.when(step == 0)
    def _():
        xs_ref[0:HALO, :] = edge_ref[...].astype(f32)
        r, c = positions()
        for h in range(heads):
            s_ref[h, :, 0:VAL] = jnp.zeros((KEY, VAL), f32)
            s_ref[h, :, VAL:] = (r == c).astype(f32)

    span = proj_ref.shape[0]
    subs = range(span // ROWS)

    @pl.when(step > 0)
    def _():
        xs_ref[0:HALO, :] = xs_ref[span : span + HALO, :]

    xs_ref[HALO : HALO + span, :] = proj_ref[...].astype(f32)
    rows, cols = positions()
    every = [(s, h) for s in subs for h in range(heads)]
    running, running_rows, strength = [], [], []
    for s in subs:
        terms = decay_terms(heads, ab_ref[s * ROWS : (s + 1) * ROWS, :], par_ref[...])
        running.append(terms[1])
        running_rows.append(terms[2])
        strength.append(terms[3])
    q, k, v, a, p, t, beta, grow = {}, {}, {}, {}, {}, {}, {}, {}
    for s, h in every:
        base = HALO + s * ROWS
        u = conv_at(xs_ref, taps_ref, base, h * KEY, KEY)
        u = u * sigmoid(u)
        q[s, h] = u * (lax.rsqrt(jnp.sum(u * u, axis=1, keepdims=True) + eps_norm) * KEY**-0.5)
        w = conv_at(xs_ref, taps_ref, base, keys + h * KEY, KEY)
        w = w * sigmoid(w)
        k[s, h] = w * lax.rsqrt(jnp.sum(w * w, axis=1, keepdims=True) + eps_norm)
        x = conv_at(xs_ref, taps_ref, base, 2 * keys + h * VAL, VAL)
        v[s, h] = x * sigmoid(x)
        beta[s, h] = strength[s][:, heads + h : heads + h + 1]
        grow[s, h] = jnp.exp(running[s][:, h : h + 1])
    for s, h in every:
        ratio = ratio_of(running[s], running_rows[s], h, rows, cols)
        gram = mm_nt(k[s, h], k[s, h])
        a[s, h] = jnp.where(rows > cols, ratio * gram, 0.0) * beta[s, h]
        p[s, h] = ratio * mm_nt(q[s, h], k[s, h])
    first = (rows // 2 == cols // 2) & (rows > cols)
    for e in every:
        t[e] = (rows == cols).astype(f32) - jnp.where(first, a[e], 0.0)
    b = 2
    while b < ROWS:
        low = (rows // (2 * b) == cols // (2 * b)) & ((rows // b) % 2 == 1) & ((cols // b) % 2 == 0)
        inner = {e: mm(jnp.where(low, a[e], 0.0), t[e]) for e in every}
        t = {e: t[e] - mm(t[e], inner[e]) for e in every}
        b *= 2
    uw = {
        e: mm(t[e], jnp.concatenate([beta[e] * v[e], (beta[e] * grow[e]) * k[e]], axis=1))
        for e in every
    }
    for s, h in every:
        inv_ref[s * ROWS : (s + 1) * ROWS, h * KEY : (h + 1) * KEY] = t[s, h].astype(bf16)
    for s, h in every:
        at = slice(s * ROWS, (s + 1) * ROWS)
        state = s_ref[h]
        state_ref[s, h] = state.astype(bf16)
        pred = mm(uw[s, h][:, VAL:], state)
        err = jnp.concatenate([uw[s, h][:, :VAL] - pred[:, :VAL], -pred[:, VAL:]], axis=1)
        out = grow[s, h] * mm(q[s, h], state) + mm(p[s, h], err)
        value_ref[at, h * VAL : (h + 1) * VAL] = out[:, :VAL]
        ident_ref[at, h * KEY : (h + 1) * KEY] = out[:, VAL:].astype(bf16)
        end = running[s][ROWS - 1 : ROWS, h : h + 1]
        tail = jnp.exp(end - running[s][:, h : h + 1]) * k[s, h]
        s_ref[h] = jnp.exp(end) * state + mm_tn(tail, err)

    @pl.when(step == pl.num_programs(0) - 1)
    def _():
        final_ref[...] = s_ref[...]


def sub_blocks(heads):
    return 2


def delta_forward(proj, edge, taps, ab, par):
    tokens = proj.shape[0]
    heads = proj.shape[1] // (2 * KEY + VAL)
    keys, vals = heads * KEY, heads * VAL
    subs = sub_blocks(heads)
    span = subs * ROWS
    blocks = tokens // span
    width = proj.shape[1]
    whole = lambda *shape: pl.BlockSpec(shape, lambda c: (0,) * len(shape))
    return pl.pallas_call(
        functools.partial(forward_kernel, heads),
        grid=(blocks,),
        in_specs=[
            pl.BlockSpec((span, width), lambda c: (c, 0)),
            whole(HALO, width),
            whole(8, width),
            pl.BlockSpec((span, 128), lambda c: (c, 0)),
            whole(8, 128),
        ],
        out_specs=[
            pl.BlockSpec((span, vals), lambda c: (c, 0)),
            pl.BlockSpec((span, keys), lambda c: (c, 0)),
            pl.BlockSpec((span, keys), lambda c: (c, 0)),
            pl.BlockSpec((subs, heads, KEY, VAL + KEY), lambda c: (c, 0, 0, 0)),
            whole(heads, KEY, VAL + KEY),
        ],
        out_shape=[
            jax.ShapeDtypeStruct((tokens, vals), f32),
            jax.ShapeDtypeStruct((tokens, keys), bf16),
            jax.ShapeDtypeStruct((tokens, keys), bf16),
            jax.ShapeDtypeStruct((blocks * subs, heads, KEY, VAL + KEY), bf16),
            jax.ShapeDtypeStruct((heads, KEY, VAL + KEY), f32),
        ],
        scratch_shapes=[
            pltpu.VMEM((HALO + span, width), f32),
            pltpu.VMEM((heads, KEY, VAL + KEY), f32),
        ],
        compiler_params=pltpu.CompilerParams(
            dimension_semantics=("arbitrary",), vmem_limit_bytes=48 * 2**20
        ),
    )(proj, edge, taps, ab, par)


UNIT = 2 * ROWS


def placed_rows(order_ref, sub):
    flip = order_ref[order_ref.shape[0] - 1]
    return pl.ds(pl.multiple_of((flip + sub - 2 * flip * sub) * ROWS, ROWS), ROWS)


def reorder_kernel(order_ref, *refs):
    count = len(refs) // 2
    for in_ref, out_ref in zip(refs[:count], refs[count:]):
        for sub in range(2):
            out_ref[placed_rows(order_ref, sub), :] = in_ref[sub * ROWS : (sub + 1) * ROWS, :]


def reordered(order, *arrays):
    tokens = arrays[0].shape[0]
    return pl.pallas_call(
        reorder_kernel,
        grid_spec=pltpu.PrefetchScalarGridSpec(
            num_scalar_prefetch=1,
            grid=(tokens // UNIT,),
            in_specs=[pl.BlockSpec((UNIT, a.shape[1]), lambda c, order: (order[c], 0)) for a in arrays],
            out_specs=[pl.BlockSpec((UNIT, a.shape[1]), lambda c, order: (c, 0)) for a in arrays],
        ),
        out_shape=[jax.ShapeDtypeStruct(a.shape, a.dtype) for a in arrays],
        compiler_params=pltpu.CompilerParams(
            dimension_semantics=("arbitrary",), vmem_limit_bytes=32 * 2**20
        ),
    )(order, *arrays)


def output_kernel(heads, order_ref, value_ref, ident_ref, state_ref, gate_ref, gain_ref, out_ref, gated_ref):
    for h in range(heads):
        span = slice(h * VAL, (h + 1) * VAL)
        out = value_ref[:, span] + mm(ident_ref[:, h * KEY : (h + 1) * KEY], state_ref[h])
        out_ref[:, span] = out
        gate = gate_ref[:, span]
        unit = out * lax.rsqrt(jnp.mean(out * out, axis=1, keepdims=True) + eps_norm)
        gated = (unit * gain_ref[0:1, :] * (gate * sigmoid(gate))).astype(bf16)
        for sub in range(2):
            gated_ref[placed_rows(order_ref, sub), span] = gated[sub * ROWS : (sub + 1) * ROWS]


def gated_outputs(order, value_out, ident, state_in, gate_pre, gain):
    tokens, vals = value_out.shape
    heads = vals // VAL
    placed = lambda width: pl.BlockSpec((UNIT, width), lambda c, order: (order[c], 0))
    return pl.pallas_call(
        functools.partial(output_kernel, heads),
        grid_spec=pltpu.PrefetchScalarGridSpec(
            num_scalar_prefetch=1,
            grid=(tokens // UNIT,),
            in_specs=[
                placed(vals),
                placed(heads * KEY),
                pl.BlockSpec((heads, KEY, VAL), lambda c, order: (0, 0, 0)),
                placed(vals),
                pl.BlockSpec((1, VAL), lambda c, order: (0, 0)),
            ],
            out_specs=[placed(vals), pl.BlockSpec((UNIT, vals), lambda c, order: (c, 0))],
        ),
        out_shape=[
            jax.ShapeDtypeStruct((tokens, vals), f32),
            jax.ShapeDtypeStruct((tokens, vals), bf16),
        ],
        compiler_params=pltpu.CompilerParams(
            dimension_semantics=("arbitrary",), vmem_limit_bytes=48 * 2**20
        ),
    )(order, value_out, ident, state_in, gate_pre, gain)


def gate_back_kernel(heads, order_ref, grad_ref, out_ref, gate_ref, gain_ref, ident_ref,
                     dout_ref, dgate_ref, dgain_ref, pull_ref):
    @pl.when(pl.program_id(0) == 0)
    def _():
        dgain_ref[...] = jnp.zeros_like(dgain_ref)
        pull_ref[...] = jnp.zeros_like(pull_ref)

    gain = gain_ref[0:1, :]
    for h in range(heads):
        span = slice(h * VAL, (h + 1) * VAL)
        grad = jnp.concatenate([grad_ref[placed_rows(order_ref, sub), span] for sub in range(2)], axis=0)
        out, gate = out_ref[:, span], gate_ref[:, span]
        scale = lax.rsqrt(jnp.mean(out * out, axis=1, keepdims=True) + eps_norm)
        unit = out * scale
        sig = sigmoid(gate)
        m = grad * (gate * sig)
        mn = m * unit
        dgain_ref[...] += jnp.sum(mn.reshape(-1, 8, VAL), axis=0)
        mean = jnp.mean(mn * gain, axis=1, keepdims=True)
        dout = (scale * (m * gain - unit * mean)).astype(bf16)
        dout_ref[:, span] = dout
        dgate = (grad * unit * gain * (sig * (1.0 + gate * (1.0 - sig)))).astype(bf16)
        for sub in range(2):
            dgate_ref[placed_rows(order_ref, sub), span] = dgate[sub * ROWS : (sub + 1) * ROWS]
        pull_ref[h] += mm_tn(ident_ref[:, h * KEY : (h + 1) * KEY], dout)


def gate_backward(order, grad_gated, outputs, gate_pre, gain, ident):
    tokens, vals = outputs.shape
    heads = vals // VAL
    placed = lambda width: pl.BlockSpec((UNIT, width), lambda c, order: (order[c], 0))
    return pl.pallas_call(
        functools.partial(gate_back_kernel, heads),
        grid_spec=pltpu.PrefetchScalarGridSpec(
            num_scalar_prefetch=1,
            grid=(tokens // UNIT,),
            in_specs=[
                pl.BlockSpec((UNIT, vals), lambda c, order: (c, 0)),
                placed(vals),
                placed(vals),
                pl.BlockSpec((1, VAL), lambda c, order: (0, 0)),
                placed(heads * KEY),
            ],
            out_specs=[
                placed(vals),
                pl.BlockSpec((UNIT, vals), lambda c, order: (c, 0)),
                pl.BlockSpec((8, VAL), lambda c, order: (0, 0)),
                pl.BlockSpec((heads, KEY, VAL), lambda c, order: (0, 0, 0)),
            ],
        ),
        out_shape=[
            jax.ShapeDtypeStruct((tokens, vals), bf16),
            jax.ShapeDtypeStruct((tokens, vals), bf16),
            jax.ShapeDtypeStruct((8, VAL), f32),
            jax.ShapeDtypeStruct((heads, KEY, VAL), f32),
        ],
        compiler_params=pltpu.CompilerParams(
            dimension_semantics=("arbitrary",), vmem_limit_bytes=48 * 2**20
        ),
    )(order, grad_gated, outputs, gate_pre, gain, ident)


def backward_kernel(heads, order_ref, proj_ref, before_ref, edge_ref, taps_ref, ab_ref, par_ref, dout_ref,
                    inv_ref, state_ref, enter_ref, dfinal_ref,
                    dproj_ref, dab_ref, dtaps_ref, dpar_ref, dhead_ref,
                    xs_ref, gs_ref, ds_ref):
    step = pl.program_id(0)
    last = pl.num_programs(0) - 1
    keys = heads * KEY
    width = 2 * keys + heads * VAL
    span = proj_ref.shape[0]

    @pl.when(step == 0)
    def _():
        ds_ref[...] = dfinal_ref[...]
        dtaps_ref[...] = jnp.zeros_like(dtaps_ref)
        dpar_ref[...] = jnp.zeros_like(dpar_ref)
        gs_ref[span : span + 8, :] = jnp.zeros((8, width), f32)

    @pl.when(step > 0)
    def _():
        gs_ref[span : span + 8, :] = gs_ref[0:8, :]

    @pl.when(step == last)
    def _():
        xs_ref[0:HALO, :] = edge_ref[...].astype(f32)

    @pl.when(step < last)
    def _():
        xs_ref[0:HALO, :] = before_ref[...].astype(f32)

    xs_ref[HALO : HALO + span, :] = proj_ref[...].astype(f32)
    rows, cols = positions()
    par = par_ref[...]
    lane = lax.broadcasted_iota(jnp.int32, (ROWS, 128), 1)
    row_at = lax.broadcasted_iota(jnp.int32, (ROWS, 1), 0)
    for s in reversed(range(span // ROWS)):
        at = slice(s * ROWS, (s + 1) * ROWS)
        ab = ab_ref[at, :]
        log_decay, running, running_rows, strength = decay_terms(heads, ab, par)
        drunning = jnp.zeros((ROWS, 128), f32)
        dbeta = jnp.zeros((ROWS, 128), f32)

        for h in range(heads):
            qs, ks, vs = h * KEY, keys + h * KEY, 2 * keys + h * VAL
            u = conv_at(xs_ref, taps_ref, HALO + s * ROWS, qs, KEY)
            su = sigmoid(u)
            wu = u * su
            ru = lax.rsqrt(jnp.sum(wu * wu, axis=1, keepdims=True) + eps_norm)
            q = wu * (ru * KEY**-0.5)
            y = conv_at(xs_ref, taps_ref, HALO + s * ROWS, ks, KEY)
            sy = sigmoid(y)
            wy = y * sy
            ry = lax.rsqrt(jnp.sum(wy * wy, axis=1, keepdims=True) + eps_norm)
            k = wy * ry
            x = conv_at(xs_ref, taps_ref, HALO + s * ROWS, vs, VAL)
            sx = sigmoid(x)
            v = x * sx
            qb, kb = q.astype(bf16), k.astype(bf16)
            beta = strength[:, heads + h : heads + h + 1]
            passed = running[:, h : h + 1]
            grow = jnp.exp(passed)
            end = running[ROWS - 1 : ROWS, h : h + 1]
            tail = jnp.exp(end - passed)
            ratio = ratio_of(running, running_rows, h, rows, cols)
            p = ratio * mm_nt(qb, kb)
            t = inv_ref[at, h * KEY : (h + 1) * KEY]
            dout = dout_ref[at, h * VAL : (h + 1) * VAL]
            state = state_ref[s, h, :, :VAL].astype(f32) + mm(state_ref[s, h, :, VAL:], enter_ref[h])
            state_b = state.astype(bf16)
            dstate = ds_ref[h]
            dstate_b = dstate.astype(bf16)
            err = mm(t, beta * (v - grow * mm(kb, state_b)))
            err_b = err.astype(bf16)
            derr = mm_tn(p, dout) + mm(tail * k, dstate_b)
            dright = mm_tn(t, derr)
            dright_b = dright.astype(bf16)
            dp = mm_nt(dout, err_b) * ratio
            dp_b = dp.astype(bf16)
            da = jnp.where(rows > cols, mm_nt(dright_b, err_b) * ratio, 0.0) * (-beta)
            da_b = da.astype(bf16)
            back = (beta * grow) * dright
            back_b = back.astype(bf16)
            dq = grow * mm_nt(dout, state_b) + mm(dp_b, kb)
            dk_read = mm(da_b, kb) - mm_nt(back_b, state_b)
            dk_tail = tail * mm_nt(err_b, dstate_b)
            dk_write = mm_tn(dp_b, qb) + mm_tn(da_b, kb) + dk_tail
            dk = dk_read + dk_write
            dv = beta * dright
            to_beta = (1.0 - beta) * jnp.sum(dright * err, axis=1, keepdims=True)
            to_decay = jnp.sum(q * dq + k * (dk_read - dk_write), axis=1, keepdims=True)
            at_end = jnp.exp(end) * jnp.sum(
                jnp.sum(state * dstate, axis=1, keepdims=True), axis=0, keepdims=True
            ) + jnp.sum(jnp.sum(k * dk_tail, axis=1, keepdims=True), axis=0, keepdims=True)
            to_decay = to_decay + jnp.where(row_at == ROWS - 1, at_end, 0.0)
            drunning = jnp.where(lane == h, to_decay, drunning)
            dbeta = jnp.where(lane == heads + h, to_beta, dbeta)
            ds_ref[h] = jnp.exp(end) * dstate + mm_tn(grow * q, dout) - mm_tn(kb, back_b)
            along = jnp.sum(wu * dq, axis=1, keepdims=True)
            du = (KEY**-0.5) * (ru * dq - wu * (ru * ru * ru * along))
            gs_ref[at, qs : qs + KEY] = du * (su * (1.0 + u * (1.0 - su)))
            along = jnp.sum(wy * dk, axis=1, keepdims=True)
            dy = ry * dk - wy * (ry * ry * ry * along)
            gs_ref[at, ks : ks + KEY] = dy * (sy * (1.0 + y * (1.0 - sy)))
            gs_ref[at, vs : vs + VAL] = dv * (sx * (1.0 + x * (1.0 - sx)))

        dlog = mm_full((rows <= cols).astype(f32), drunning)
        dalpha = -dlog * par[0:1, :] * sigmoid(ab + par[1:2, :])
        dab_ref[placed_rows(order_ref, s), :] = jnp.where(lane < heads, dalpha, dbeta).astype(bf16)
        dpar_ref[0:8, :] += jnp.sum((dlog * log_decay).reshape(-1, 8, 128), axis=0)
        dpar_ref[8:16, :] += jnp.sum(dalpha.reshape(-1, 8, 128), axis=0)

    for lo in range(0, width, 256):
        lanes = slice(lo, lo + 256)
        grad = gs_ref[0:span, lanes]
        total = taps_ref[3:4, lanes] * grad
        for i in range(4):
            moved = xs_ref[HALO - 3 + i : HALO - 3 + i + span, lanes] * grad
            dtaps_ref[8 * i : 8 * i + 8, lanes] += jnp.sum(moved.reshape(-1, 8, 256), axis=0)
            if i < 3:
                total = total + taps_ref[i : i + 1, lanes] * gs_ref[3 - i : 3 - i + span, lanes]
        total = total.astype(bf16)
        for s in range(2):
            dproj_ref[placed_rows(order_ref, s), lanes] = total[s * ROWS : (s + 1) * ROWS]

    @pl.when(step == last)
    def _():
        dhead_ref[...] = gs_ref[0:8, :]


def delta_backward(order, proj, edge, taps, ab, par, dout, inverse, states, entering, dfinal):
    tokens, width = proj.shape
    heads = width // (2 * KEY + VAL)
    keys, vals = heads * KEY, heads * VAL
    subs = sub_blocks(heads)
    span = subs * ROWS
    blocks = tokens // span
    whole = lambda *shape: pl.BlockSpec(shape, lambda c, order: (0,) * len(shape))
    rev = lambda w: pl.BlockSpec((span, w), lambda c, order: (blocks - 1 - c, 0))
    sent = lambda w: pl.BlockSpec((span, w), lambda c, order: (order[blocks + blocks - 1 - c], 0))
    per = span // HALO
    return pl.pallas_call(
        functools.partial(backward_kernel, heads),
        grid_spec=pltpu.PrefetchScalarGridSpec(
            num_scalar_prefetch=1,
            grid=(blocks,),
            in_specs=[
                rev(width),
                pl.BlockSpec((HALO, width), lambda c, order: (jnp.maximum((blocks - 1 - c) * per - 1, 0), 0)),
                whole(HALO, width),
                whole(8, width),
                rev(128),
                whole(8, 128),
                rev(vals),
                rev(keys),
                pl.BlockSpec((subs, heads, KEY, VAL + KEY), lambda c, order: (blocks - 1 - c, 0, 0, 0)),
                whole(heads, KEY, VAL),
                whole(heads, KEY, VAL),
            ],
            out_specs=[
                sent(width),
                sent(128),
                whole(32, width),
                whole(16, 128),
                whole(8, width),
            ],
            scratch_shapes=[
                pltpu.VMEM((HALO + span, width), f32),
                pltpu.VMEM((span + 8, width), f32),
                pltpu.VMEM((heads, KEY, VAL), f32),
            ],
        ),
        out_shape=[
            jax.ShapeDtypeStruct((tokens, width), bf16),
            jax.ShapeDtypeStruct((tokens, 128), bf16),
            jax.ShapeDtypeStruct((32, width), f32),
            jax.ShapeDtypeStruct((16, 128), f32),
            jax.ShapeDtypeStruct((8, width), f32),
        ],
        compiler_params=pltpu.CompilerParams(
            dimension_semantics=("arbitrary",), vmem_limit_bytes=56 * 2**20
        ),
    )(order, proj, proj, edge, taps, ab, par, dout, inverse, states, entering, dfinal)


def dot_rows(a, b):
    return lax.dot_general(a, b, (((1,), (0,)), ((), ())), preferred_element_type=f32)


def dot_left(a, b):
    return lax.dot_general(a, b, (((0,), (0,)), ((), ())), preferred_element_type=f32)


def dot_right(a, b):
    return lax.dot_general(a, b, (((1,), (1,)), ((), ())), preferred_element_type=f32)


def batched(a, b):
    return lax.dot_general(a, b, (((2,), (1,)), ((0,), (0,))), preferred_element_type=f32)


def batched_t(a, b):
    return lax.dot_general(a, b, (((1,), (1,)), ((0,), (0,))), preferred_element_type=f32)


def tie(first, *then):
    return lax.optimization_barrier((first, *then))[0] if then else first


def fold_of():
    return 2 if lax.axis_size("seq") == 8 and lax.axis_size("head") == 4 else 1


def lines_of():
    fold = fold_of()
    return [list(range(x, lax.axis_size("seq"), fold)) for x in range(fold)]


def side_of():
    return lax.axis_index("seq") % fold_of()


def swap_pair(v):
    return lax.ppermute(v, "seq", [(i, i ^ 1) for i in range(lax.axis_size("seq"))])


def swap_chip(v):
    return lax.ppermute(v, "head", [(i, i ^ 2) for i in range(4)])


def swap_core(v):
    return lax.ppermute(v, "head", [(i, i ^ 1) for i in range(4)])


def pick(v, at, axis=0):
    half = v.shape[axis] // 2
    return lax.dynamic_slice_in_dim(v, at * half, half, axis)


def join(at, mine, other, axis=0):
    first, second = jnp.where(at == 0, mine, other), jnp.where(at == 0, other, mine)
    return jnp.concatenate([first, second], axis=axis)


def plus(a, b):
    return (a.astype(f32) + b.astype(f32)).astype(bf16)


def place_of():
    core, chip = lax.axis_index("head") % 2, lax.axis_index("head") // 2
    return core, chip, side_of()


def unit_order(count):
    if fold_of() == 1:
        same = [jnp.int32(i) for i in range(count)]
        return same, same, jnp.int32(0)
    core, chip, side = place_of()
    bits = [(i // 4, i // 2 % 2, i % 2) for i in range(8)]
    at_place = [((s ^ side) * 4 + (c ^ core) * 2 + kind).astype(jnp.int32) for c, kind, s in bits]
    of_unit = [((c ^ core) * 4 + kind * 2 + (s ^ side)).astype(jnp.int32) for s, c, kind in bits]
    return at_place, of_unit, chip.astype(jnp.int32)


def chip_sum(away, near):
    if fold_of() == 1:
        return jnp.concatenate([near, away], axis=0).astype(bf16)
    return plus(near, swap_core(away.astype(bf16)))


def summed_rows(mine, beside=(), later=()):
    if fold_of() == 1:
        return [lax.psum(mine, "head")]
    n = mine.shape[0] // 8
    blocks = [mine[i * n : (i + 1) * n] for i in range(8)]
    a = plus(mine[: 2 * n], swap_pair(mine[2 * n : 4 * n]))
    keep, give = (jnp.concatenate([blocks[4 + i], blocks[6 + i]], axis=0) for i in range(2))
    b = plus(keep, swap_chip(give))
    a, b = tie(a, *beside), tie(b, *beside)
    a, b = plus(a[:n], swap_chip(a[n:])), plus(b[:n], swap_pair(b[n:]))
    return [tie(a, *later), tie(b, *later)]


def all_rows(pieces, beside=()):
    if fold_of() == 1:
        return pieces[0]
    a, b = pieces
    a = jnp.concatenate([a, swap_chip(a)], axis=0)
    b = jnp.concatenate([b, swap_pair(b)], axis=0)
    a, b = tie(a, *beside), tie(b, *beside)
    far = swap_chip(b)
    n = far.shape[0] // 2
    b = jnp.concatenate([b[:n], far[:n], b[n:], far[n:]], axis=0)
    near = [a, swap_pair(a), b]
    return jnp.concatenate(near + [swap_core(v) for v in near], axis=0)


def own_tokens(pieces, *beside):
    if fold_of() == 1:
        return pieces[0]
    core, chip, _ = place_of()
    near = jnp.concatenate([join(chip, v, swap_chip(v)) for v in pieces], axis=0)
    near = tie(near, *beside)
    return join(core, near, swap_core(near))


def own_blocks(v):
    if fold_of() == 1:
        return [v]
    core, chip, _ = place_of()
    n = v.shape[0] // 8
    return [lax.dynamic_slice_in_dim(v, core * 4 * n + kind * 2 * n + chip * n, n) for kind in range(2)]


def line_total(v):
    fold, step = fold_of(), fold_of()
    while step < lax.axis_size("seq"):
        v = v + lax.ppermute(v, "seq", [(i, i ^ step) for i in range(lax.axis_size("seq"))])
        step *= 2
    return v


def shards_of(v):
    count, step = lax.axis_size("seq"), 1
    held = v[None]
    while step < count:
        held = jnp.concatenate(
            [held, lax.ppermute(held, "seq", [(i, i ^ step) for i in range(count)])], axis=0
        )
        step *= 2
    me = lax.axis_index("seq")
    return jnp.concatenate([lax.dynamic_slice_in_dim(held, me ^ i, 1) for i in range(count)], axis=0)


def pair_rows(v, *after):
    if fold_of() == 1:
        return v
    core = lax.axis_index("head") % 2
    got = tie(swap_pair(pick(v, core)), *after)
    return join(side_of(), v, join(core, got, swap_core(got)))


def my_part(v):
    if fold_of() == 1:
        return v, None
    half = v.shape[0] // 2
    at = side_of()
    return jnp.where(at == 0, v[:half], v[half:]), jnp.where(at == 0, v[half:], v[:half])


def side_parts(masters):
    parts = [my_part(m.astype(bf16)) for m in masters]
    mine = jnp.concatenate([p[0] for p in parts], axis=0)
    if fold_of() == 2:
        away = jnp.concatenate([p[1] for p in parts], axis=0)
        mine = join(side_of(), mine, swap_pair(away), axis=1)
    return mine


def gathered(mine):
    return lax.all_gather(mine, "seq", axis=1, tiled=True, axis_index_groups=lines_of())


def line_scatter(grad):
    return lax.psum_scatter(grad, "seq", scatter_dimension=1, tiled=True, axis_index_groups=lines_of())


def columns_of_sides(summed):
    if fold_of() == 1:
        return [summed.astype(f32)]
    at = side_of()
    mine, other = pick(summed, at, 1), swap_pair(pick(summed, 1 - at, 1))
    return [jnp.where(at == 0, mine, other).astype(f32), jnp.where(at == 0, other, mine).astype(f32)]


def both(sides, lo, hi):
    return jnp.concatenate([s[lo:hi] for s in sides], axis=0)


def states_in(final):
    fold, count = fold_of(), lax.axis_size("seq")
    onward = [(i, i + fold) for i in range(count - fold)]
    bias, move = final[:, :, :VAL], final[:, :, VAL:].astype(bf16)
    state = jnp.zeros_like(bias).astype(bf16)
    for hop in range(count // fold - 1):
        sent = bias if hop == 0 else batched(move, state) + bias
        state = lax.ppermute(sent.astype(bf16), "seq", onward)
    return state, move


def states_back(local, move):
    fold, count = fold_of(), lax.axis_size("seq")
    onward = [(i + fold, i) for i in range(count - fold)]
    state = jnp.zeros_like(local).astype(bf16)
    for hop in range(count // fold - 1):
        sent = local if hop == 0 else batched_t(move, state) + local
        state = lax.ppermute(sent.astype(bf16), "seq", onward)
    return state.astype(f32)


def on_device(
    tokens, cotangent, norm1_gain, w_query, w_key, w_value, w_gate_out, w_alpha, w_beta,
    conv_query, conv_key, conv_value, a_log, dt_bias, out_gain, w_out, norm2_gain, w_gate, w_up, w_down,
):
    fold, side = fold_of(), side_of()
    shards = lax.axis_size("seq")
    model = tokens.shape[1]
    share = model // shards
    all_heads = w_alpha.shape[1]
    heads = all_heads // fold
    hidden = w_gate.shape[1] // fold
    keys, vals = heads * KEY, heads * VAL
    width = 2 * keys + vals
    head_at = lax.axis_index("head") * all_heads + side * heads

    proj_parts = side_parts([w_query.T, w_key.T, w_value.T])
    proj_weight = gathered(proj_parts)
    mid_weight = gathered(side_parts([w_gate_out.T, w_out]))
    gate_weight, out_weight = mid_weight[:vals], mid_weight[vals:]
    mlp_parts = side_parts([w_gate.T, w_up.T, w_down])
    mlp_weight = gathered(mlp_parts)
    mlp_gate, mlp_up, mlp_down = (mlp_weight[i * hidden : (i + 1) * hidden] for i in range(3))
    mlp_in = mlp_weight[: 2 * hidden]

    small = [norm1_gain, norm2_gain, w_alpha, w_beta, conv_query, conv_key, conv_value, a_log, dt_bias, out_gain]
    flat = jnp.concatenate([s.astype(bf16).reshape(-1) for s in small])
    flat = shards_of(jnp.pad(flat, (0, -flat.shape[0] % 1024))).astype(f32)
    parts, at = [], 0
    for s in small:
        parts.append(flat[:, at : at + s.size].reshape((shards,) + s.shape))
        at += s.size
    gain_first, gain_second = parts[0].reshape(-1), parts[1].reshape(-1)
    of_side = lambda v, axis: lax.dynamic_slice_in_dim(v, side * heads, heads, axis)
    mix_weight = jnp.concatenate(
        [of_side(parts[2].reshape(model, all_heads), 1), of_side(parts[3].reshape(model, all_heads), 1)], axis=1
    )
    mix_weight = jnp.pad(mix_weight, ((0, 0), (0, 128 - 2 * heads))).astype(bf16)
    taps = jnp.concatenate(
        [of_side(jnp.moveaxis(p, 0, 2).reshape(4, all_heads, -1), 1).reshape(4, -1) for p in parts[4:7]], axis=1
    )
    taps = jnp.pad(taps, ((0, 4), (0, 0)))
    rate = lax.dynamic_slice_in_dim(parts[7].reshape(-1), head_at, heads)
    bias = lax.dynamic_slice_in_dim(parts[8].reshape(-1), head_at, heads)
    gain_out = parts[9].reshape(1, -1)
    par = jnp.pad(jnp.stack([jnp.exp(rate), bias]), ((0, 6), (0, 128 - heads)))

    inputs = pair_rows(tie(tokens, proj_parts)).astype(f32)
    row_count = inputs.shape[0]
    scale_first = lax.rsqrt(jnp.mean(inputs * inputs, axis=1, keepdims=True) + eps_norm)
    normed_first = (inputs * scale_first * gain_first).astype(bf16)
    proj = dot_right(normed_first, proj_weight).astype(bf16)
    mix_pre = dot_rows(normed_first, mix_weight)
    forward = [(i, i + fold) for i in range(shards - fold)]
    backward = [(i + fold, i) for i in range(shards - fold)]
    edge = lax.ppermute(proj[row_count - HALO :], "seq", forward)
    value_out, ident, inverse, states, final = delta_forward(proj, edge, taps, mix_pre, par)
    gate_pre = dot_right(normed_first, gate_weight)
    entering, move = states_in(final)
    order = unit_order(row_count // UNIT)
    places = jnp.stack(order[0] + order[1] + [order[2]])
    both_cot = pair_rows(tie(cotangent, proj), final)
    both_cot, turned_first = reordered(places, both_cot, normed_first)
    entering = tie(entering, both_cot)
    outputs, gated = gated_outputs(places, value_out, ident, entering, gate_pre, gain_out)
    half = row_count // 2
    attention = summed_rows(chip_sum(dot_rows(gated[half:], out_weight), dot_rows(gated[:half], out_weight)))
    own_inputs = own_blocks(tokens)
    hidden_state = [x.astype(f32) + v.astype(f32) for x, v in zip(own_inputs, attention)]
    scale_second = [lax.rsqrt(jnp.mean(v * v, axis=1, keepdims=True) + eps_norm) for v in hidden_state]
    hat_second = [v * r for v, r in zip(hidden_state, scale_second)]
    normed_second = all_rows([(v * gain_second).astype(bf16) for v in hat_second], (mlp_weight,) if fold == 2 else ())
    act = dot_right(mlp_in, normed_second)
    gate_act, up_act = act[:hidden], act[hidden:]
    sig = jax.nn.sigmoid(gate_act)
    mixed = (gate_act * sig * up_act).astype(bf16)
    grad_mixed = dot_right(mlp_down, both_cot)
    grad_act = jnp.concatenate(
        [grad_mixed * up_act * sig * (1.0 + gate_act * (1.0 - sig)), grad_mixed * (gate_act * sig)], axis=0
    ).astype(bf16)
    mine = chip_sum(dot_left(grad_act[:, half:], mlp_in), dot_left(grad_act[:, :half], mlp_in))
    in_grad = dot_rows(tie(grad_act, mine), normed_second).astype(bf16)
    down_grad = dot_rows(tie(mixed, in_grad), both_cot).astype(bf16)
    in_sum = line_scatter(in_grad)
    down_sum = line_scatter(tie(down_grad, in_sum))
    grad_normed_second = summed_rows(mine, *(((in_grad,), (down_grad,)) if fold == 2 else ()))
    grad_hidden = []
    for d, v, hat, r in zip(own_blocks(cotangent), grad_normed_second, hat_second, scale_second):
        g = v.astype(f32) * gain_second
        grad_hidden.append(d.astype(f32) + r * (g - hat * jnp.mean(g * hat, axis=1, keepdims=True)))
    attention_rounded = [v.astype(bf16) for v in grad_hidden]
    grad_gain_second = jnp.sum(
        mlp_in.astype(f32) * lax.optimization_barrier(in_grad).astype(f32), axis=0
    ) / gain_second
    near_rounded = own_tokens(attention_rounded)
    attention_rounded = tie(all_rows(attention_rounded), in_sum)
    grad_gated = dot_right(attention_rounded, out_weight)
    mixed = tie(mixed, grad_gated)
    branch = summed_rows(chip_sum(dot_left(mixed[:, half:], mlp_down), dot_left(mixed[:, :half], mlp_down)))
    result = own_tokens([(v + w.astype(f32)).astype(bf16) for v, w in zip(hidden_state, branch)])
    grad_outputs, grad_gate, grad_gain_out, local_pull = gate_backward(
        places, grad_gated, outputs, gate_pre, gain_out, ident
    )
    out_grad = dot_left(gated, attention_rounded).astype(bf16)
    gate_grad = dot_left(grad_gate, turned_first).astype(bf16)
    leaving = states_back(local_pull, move)
    leaving = tie(leaving, out_grad, gate_grad, down_sum)
    mid_sum = line_scatter(jnp.concatenate([out_grad, gate_grad], axis=0))
    grad_proj, grad_mix, grad_taps, grad_par, grad_head = delta_backward(
        places, proj, edge, taps, mix_pre, par, grad_outputs, inverse, states, entering, leaving
    )
    following = lax.ppermute(grad_head, "seq", backward)
    fixes = []
    for s in range(3):
        fixes.append(sum(taps[3 - j] * following[s - 3 + j] for j in range(3 - s, 4)))
    at_end = order[1][-1] * UNIT + (1 ^ order[2]) * ROWS + ROWS - HALO
    ending = lax.dynamic_slice_in_dim(grad_proj, at_end, HALO).astype(f32)
    ending = (ending + jnp.pad(jnp.stack(fixes), ((HALO - 3, 0), (0, 0)))).astype(bf16)
    grad_proj = lax.dynamic_update_slice_in_dim(grad_proj, ending, at_end, 0)
    mix_turned = mix_weight.T
    first = lambda lo, hi: (
        dot_rows(grad_proj[lo:hi], proj_weight)
        + dot_rows(grad_gate[lo:hi], gate_weight)
        + dot_rows(grad_mix[lo:hi], mix_turned)
    )
    mine = chip_sum(first(half, row_count), first(0, half))
    proj_grad = dot_left(tie(grad_proj, mine), turned_first).astype(bf16)
    last_sum = line_scatter(tie(proj_grad, mid_sum))
    grad_normed_first = summed_rows(mine, (proj_grad,) if fold == 2 else ())
    grad_taps, grad_par, grad_mix, gate_grad = (
        tie(v, grad_normed_first[0]) for v in (grad_taps, grad_par, grad_mix, gate_grad)
    )
    grad_normed_first = own_tokens(grad_normed_first, last_sum).astype(f32)
    taps_sum = jnp.sum(grad_taps.reshape(4, 8, width), axis=1)
    par_sum = jnp.sum(grad_par.reshape(2, 8, 128), axis=1)
    every = jnp.zeros((2, shards * a_log.shape[0]), f32)
    every = lax.dynamic_update_slice(every, par_sum[:, :heads], (0, head_at))

    def by_shard(lo, like):
        block = taps_sum[:, lo : lo + like.shape[2] * shards * heads].reshape(4, heads, shards, like.shape[2])
        return jnp.moveaxis(block, 2, 0).reshape(shards, -1)

    few = jnp.concatenate(
        [every[0].reshape(shards, -1), every[1].reshape(shards, -1), jnp.sum(grad_gain_out, axis=0).reshape(shards, -1)],
        axis=1,
    )
    few = jnp.pad(few, ((0, 0), (0, share - few.shape[1]))).reshape(1, model)
    of_taps = jnp.concatenate(
        [by_shard(0, conv_query), by_shard(keys, conv_key), by_shard(2 * keys, conv_value)], axis=1
    ).reshape(shards, heads, share)
    of_taps = jnp.moveaxis(of_taps, 1, 0).reshape(heads, model)
    mix_grad = dot_left(grad_mix, turned_first)
    done_grad, done_gate = (tie(proj_grad, grad_mix), gate_grad)
    products = (
        jnp.sum(proj_weight.astype(f32) * done_grad.astype(f32), axis=0)
        + jnp.sum(gate_weight.astype(f32) * done_gate.astype(f32), axis=0)
        + jnp.sum(mix_turned.astype(f32) * mix_grad, axis=0)
    )
    extra = jnp.concatenate(
        [mix_grad[: 2 * heads], of_taps, (products / gain_first)[None], grad_gain_second[None], few], axis=0
    )
    extra = line_total(extra)
    extra_sides = columns_of_sides(lax.dynamic_slice_in_dim(extra, lax.axis_index("seq") // fold * fold * share, fold * share, 1))
    grad_down, grad_mid, grad_last = columns_of_sides(down_sum), columns_of_sides(mid_sum), columns_of_sides(last_sum)
    grad_in = columns_of_sides(in_sum)

    small_at = 2 * heads
    shared = sum(s[small_at + heads : small_at + heads + 3] for s in extra_sides)
    if fold == 2:
        shared = shared + swap_core(shared)
        shared = shared + swap_chip(shared)
    else:
        shared = lax.psum(shared, "head")
    few = shared[2]
    n_rate, n_gain = a_log.shape[0], out_gain.shape[0]
    filters = []
    for like, lo in ((conv_query, 0), (conv_key, 1), (conv_value, 2)):
        n = 4 * heads * like.shape[2]
        start = (0, 4 * heads * conv_query.shape[2], 8 * heads * conv_query.shape[2])[lo]
        filters.append(jnp.concatenate(
            [s[small_at : small_at + heads].reshape(-1)[start : start + n].reshape(4, heads, -1) for s in extra_sides],
            axis=1,
        ))
    own_inputs = tokens.astype(f32)
    own_scale = lax.rsqrt(jnp.mean(own_inputs * own_inputs, axis=1, keepdims=True) + eps_norm)
    own_hat = own_inputs * own_scale
    g = grad_normed_first * gain_first
    grad_tokens = near_rounded.astype(f32) + own_scale * (
        g - own_hat * jnp.mean(g * own_hat, axis=1, keepdims=True)
    )
    return (
        result,
        grad_tokens,
        shared[0],
        both(grad_last, 0, keys).T,
        both(grad_last, keys, 2 * keys).T,
        both(grad_last, 2 * keys, width).T,
        both(grad_mid, vals, 2 * vals).T,
        both(extra_sides, 0, heads).T,
        both(extra_sides, heads, 2 * heads).T,
        filters[0],
        filters[1],
        filters[2],
        few[:n_rate],
        few[n_rate : 2 * n_rate],
        few[2 * n_rate : 2 * n_rate + n_gain],
        both(grad_mid, 0, vals),
        shared[1],
        both(grad_in, 0, hidden).T,
        both(grad_in, hidden, 2 * hidden).T,
        both(grad_down, 0, hidden),
    )


def solution(mesh):
    P = jax.sharding.PartitionSpec
    rows, vector, filters, turned = P("seq", None), P("seq"), P(None, "head", "seq"), P("head", "seq")
    matrix = P("seq", "head")
    placed = (rows, rows, vector) + (matrix,) * 6 + (filters,) * 3 + (vector,) * 3 + (
        turned, vector, matrix, matrix, turned)
    return jax.shard_map(
        on_device, mesh=mesh, in_specs=placed, out_specs=placed, check_vma=False
    )
```

```python
import functools
import jax
import jax.numpy as jnp
from jax import lax
from jax.experimental import pallas as pl
from jax.experimental.pallas import tpu as pltpu

ROWS = 128
KEY = 128
VAL = 256
HALO = 16
eps_norm = 1e-06
f32 = jnp.float32
bf16 = jnp.bfloat16


def mm(a, b):
    return lax.dot_general(
        a.astype(bf16), b.astype(bf16), (((1,), (0,)), ((), ())), preferred_element_type=f32
    )


def mm_nt(a, b):
    return lax.dot_general(
        a.astype(bf16), b.astype(bf16), (((1,), (1,)), ((), ())), preferred_element_type=f32
    )


def mm_tn(a, b):
    return lax.dot_general(
        a.astype(bf16), b.astype(bf16), (((0,), (0,)), ((), ())), preferred_element_type=f32
    )


def mm_full(a, b):
    return lax.dot_general(
        a, b, (((1,), (0,)), ((), ())), precision=lax.Precision.HIGHEST, preferred_element_type=f32
    )


def sigmoid(x):
    return 1.0 / (1.0 + jnp.exp(-x))


def softplus(x):
    return jnp.maximum(x, 0.0) + jnp.log(1.0 + jnp.exp(-jnp.abs(x)))


def positions():
    rows = lax.broadcasted_iota(jnp.int32, (ROWS, ROWS), 0)
    cols = lax.broadcasted_iota(jnp.int32, (ROWS, ROWS), 1)
    return rows, cols


def decay_terms(heads, ab, par):
    rows, cols = positions()
    log_decay = -par[0:1, :] * softplus(ab + par[1:2, :])
    running = mm_full((rows >= cols).astype(f32), log_decay)
    return log_decay, running, running.T, sigmoid(ab)


def ratio_of(running, running_rows, h, rows, cols):
    gap = running[:, h : h + 1] - running_rows[h : h + 1, :]
    return jnp.where(rows >= cols, jnp.exp(jnp.where(rows >= cols, gap, 0.0)), 0.0)


def conv_at(xs_ref, taps_ref, base, lo, width):
    total = taps_ref[0:1, lo : lo + width] * xs_ref[base - 3 : base - 3 + ROWS, lo : lo + width]
    for i in range(1, 4):
        total = total + taps_ref[i : i + 1, lo : lo + width] * (
            xs_ref[base - 3 + i : base - 3 + i + ROWS, lo : lo + width]
        )
    return total


def forward_kernel(heads, proj_ref, edge_ref, taps_ref, ab_ref, par_ref,
                   value_ref, ident_ref, inv_ref, state_ref, final_ref, xs_ref, s_ref):
    step = pl.program_id(0)
    keys = heads * KEY

    @pl.when(step == 0)
    def _():
        xs_ref[0:HALO, :] = edge_ref[...].astype(f32)
        r, c = positions()
        for h in range(heads):
            s_ref[h, :, 0:VAL] = jnp.zeros((KEY, VAL), f32)
            s_ref[h, :, VAL:] = (r == c).astype(f32)

    span = proj_ref.shape[0]
    subs = range(span // ROWS)

    @pl.when(step > 0)
    def _():
        xs_ref[0:HALO, :] = xs_ref[span : span + HALO, :]

    xs_ref[HALO : HALO + span, :] = proj_ref[...].astype(f32)
    rows, cols = positions()
    every = [(s, h) for s in subs for h in range(heads)]
    running, running_rows, strength = [], [], []
    for s in subs:
        terms = decay_terms(heads, ab_ref[s * ROWS : (s + 1) * ROWS, :], par_ref[...])
        running.append(terms[1])
        running_rows.append(terms[2])
        strength.append(terms[3])
    q, k, v, a, p, t, beta, grow = {}, {}, {}, {}, {}, {}, {}, {}
    for s, h in every:
        base = HALO + s * ROWS
        u = conv_at(xs_ref, taps_ref, base, h * KEY, KEY)
        u = u * sigmoid(u)
        q[s, h] = u * (lax.rsqrt(jnp.sum(u * u, axis=1, keepdims=True) + eps_norm) * KEY**-0.5)
        w = conv_at(xs_ref, taps_ref, base, keys + h * KEY, KEY)
        w = w * sigmoid(w)
        k[s, h] = w * lax.rsqrt(jnp.sum(w * w, axis=1, keepdims=True) + eps_norm)
        x = conv_at(xs_ref, taps_ref, base, 2 * keys + h * VAL, VAL)
        v[s, h] = x * sigmoid(x)
        beta[s, h] = strength[s][:, heads + h : heads + h + 1]
        grow[s, h] = jnp.exp(running[s][:, h : h + 1])
    for s, h in every:
        ratio = ratio_of(running[s], running_rows[s], h, rows, cols)
        gram = mm_nt(k[s, h], k[s, h])
        a[s, h] = jnp.where(rows > cols, ratio * gram, 0.0) * beta[s, h]
        p[s, h] = ratio * mm_nt(q[s, h], k[s, h])
    first = (rows // 2 == cols // 2) & (rows > cols)
    for e in every:
        t[e] = (rows == cols).astype(f32) - jnp.where(first, a[e], 0.0)
    b = 2
    while b < ROWS:
        low = (rows // (2 * b) == cols // (2 * b)) & ((rows // b) % 2 == 1) & ((cols // b) % 2 == 0)
        inner = {e: mm(jnp.where(low, a[e], 0.0), t[e]) for e in every}
        t = {e: t[e] - mm(t[e], inner[e]) for e in every}
        b *= 2
    uw = {
        e: mm(t[e], jnp.concatenate([beta[e] * v[e], (beta[e] * grow[e]) * k[e]], axis=1))
        for e in every
    }
    for s, h in every:
        inv_ref[s * ROWS : (s + 1) * ROWS, h * KEY : (h + 1) * KEY] = t[s, h].astype(bf16)
    for s, h in every:
        at = slice(s * ROWS, (s + 1) * ROWS)
        state = s_ref[h]
        state_ref[s, h] = state.astype(bf16)
        pred = mm(uw[s, h][:, VAL:], state)
        err = jnp.concatenate([uw[s, h][:, :VAL] - pred[:, :VAL], -pred[:, VAL:]], axis=1)
        out = grow[s, h] * mm(q[s, h], state) + mm(p[s, h], err)
        value_ref[at, h * VAL : (h + 1) * VAL] = out[:, :VAL]
        ident_ref[at, h * KEY : (h + 1) * KEY] = out[:, VAL:].astype(bf16)
        end = running[s][ROWS - 1 : ROWS, h : h + 1]
        tail = jnp.exp(end - running[s][:, h : h + 1]) * k[s, h]
        s_ref[h] = jnp.exp(end) * state + mm_tn(tail, err)

    @pl.when(step == pl.num_programs(0) - 1)
    def _():
        final_ref[...] = s_ref[...]


def sub_blocks(heads):
    return 2


def delta_forward(proj, edge, taps, ab, par):
    tokens = proj.shape[0]
    heads = proj.shape[1] // (2 * KEY + VAL)
    keys, vals = heads * KEY, heads * VAL
    subs = sub_blocks(heads)
    span = subs * ROWS
    blocks = tokens // span
    width = proj.shape[1]
    whole = lambda *shape: pl.BlockSpec(shape, lambda c: (0,) * len(shape))
    return pl.pallas_call(
        functools.partial(forward_kernel, heads),
        grid=(blocks,),
        in_specs=[
            pl.BlockSpec((span, width), lambda c: (c, 0)),
            whole(HALO, width),
            whole(8, width),
            pl.BlockSpec((span, 128), lambda c: (c, 0)),
            whole(8, 128),
        ],
        out_specs=[
            pl.BlockSpec((span, vals), lambda c: (c, 0)),
            pl.BlockSpec((span, keys), lambda c: (c, 0)),
            pl.BlockSpec((span, keys), lambda c: (c, 0)),
            pl.BlockSpec((subs, heads, KEY, VAL + KEY), lambda c: (c, 0, 0, 0)),
            whole(heads, KEY, VAL + KEY),
        ],
        out_shape=[
            jax.ShapeDtypeStruct((tokens, vals), f32),
            jax.ShapeDtypeStruct((tokens, keys), bf16),
            jax.ShapeDtypeStruct((tokens, keys), bf16),
            jax.ShapeDtypeStruct((blocks * subs, heads, KEY, VAL + KEY), bf16),
            jax.ShapeDtypeStruct((heads, KEY, VAL + KEY), f32),
        ],
        scratch_shapes=[
            pltpu.VMEM((HALO + span, width), f32),
            pltpu.VMEM((heads, KEY, VAL + KEY), f32),
        ],
        compiler_params=pltpu.CompilerParams(
            dimension_semantics=("arbitrary",), vmem_limit_bytes=48 * 2**20
        ),
    )(proj, edge, taps, ab, par)


UNIT = 2 * ROWS


def placed_rows(order_ref, sub):
    flip = order_ref[order_ref.shape[0] - 1]
    return pl.ds(pl.multiple_of((flip + sub - 2 * flip * sub) * ROWS, ROWS), ROWS)


def reorder_kernel(order_ref, *refs):
    count = len(refs) // 2
    for in_ref, out_ref in zip(refs[:count], refs[count:]):
        for sub in range(2):
            out_ref[placed_rows(order_ref, sub), :] = in_ref[sub * ROWS : (sub + 1) * ROWS, :]


def reordered(order, *arrays):
    tokens = arrays[0].shape[0]
    return pl.pallas_call(
        reorder_kernel,
        grid_spec=pltpu.PrefetchScalarGridSpec(
            num_scalar_prefetch=1,
            grid=(tokens // UNIT,),
            in_specs=[pl.BlockSpec((UNIT, a.shape[1]), lambda c, order: (order[c], 0)) for a in arrays],
            out_specs=[pl.BlockSpec((UNIT, a.shape[1]), lambda c, order: (c, 0)) for a in arrays],
        ),
        out_shape=[jax.ShapeDtypeStruct(a.shape, a.dtype) for a in arrays],
        compiler_params=pltpu.CompilerParams(
            dimension_semantics=("arbitrary",), vmem_limit_bytes=32 * 2**20
        ),
    )(order, *arrays)


def output_kernel(heads, order_ref, value_ref, ident_ref, state_ref, gate_ref, gain_ref, out_ref, gated_ref):
    for h in range(heads):
        span = slice(h * VAL, (h + 1) * VAL)
        out = value_ref[:, span] + mm(ident_ref[:, h * KEY : (h + 1) * KEY], state_ref[h])
        out_ref[:, span] = out
        gate = gate_ref[:, span]
        unit = out * lax.rsqrt(jnp.mean(out * out, axis=1, keepdims=True) + eps_norm)
        gated = (unit * gain_ref[0:1, :] * (gate * sigmoid(gate))).astype(bf16)
        for sub in range(2):
            gated_ref[placed_rows(order_ref, sub), span] = gated[sub * ROWS : (sub + 1) * ROWS]


def gated_outputs(order, value_out, ident, state_in, gate_pre, gain):
    tokens, vals = value_out.shape
    heads = vals // VAL
    placed = lambda width: pl.BlockSpec((UNIT, width), lambda c, order: (order[c], 0))
    return pl.pallas_call(
        functools.partial(output_kernel, heads),
        grid_spec=pltpu.PrefetchScalarGridSpec(
            num_scalar_prefetch=1,
            grid=(tokens // UNIT,),
            in_specs=[
                placed(vals),
                placed(heads * KEY),
                pl.BlockSpec((heads, KEY, VAL), lambda c, order: (0, 0, 0)),
                placed(vals),
                pl.BlockSpec((1, VAL), lambda c, order: (0, 0)),
            ],
            out_specs=[placed(vals), pl.BlockSpec((UNIT, vals), lambda c, order: (c, 0))],
        ),
        out_shape=[
            jax.ShapeDtypeStruct((tokens, vals), f32),
            jax.ShapeDtypeStruct((tokens, vals), bf16),
        ],
        compiler_params=pltpu.CompilerParams(
            dimension_semantics=("arbitrary",), vmem_limit_bytes=48 * 2**20
        ),
    )(order, value_out, ident, state_in, gate_pre, gain)


def gate_back_kernel(heads, order_ref, grad_ref, out_ref, gate_ref, gain_ref, ident_ref,
                     dout_ref, dgate_ref, dgain_ref, pull_ref):
    @pl.when(pl.program_id(0) == 0)
    def _():
        dgain_ref[...] = jnp.zeros_like(dgain_ref)
        pull_ref[...] = jnp.zeros_like(pull_ref)

    gain = gain_ref[0:1, :]
    for h in range(heads):
        span = slice(h * VAL, (h + 1) * VAL)
        grad = jnp.concatenate([grad_ref[placed_rows(order_ref, sub), span] for sub in range(2)], axis=0)
        out, gate = out_ref[:, span], gate_ref[:, span]
        scale = lax.rsqrt(jnp.mean(out * out, axis=1, keepdims=True) + eps_norm)
        unit = out * scale
        sig = sigmoid(gate)
        m = grad * (gate * sig)
        mn = m * unit
        dgain_ref[...] += jnp.sum(mn.reshape(-1, 8, VAL), axis=0)
        mean = jnp.mean(mn * gain, axis=1, keepdims=True)
        dout = (scale * (m * gain - unit * mean)).astype(bf16)
        dout_ref[:, span] = dout
        dgate = (grad * unit * gain * (sig * (1.0 + gate * (1.0 - sig)))).astype(bf16)
        for sub in range(2):
            dgate_ref[placed_rows(order_ref, sub), span] = dgate[sub * ROWS : (sub + 1) * ROWS]
        pull_ref[h] += mm_tn(ident_ref[:, h * KEY : (h + 1) * KEY], dout)


def gate_backward(order, grad_gated, outputs, gate_pre, gain, ident):
    tokens, vals = outputs.shape
    heads = vals // VAL
    placed = lambda width: pl.BlockSpec((UNIT, width), lambda c, order: (order[c], 0))
    return pl.pallas_call(
        functools.partial(gate_back_kernel, heads),
        grid_spec=pltpu.PrefetchScalarGridSpec(
            num_scalar_prefetch=1,
            grid=(tokens // UNIT,),
            in_specs=[
                pl.BlockSpec((UNIT, vals), lambda c, order: (c, 0)),
                placed(vals),
                placed(vals),
                pl.BlockSpec((1, VAL), lambda c, order: (0, 0)),
                placed(heads * KEY),
            ],
            out_specs=[
                placed(vals),
                pl.BlockSpec((UNIT, vals), lambda c, order: (c, 0)),
                pl.BlockSpec((8, VAL), lambda c, order: (0, 0)),
                pl.BlockSpec((heads, KEY, VAL), lambda c, order: (0, 0, 0)),
            ],
        ),
        out_shape=[
            jax.ShapeDtypeStruct((tokens, vals), bf16),
            jax.ShapeDtypeStruct((tokens, vals), bf16),
            jax.ShapeDtypeStruct((8, VAL), f32),
            jax.ShapeDtypeStruct((heads, KEY, VAL), f32),
        ],
        compiler_params=pltpu.CompilerParams(
            dimension_semantics=("arbitrary",), vmem_limit_bytes=48 * 2**20
        ),
    )(order, grad_gated, outputs, gate_pre, gain, ident)


def backward_kernel(heads, order_ref, gate_ref, proj_ref, before_ref, edge_ref, taps_ref, ab_ref, par_ref, dout_ref,
                    inv_ref, state_ref, enter_ref, dfinal_ref,
                    dproj_ref, dtaps_ref, dpar_ref, dhead_ref,
                    xs_ref, gs_ref, ds_ref):
    step = pl.program_id(0)
    last = pl.num_programs(0) - 1
    keys = heads * KEY
    width = 2 * keys + heads * VAL
    span = proj_ref.shape[0]

    @pl.when(step == 0)
    def _():
        ds_ref[...] = dfinal_ref[...]
        dtaps_ref[...] = jnp.zeros_like(dtaps_ref)
        dpar_ref[...] = jnp.zeros_like(dpar_ref)
        gs_ref[span : span + 8, :] = jnp.zeros((8, width), f32)

    @pl.when(step > 0)
    def _():
        gs_ref[span : span + 8, :] = gs_ref[0:8, :]

    @pl.when(step == last)
    def _():
        xs_ref[0:HALO, :] = edge_ref[...].astype(f32)

    @pl.when(step < last)
    def _():
        xs_ref[0:HALO, :] = before_ref[...].astype(f32)

    xs_ref[HALO : HALO + span, :] = proj_ref[...].astype(f32)
    rows, cols = positions()
    par = par_ref[...]
    lane = lax.broadcasted_iota(jnp.int32, (ROWS, 128), 1)
    row_at = lax.broadcasted_iota(jnp.int32, (ROWS, 1), 0)
    for s in reversed(range(span // ROWS)):
        at = slice(s * ROWS, (s + 1) * ROWS)
        ab = ab_ref[at, :]
        log_decay, running, running_rows, strength = decay_terms(heads, ab, par)
        drunning = jnp.zeros((ROWS, 128), f32)
        dbeta = jnp.zeros((ROWS, 128), f32)

        for h in range(heads):
            qs, ks, vs = h * KEY, keys + h * KEY, 2 * keys + h * VAL
            u = conv_at(xs_ref, taps_ref, HALO + s * ROWS, qs, KEY)
            su = sigmoid(u)
            wu = u * su
            ru = lax.rsqrt(jnp.sum(wu * wu, axis=1, keepdims=True) + eps_norm)
            q = wu * (ru * KEY**-0.5)
            y = conv_at(xs_ref, taps_ref, HALO + s * ROWS, ks, KEY)
            sy = sigmoid(y)
            wy = y * sy
            ry = lax.rsqrt(jnp.sum(wy * wy, axis=1, keepdims=True) + eps_norm)
            k = wy * ry
            x = conv_at(xs_ref, taps_ref, HALO + s * ROWS, vs, VAL)
            sx = sigmoid(x)
            v = x * sx
            qb, kb = q.astype(bf16), k.astype(bf16)
            beta = strength[:, heads + h : heads + h + 1]
            passed = running[:, h : h + 1]
            grow = jnp.exp(passed)
            end = running[ROWS - 1 : ROWS, h : h + 1]
            tail = jnp.exp(end - passed)
            ratio = ratio_of(running, running_rows, h, rows, cols)
            p = ratio * mm_nt(qb, kb)
            t = inv_ref[at, h * KEY : (h + 1) * KEY]
            dout = dout_ref[at, h * VAL : (h + 1) * VAL]
            state = state_ref[s, h, :, :VAL].astype(f32) + mm(state_ref[s, h, :, VAL:], enter_ref[h])
            state_b = state.astype(bf16)
            dstate = ds_ref[h]
            dstate_b = dstate.astype(bf16)
            err = mm(t, beta * (v - grow * mm(kb, state_b)))
            err_b = err.astype(bf16)
            derr = mm_tn(p, dout) + mm(tail * k, dstate_b)
            dright = mm_tn(t, derr)
            dright_b = dright.astype(bf16)
            dp = mm_nt(dout, err_b) * ratio
            dp_b = dp.astype(bf16)
            da = jnp.where(rows > cols, mm_nt(dright_b, err_b) * ratio, 0.0) * (-beta)
            da_b = da.astype(bf16)
            back = (beta * grow) * dright
            back_b = back.astype(bf16)
            dq = grow * mm_nt(dout, state_b) + mm(dp_b, kb)
            dk_read = mm(da_b, kb) - mm_nt(back_b, state_b)
            dk_tail = tail * mm_nt(err_b, dstate_b)
            dk_write = mm_tn(dp_b, qb) + mm_tn(da_b, kb) + dk_tail
            dk = dk_read + dk_write
            dv = beta * dright
            to_beta = (1.0 - beta) * jnp.sum(dright * err, axis=1, keepdims=True)
            to_decay = jnp.sum(q * dq + k * (dk_read - dk_write), axis=1, keepdims=True)
            at_end = jnp.exp(end) * jnp.sum(
                jnp.sum(state * dstate, axis=1, keepdims=True), axis=0, keepdims=True
            ) + jnp.sum(jnp.sum(k * dk_tail, axis=1, keepdims=True), axis=0, keepdims=True)
            to_decay = to_decay + jnp.where(row_at == ROWS - 1, at_end, 0.0)
            drunning = jnp.where(lane == h, to_decay, drunning)
            dbeta = jnp.where(lane == heads + h, to_beta, dbeta)
            ds_ref[h] = jnp.exp(end) * dstate + mm_tn(grow * q, dout) - mm_tn(kb, back_b)
            along = jnp.sum(wu * dq, axis=1, keepdims=True)
            du = (KEY**-0.5) * (ru * dq - wu * (ru * ru * ru * along))
            gs_ref[at, qs : qs + KEY] = du * (su * (1.0 + u * (1.0 - su)))
            along = jnp.sum(wy * dk, axis=1, keepdims=True)
            dy = ry * dk - wy * (ry * ry * ry * along)
            gs_ref[at, ks : ks + KEY] = dy * (sy * (1.0 + y * (1.0 - sy)))
            gs_ref[at, vs : vs + VAL] = dv * (sx * (1.0 + x * (1.0 - sx)))

        dlog = mm_full((rows <= cols).astype(f32), drunning)
        dalpha = -dlog * par[0:1, :] * sigmoid(ab + par[1:2, :])
        dproj_ref[placed_rows(order_ref, s), width + heads * VAL :] = jnp.where(lane < heads, dalpha, dbeta).astype(bf16)
        dpar_ref[0:8, :] += jnp.sum((dlog * log_decay).reshape(-1, 8, 128), axis=0)
        dpar_ref[8:16, :] += jnp.sum(dalpha.reshape(-1, 8, 128), axis=0)

    for lo in range(0, width, 256):
        lanes = slice(lo, lo + 256)
        grad = gs_ref[0:span, lanes]
        total = taps_ref[3:4, lanes] * grad
        for i in range(4):
            moved = xs_ref[HALO - 3 + i : HALO - 3 + i + span, lanes] * grad
            dtaps_ref[8 * i : 8 * i + 8, lanes] += jnp.sum(moved.reshape(-1, 8, 256), axis=0)
            if i < 3:
                total = total + taps_ref[i : i + 1, lanes] * gs_ref[3 - i : 3 - i + span, lanes]
        total = total.astype(bf16)
        for s in range(2):
            dproj_ref[placed_rows(order_ref, s), lanes] = total[s * ROWS : (s + 1) * ROWS]

    dproj_ref[:, width : width + heads * VAL] = gate_ref[...]

    @pl.when(step == last)
    def _():
        dhead_ref[...] = gs_ref[0:8, :]


def delta_backward(order, dgate, proj, edge, taps, ab, par, dout, inverse, states, entering, dfinal):
    tokens, width = proj.shape
    heads = width // (2 * KEY + VAL)
    keys, vals = heads * KEY, heads * VAL
    subs = sub_blocks(heads)
    span = subs * ROWS
    blocks = tokens // span
    whole = lambda *shape: pl.BlockSpec(shape, lambda c, order: (0,) * len(shape))
    rev = lambda w: pl.BlockSpec((span, w), lambda c, order: (blocks - 1 - c, 0))
    sent = lambda w: pl.BlockSpec((span, w), lambda c, order: (order[blocks + blocks - 1 - c], 0))
    per = span // HALO
    return pl.pallas_call(
        functools.partial(backward_kernel, heads),
        grid_spec=pltpu.PrefetchScalarGridSpec(
            num_scalar_prefetch=1,
            grid=(blocks,),
            in_specs=[
                sent(vals),
                rev(width),
                pl.BlockSpec((HALO, width), lambda c, order: (jnp.maximum((blocks - 1 - c) * per - 1, 0), 0)),
                whole(HALO, width),
                whole(8, width),
                rev(128),
                whole(8, 128),
                rev(vals),
                rev(keys),
                pl.BlockSpec((subs, heads, KEY, VAL + KEY), lambda c, order: (blocks - 1 - c, 0, 0, 0)),
                whole(heads, KEY, VAL),
                whole(heads, KEY, VAL),
            ],
            out_specs=[
                sent(width + vals + 128),
                whole(32, width),
                whole(16, 128),
                whole(8, width),
            ],
            scratch_shapes=[
                pltpu.VMEM((HALO + span, width), f32),
                pltpu.VMEM((span + 8, width), f32),
                pltpu.VMEM((heads, KEY, VAL), f32),
            ],
        ),
        out_shape=[
            jax.ShapeDtypeStruct((tokens, width + vals + 128), bf16),
            jax.ShapeDtypeStruct((32, width), f32),
            jax.ShapeDtypeStruct((16, 128), f32),
            jax.ShapeDtypeStruct((8, width), f32),
        ],
        compiler_params=pltpu.CompilerParams(
            dimension_semantics=("arbitrary",), vmem_limit_bytes=56 * 2**20
        ),
    )(order, dgate, proj, proj, edge, taps, ab, par, dout, inverse, states, entering, dfinal)


def assemble_kernel(parts, *refs):
    out_ref, sems = refs[-2], refs[-1]
    copies, at = [], 0
    for i, (which, start, rows) in enumerate(parts):
        copies.append(pltpu.make_async_copy(
            refs[which].at[pl.ds(start, rows)], out_ref.at[pl.ds(at, rows)], sems.at[i]))
        at += rows
    for copy in copies:
        copy.start()
    for copy in copies:
        copy.wait()


def assembled(pieces, parts):
    rows = sum(p[2] for p in parts)
    return pl.pallas_call(
        functools.partial(assemble_kernel, parts),
        in_specs=[pl.BlockSpec(memory_space=pltpu.VMEM)] * len(pieces),
        out_specs=pl.BlockSpec(memory_space=pl.ANY),
        out_shape=jax.ShapeDtypeStruct((rows,) + pieces[0].shape[1:], pieces[0].dtype),
        scratch_shapes=[pltpu.SemaphoreType.DMA((len(parts),))],
        compiler_params=pltpu.CompilerParams(vmem_limit_bytes=32 * 2**20),
    )(*pieces)


def dot_rows(a, b):
    return lax.dot_general(a, b, (((1,), (0,)), ((), ())), preferred_element_type=f32)


def dot_left(a, b):
    return lax.dot_general(a, b, (((0,), (0,)), ((), ())), preferred_element_type=f32)


def dot_right(a, b):
    return lax.dot_general(a, b, (((1,), (1,)), ((), ())), preferred_element_type=f32)


def batched(a, b):
    return lax.dot_general(a, b, (((2,), (1,)), ((0,), (0,))), preferred_element_type=f32)


def batched_t(a, b):
    return lax.dot_general(a, b, (((1,), (1,)), ((0,), (0,))), preferred_element_type=f32)


def tie(first, *then):
    return lax.optimization_barrier((first, *then))[0] if then else first


def fold_of():
    return 2 if lax.axis_size("seq") == 8 and lax.axis_size("head") == 4 else 1


def lines_of():
    fold = fold_of()
    return [list(range(x, lax.axis_size("seq"), fold)) for x in range(fold)]


def side_of():
    return lax.axis_index("seq") % fold_of()


def swap_pair(v):
    return lax.ppermute(v, "seq", [(i, i ^ 1) for i in range(lax.axis_size("seq"))])


def swap_chip(v):
    return lax.ppermute(v, "head", [(i, i ^ 2) for i in range(4)])


def swap_core(v):
    return lax.ppermute(v, "head", [(i, i ^ 1) for i in range(4)])


def pick(v, at, axis=0):
    half = v.shape[axis] // 2
    return lax.dynamic_slice_in_dim(v, at * half, half, axis)


def join(at, mine, other, axis=0):
    first, second = jnp.where(at == 0, mine, other), jnp.where(at == 0, other, mine)
    return jnp.concatenate([first, second], axis=axis)


def plus(a, b):
    return (a.astype(f32) + b.astype(f32)).astype(bf16)


def place_of():
    core, chip = lax.axis_index("head") % 2, lax.axis_index("head") // 2
    return core, chip, side_of()


def unit_order(count):
    if fold_of() == 1:
        same = [jnp.int32(i) for i in range(count)]
        return same, same, jnp.int32(0)
    core, chip, side = place_of()
    bits = [(i // 4, i // 2 % 2, i % 2) for i in range(8)]
    at_place = [((s ^ side) * 4 + (c ^ core) * 2 + kind).astype(jnp.int32) for c, kind, s in bits]
    of_unit = [((c ^ core) * 4 + kind * 2 + (s ^ side)).astype(jnp.int32) for s, c, kind in bits]
    return at_place, of_unit, chip.astype(jnp.int32)


def chip_sum(away, near):
    if fold_of() == 1:
        return jnp.concatenate([near, away], axis=0).astype(bf16)
    return plus(lax.optimization_barrier(near.astype(bf16)), swap_core(away.astype(bf16)))


def together(*arrays):
    return lax.optimization_barrier(arrays)


def first_exchange(mine):
    if fold_of() == 1:
        return (mine,)
    n = mine.shape[0] // 8
    blocks = [mine[i * n : (i + 1) * n] for i in range(8)]
    keep, give = (jnp.concatenate([blocks[4 + i], blocks[6 + i]], axis=0) for i in range(2))
    by_x, by_y = together(mine[2 * n : 4 * n], give)
    return mine[: 2 * n], keep, swap_pair(by_x), swap_chip(by_y)


def first_total(parts, *beside):
    if fold_of() == 1:
        return parts
    a, b, far_a, far_b = together(*parts, *beside)[:4]
    return together(plus(a, far_a), plus(b, far_b))


def second_exchange(parts):
    if fold_of() == 1:
        return parts
    a, b = parts
    n = a.shape[0] // 2
    return a[:n], b[:n], swap_chip(a[n:]), swap_pair(b[n:])


def second_total(parts, *beside):
    if fold_of() == 1:
        return [lax.psum(parts[0], "head")]
    a, b, far_a, far_b = together(*parts, *beside)[:4]
    return list(together(plus(a, far_a), plus(b, far_b)))


def all_rows(pieces, beside=(), work=None):
    if fold_of() == 1:
        return pieces[0], () if work is None else work(pieces[0])
    a, b = together(*pieces)
    far_a, far_b = together(swap_chip(a), swap_pair(b), *beside)[:2]
    a, b = together(jnp.concatenate([a, far_a], axis=0), jnp.concatenate([b, far_b], axis=0))
    done = () if work is None else work(a)
    far_a, far_b, *done = together(swap_pair(a), swap_chip(b), *done)
    n = far_b.shape[0] // 2
    near = together(a, far_a, b, far_b)
    far = together(*(swap_core(v) for v in near))
    parts = []
    for at in (0, 4):
        parts += [(at, 0, 2 * n), (at + 1, 0, 2 * n)]
        parts += [(at + 2, 0, n), (at + 3, 0, n), (at + 2, n, n), (at + 3, n, n)]
    return assembled(near + far, tuple(parts)), tuple(done)


def chip_rows(pieces):
    if fold_of() == 1:
        return pieces
    a, b = pieces
    both_here = jnp.concatenate([a, b], axis=0)
    return both_here, swap_chip(both_here)


def own_tokens(parts, *beside):
    if fold_of() == 1:
        return parts[0]
    core, chip, _ = place_of()
    here, far = together(*parts, *beside)[:2]
    n = here.shape[0] // 2
    near = jnp.concatenate([join(chip, here[:n], far[:n]), join(chip, here[n:], far[n:])], axis=0)
    return join(core, near, swap_core(near))


def own_blocks(v):
    if fold_of() == 1:
        return [v]
    core, chip, _ = place_of()
    n = v.shape[0] // 8
    return [lax.dynamic_slice_in_dim(v, core * 4 * n + kind * 2 * n + chip * n, n) for kind in range(2)]


def line_total(v):
    fold, step = fold_of(), fold_of()
    while step < lax.axis_size("seq"):
        v = v + lax.ppermute(v, "seq", [(i, i ^ step) for i in range(lax.axis_size("seq"))])
        step *= 2
    return v


def shards_of(v):
    count, step = lax.axis_size("seq"), 1
    held = v[None]
    while step < count:
        held = jnp.concatenate(
            [held, lax.ppermute(held, "seq", [(i, i ^ step) for i in range(count)])], axis=0
        )
        step *= 2
    me = lax.axis_index("seq")
    return jnp.concatenate([lax.dynamic_slice_in_dim(held, me ^ i, 1) for i in range(count)], axis=0)


def pair_rows(v, *after):
    if fold_of() == 1:
        return v
    core = lax.axis_index("head") % 2
    got = tie(swap_pair(pick(v, core)), *after)
    return join(side_of(), v, join(core, got, swap_core(got)))


def my_part(v):
    if fold_of() == 1:
        return v, None
    half = v.shape[0] // 2
    at = side_of()
    return jnp.where(at == 0, v[:half], v[half:]), jnp.where(at == 0, v[half:], v[:half])


def side_parts(masters):
    parts = [my_part(m.astype(bf16)) for m in masters]
    mine = jnp.concatenate([p[0] for p in parts], axis=0)
    if fold_of() == 2:
        away = jnp.concatenate([p[1] for p in parts], axis=0)
        mine = join(side_of(), mine, swap_pair(away), axis=1)
    return mine


def gathered(mine):
    return lax.all_gather(mine, "seq", axis=1, tiled=True, axis_index_groups=lines_of())


def line_scatter(grad, axis=1):
    return lax.psum_scatter(grad, "seq", scatter_dimension=axis, tiled=True, axis_index_groups=lines_of())


def swapped_share(summed, axis=1):
    return swap_pair(pick(summed, 1 - side_of(), axis)) if fold_of() == 2 else None


def in_sides(summed, other, axis=1):
    if fold_of() == 1:
        return [summed.astype(f32)]
    at = side_of()
    mine = pick(summed, at, axis)
    return [jnp.where(at == 0, mine, other).astype(f32), jnp.where(at == 0, other, mine).astype(f32)]


def both(sides, lo, hi):
    return jnp.concatenate([s[lo:hi] for s in sides], axis=0)


def states_in(final):
    fold, count = fold_of(), lax.axis_size("seq")
    onward = [(i, i + fold) for i in range(count - fold)]
    bias, move = final[:, :, :VAL], final[:, :, VAL:].astype(bf16)
    state = jnp.zeros_like(bias).astype(bf16)
    for hop in range(count // fold - 1):
        sent = bias if hop == 0 else batched(move, state) + bias
        state = lax.ppermute(sent.astype(bf16), "seq", onward)
    return state, jnp.swapaxes(move, 1, 2)


def states_back(local, turned, works):
    fold, count = fold_of(), lax.axis_size("seq")
    onward = [(i + fold, i) for i in range(count - fold)]
    sent, carried = local.astype(bf16), ()
    for hop in range(count // fold - 1):
        if hop:
            sent = (batched(turned, state) + local).astype(bf16)
        state = lax.ppermute(sent, "seq", onward)
        if hop < len(works):
            carried = works[hop](sent, carried)
        state, *carried = together(state, *carried)
    return state.astype(f32), carried


def on_device(
    tokens, cotangent, norm1_gain, w_query, w_key, w_value, w_gate_out, w_alpha, w_beta,
    conv_query, conv_key, conv_value, a_log, dt_bias, out_gain, w_out, norm2_gain, w_gate, w_up, w_down,
):
    fold, side = fold_of(), side_of()
    shards = lax.axis_size("seq")
    model = tokens.shape[1]
    share = model // shards
    all_heads = w_alpha.shape[1]
    heads = all_heads // fold
    hidden = w_gate.shape[1] // fold
    keys, vals = heads * KEY, heads * VAL
    width = 2 * keys + vals
    head_at = lax.axis_index("head") * all_heads + side * heads

    proj_parts = side_parts([w_query.T, w_key.T, w_value.T])
    proj_weight = gathered(proj_parts)
    mid_weight = gathered(side_parts([w_gate_out.T, w_out]))
    gate_weight, out_weight = mid_weight[:vals], mid_weight[vals:]
    mlp_parts = side_parts([w_gate.T, w_up.T, w_down])
    mlp_weight = gathered(mlp_parts)
    mlp_gate, mlp_up, mlp_down = (mlp_weight[i * hidden : (i + 1) * hidden] for i in range(3))
    mlp_in = mlp_weight[: 2 * hidden]

    small = [norm1_gain, norm2_gain, w_alpha, w_beta, conv_query, conv_key, conv_value, a_log, dt_bias, out_gain]
    flat = jnp.concatenate([s.astype(bf16).reshape(-1) for s in small])
    flat = shards_of(jnp.pad(flat, (0, -flat.shape[0] % 1024))).astype(f32)
    parts, at = [], 0
    for s in small:
        parts.append(flat[:, at : at + s.size].reshape((shards,) + s.shape))
        at += s.size
    gain_first, gain_second = parts[0].reshape(-1), parts[1].reshape(-1)
    of_side = lambda v, axis: lax.dynamic_slice_in_dim(v, side * heads, heads, axis)
    mix_weight = jnp.concatenate(
        [of_side(parts[2].reshape(model, all_heads), 1), of_side(parts[3].reshape(model, all_heads), 1)], axis=1
    )
    mix_weight = jnp.pad(mix_weight, ((0, 0), (0, 128 - 2 * heads))).astype(bf16)
    taps = jnp.concatenate(
        [of_side(jnp.moveaxis(p, 0, 2).reshape(4, all_heads, -1), 1).reshape(4, -1) for p in parts[4:7]], axis=1
    )
    taps = jnp.pad(taps, ((0, 4), (0, 0)))
    rate = lax.dynamic_slice_in_dim(parts[7].reshape(-1), head_at, heads)
    bias = lax.dynamic_slice_in_dim(parts[8].reshape(-1), head_at, heads)
    gain_out = parts[9].reshape(1, -1)
    par = jnp.pad(jnp.stack([jnp.exp(rate), bias]), ((0, 6), (0, 128 - heads)))

    inputs = pair_rows(tie(tokens, proj_parts)).astype(f32)
    row_count = inputs.shape[0]
    scale_first = lax.rsqrt(jnp.mean(inputs * inputs, axis=1, keepdims=True) + eps_norm)
    normed_first = (inputs * scale_first * gain_first).astype(bf16)
    proj = dot_right(normed_first, proj_weight).astype(bf16)
    mix_pre = dot_rows(normed_first, mix_weight)
    forward = [(i, i + fold) for i in range(shards - fold)]
    backward = [(i + fold, i) for i in range(shards - fold)]
    edge = lax.ppermute(proj[row_count - HALO :], "seq", forward)
    value_out, ident, inverse, states, final = delta_forward(proj, edge, taps, mix_pre, par)
    gate_pre = dot_right(normed_first, gate_weight)
    entering, move = states_in(final)
    order = unit_order(row_count // UNIT)
    places = jnp.stack(order[0] + order[1] + [order[2]])
    both_cot = pair_rows(tie(cotangent, proj), final)
    both_cot, turned_first = reordered(places, both_cot, normed_first)
    mix_turned = mix_weight.T
    side_weight = jnp.concatenate(
        [tie(proj_weight, both_cot), tie(gate_weight, both_cot), tie(mix_turned, both_cot)], axis=0
    )
    entering = tie(entering, both_cot)
    outputs, gated = gated_outputs(places, value_out, ident, entering, gate_pre, gain_out)
    half = row_count // 2
    mine = chip_sum(dot_rows(gated[half:], out_weight), dot_rows(gated[:half], out_weight))
    attention = second_total(second_exchange(first_total(first_exchange(mine))))
    own_inputs = own_blocks(tokens)
    hidden_state = [x.astype(f32) + v.astype(f32) for x, v in zip(own_inputs, attention)]
    scale_second = [lax.rsqrt(jnp.mean(v * v, axis=1, keepdims=True) + eps_norm) for v in hidden_state]
    hat_second = [v * r for v, r in zip(hidden_state, scale_second)]
    normed_second, _ = all_rows([(v * gain_second).astype(bf16) for v in hat_second], (mlp_weight,))
    act = dot_right(mlp_in, normed_second)
    gate_act, up_act = act[:hidden], act[hidden:]
    sig = jax.nn.sigmoid(gate_act)
    mixed = (gate_act * sig * up_act).astype(bf16)
    grad_mixed = dot_right(mlp_down, both_cot)
    grad_act = jnp.concatenate(
        [grad_mixed * up_act * sig * (1.0 + gate_act * (1.0 - sig)), grad_mixed * (gate_act * sig)], axis=0
    ).astype(bf16)
    mine = chip_sum(dot_left(grad_act[:, half:], mlp_in), dot_left(grad_act[:, :half], mlp_in))
    down_grad = dot_rows(tie(mixed, mine), both_cot).astype(bf16)
    in_grad = dot_rows(tie(grad_act, down_grad), normed_second).astype(bf16)
    down_sum = line_scatter(down_grad)
    in_sum = line_scatter(tie(in_grad, down_sum))
    grad_normed_second = first_total(first_exchange(mine), down_grad, in_grad)
    grad_normed_second = second_total(second_exchange(grad_normed_second))
    grad_hidden = []
    for d, v, hat, r in zip(own_blocks(cotangent), grad_normed_second, hat_second, scale_second):
        g = v.astype(f32) * gain_second
        grad_hidden.append(d.astype(f32) + r * (g - hat * jnp.mean(g * hat, axis=1, keepdims=True)))
    attention_rounded = [v.astype(bf16) for v in grad_hidden]
    gain_part = sum(
        jnp.sum(v.astype(f32) * hat, axis=0) for v, hat in zip(grad_normed_second, hat_second)
    )

    if fold == 1:
        gain_part = gain_part / lax.axis_size("head")

    def branch_beside(after):
        m = tie(mixed, after, down_sum)
        return (chip_sum(dot_left(m[:, half:], mlp_down), dot_left(m[:, :half], mlp_down)),)

    attention_rounded, (branch,) = all_rows(attention_rounded, (), branch_beside)
    branch, attention_rounded = together(branch, attention_rounded)
    branch = first_exchange(branch)
    grad_gated = dot_right(attention_rounded, out_weight)
    grad_outputs, grad_gate, grad_gain_out, local_pull = gate_backward(
        places, grad_gated, outputs, gate_pre, gain_out, ident
    )

    line_in = in_sum

    def first_work(sent, carried):
        parts = first_total(branch, sent)
        return dot_left(gated, tie(attention_rounded, parts[0])).astype(bf16), *parts

    def second_work(sent, carried):
        parts = second_exchange(tuple(carried[1:]))
        return carried[0], dot_left(tie(grad_gate, sent), turned_first).astype(bf16), *parts

    def third_work(sent, carried):
        parts = second_total(tuple(carried[2:]))
        rows = [(v + w.astype(f32)).astype(bf16) for v, w in zip(hidden_state, parts)]
        return jnp.concatenate(carried[:2], axis=0), line_in, *rows

    leaving, (mid_grad, in_sum, *result) = states_back(local_pull, move, (first_work, second_work, third_work))
    leaving, mid_grad, down_sum, *result = together(leaving, mid_grad, down_sum, *result)
    result = chip_rows(result)
    in_other, down_other = swapped_share(in_sum), swapped_share(down_sum)
    mid_sum = line_scatter(tie(mid_grad, in_sum))
    grad_side, grad_taps, grad_par, grad_head = delta_backward(
        places, grad_gate, proj, edge, taps, mix_pre, par, grad_outputs, inverse, states, entering, leaving
    )
    following = lax.ppermute(grad_head, "seq", backward)
    fixes = []
    for s in range(3):
        fixes.append(sum(taps[3 - j] * following[s - 3 + j] for j in range(3 - s, 4)))
    at_end = order[1][-1] * UNIT + (1 ^ order[2]) * ROWS + ROWS - HALO
    if fold == 2:
        grad_side, in_other, down_other, *result = together(grad_side, in_other, down_other, *result)
    ending = lax.dynamic_slice(grad_side, (at_end, 0), (HALO, width)).astype(f32)
    ending = (ending + jnp.pad(jnp.stack(fixes), ((HALO - 3, 0), (0, 0)))).astype(bf16)
    grad_side = lax.dynamic_update_slice(grad_side, ending, (at_end, 0))
    proj_grad = dot_left(turned_first, grad_side[:, :width]).astype(bf16)
    last_sum = line_scatter(proj_grad, 0)
    away = dot_rows(tie(grad_side, proj_grad, mid_sum)[half:], side_weight).astype(bf16)
    near = dot_rows(tie(grad_side, away)[:half], side_weight)
    mine = chip_sum(away, near)
    grad_normed_first = first_exchange(mine)
    in_sum, down_sum, mid_sum, grad_taps, grad_par, grad_side, proj_grad = (
        tie(v, mine) for v in (in_sum, down_sum, mid_sum, grad_taps, grad_par, grad_side, proj_grad)
    )
    taps_sum = jnp.sum(grad_taps.reshape(4, 8, width), axis=1)
    par_sum = jnp.sum(grad_par.reshape(2, 8, 128), axis=1)
    every = jnp.zeros((2, shards * a_log.shape[0]), f32)
    every = lax.dynamic_update_slice(every, par_sum[:, :heads], (0, head_at))
    mix_grad = dot_left(grad_side[:, width + vals :], turned_first)
    few = jnp.concatenate([every.reshape(1, -1), jnp.sum(grad_gain_out, axis=0).reshape(1, -1)], axis=1)
    fill = lambda v: jnp.pad(v, ((0, 0), (0, model - v.shape[1])))
    extra = jnp.concatenate([gain_part[None], fill(few), mix_grad[: 2 * heads], fill(taps_sum)], axis=0)
    extra = jnp.pad(extra, ((0, -extra.shape[0] % 8), (0, 0)))
    grad_down, grad_in = in_sides(down_sum, down_other), in_sides(in_sum, in_other)
    ready = (
        both(grad_in, 0, hidden).T, both(grad_in, hidden, 2 * hidden).T, both(grad_down, 0, hidden),
    )
    step = lambda v, by: lax.ppermute(v, "seq", [(i, i ^ by) for i in range(shards)])
    if fold == 2:
        far_a, far_b, extra, *ready = together(*grad_normed_first[2:], extra, *ready)
        grad_normed_first = first_total((*grad_normed_first[:2], far_a, far_b))
        far_extra = step(tie(extra, grad_normed_first[0]), 2)
        own_result = own_tokens([tie(v, grad_normed_first[0]) for v in result])
        grad_normed_first = second_total(second_exchange(grad_normed_first), far_extra, own_result)
        extra = extra + tie(far_extra, grad_normed_first[0])
    else:
        own_result = own_tokens(result)
        grad_normed_first, extra = second_total(grad_normed_first), line_total(extra)
    after = grad_normed_first[0]
    grad_tokens, gain_row = [], 0.0
    for x, d, v in zip(own_inputs, grad_hidden, grad_normed_first):
        x, v = x.astype(f32), v.astype(f32)
        r = lax.rsqrt(jnp.mean(x * x, axis=1, keepdims=True) + eps_norm)
        hat = x * r
        g = v * gain_first
        gain_row = gain_row + jnp.sum(v * hat, axis=0, keepdims=True)
        grad_tokens.append((d + r * (g - hat * jnp.mean(g * hat, axis=1, keepdims=True))).astype(bf16))
    grad_tokens = chip_rows(grad_tokens)
    mid_other = swapped_share(tie(mid_sum, after))
    if fold == 2:
        far_extra, far_row = step(extra, 4), step(gain_row, 2)
        *grad_tokens, far_extra, far_row, last_sum = together(*grad_tokens, far_extra, far_row, last_sum)
        extra, gain_row = extra + far_extra, gain_row + far_row
        last_other, other, far_row = swap_pair(pick(last_sum, 1 - side, 0)), swap_pair(extra), step(gain_row, 4)
        grad_tokens = own_tokens(grad_tokens).astype(f32)
        gain_row = gain_row + far_row
        gain_row = gain_row + swap_pair(gain_row)
        sides = [jnp.where(side == 0, extra, other), jnp.where(side == 0, other, extra)]
        shared = jnp.concatenate([gain_row, extra[:2] + other[:2]], axis=0)
        shared = shared + swap_core(shared)
        shared = shared + swap_chip(shared)
    else:
        last_other, sides = None, [extra]
        grad_tokens = own_tokens(grad_tokens).astype(f32)
        gain_row = line_total(gain_row) / lax.axis_size("head")
        shared = lax.psum(jnp.concatenate([gain_row, extra[:2]], axis=0), "head")
    result = own_result
    me = lax.axis_index("seq")
    take = lambda v, at, n: lax.dynamic_slice_in_dim(v, at, n, v.ndim - 1)
    grad_alpha = jnp.concatenate([take(v[2 : 2 + heads], me * share, share) for v in sides], axis=0).T
    grad_beta = jnp.concatenate([take(v[2 + heads : 2 + 2 * heads], me * share, share) for v in sides], axis=0).T
    filters = []
    for like, lo, size in ((conv_query, 0, KEY), (conv_key, keys, KEY), (conv_value, 2 * keys, VAL)):
        n = like.shape[2]
        filters.append(jnp.stack(
            [take(v[2 + 2 * heads : 6 + 2 * heads], lo + h * size + me * n, n) for v in sides for h in range(heads)],
            axis=1,
        ))
    n_rate, n_gain = a_log.shape[0], out_gain.shape[0]
    few = shared[2]
    grad_mid, grad_last = in_sides(mid_sum, mid_other), in_sides(last_sum, last_other, 0)
    channels = lambda lo, hi: jnp.concatenate([v[:, lo:hi] for v in grad_last], axis=1)

    return (
        result,
        grad_tokens,
        take(shared[0], me * share, share),
        channels(0, keys),
        channels(keys, 2 * keys),
        channels(2 * keys, width),
        both(grad_mid, vals, 2 * vals).T,
        grad_alpha,
        grad_beta,
        filters[0],
        filters[1],
        filters[2],
        take(few, me * n_rate, n_rate),
        take(few, (shards + me) * n_rate, n_rate),
        take(few, 2 * shards * n_rate + me * n_gain, n_gain),
        both(grad_mid, 0, vals),
        take(shared[1], me * share, share),
        *ready,
    )


def solution(mesh):
    P = jax.sharding.PartitionSpec
    rows, vector, filters, turned = P("seq", None), P("seq"), P(None, "head", "seq"), P("head", "seq")
    matrix = P("seq", "head")
    placed = (rows, rows, vector) + (matrix,) * 6 + (filters,) * 3 + (vector,) * 3 + (
        turned, vector, matrix, matrix, turned)
    return jax.shard_map(
        on_device, mesh=mesh, in_specs=placed, out_specs=placed, check_vma=False
    )
```

```python
import functools
import jax
import jax.numpy as jnp
from jax import lax
from jax.experimental import pallas as pl
from jax.experimental.pallas import tpu as pltpu

ROWS = 128
KEY = 128
VAL = 256
HALO = 16
eps_norm = 1e-06
f32 = jnp.float32
bf16 = jnp.bfloat16


def mm(a, b):
    return lax.dot_general(
        a.astype(bf16), b.astype(bf16), (((1,), (0,)), ((), ())), preferred_element_type=f32
    )


def mm_nt(a, b):
    return lax.dot_general(
        a.astype(bf16), b.astype(bf16), (((1,), (1,)), ((), ())), preferred_element_type=f32
    )


def mm_tn(a, b):
    return lax.dot_general(
        a.astype(bf16), b.astype(bf16), (((0,), (0,)), ((), ())), preferred_element_type=f32
    )


def mm_full(a, b):
    return lax.dot_general(
        a, b, (((1,), (0,)), ((), ())), precision=lax.Precision.HIGHEST, preferred_element_type=f32
    )


def sigmoid(x):
    return 1.0 / (1.0 + jnp.exp(-x))


def softplus(x):
    return jnp.maximum(x, 0.0) + jnp.log(1.0 + jnp.exp(-jnp.abs(x)))


def positions():
    rows = lax.broadcasted_iota(jnp.int32, (ROWS, ROWS), 0)
    cols = lax.broadcasted_iota(jnp.int32, (ROWS, ROWS), 1)
    return rows, cols


def decay_terms(heads, ab, par):
    rows, cols = positions()
    log_decay = -par[0:1, :] * softplus(ab + par[1:2, :])
    running = mm_full((rows >= cols).astype(f32), log_decay)
    return log_decay, running, running.T, sigmoid(ab)


def ratio_of(running, running_rows, h, rows, cols):
    gap = running[:, h : h + 1] - running_rows[h : h + 1, :]
    return jnp.where(rows >= cols, jnp.exp(jnp.where(rows >= cols, gap, 0.0)), 0.0)


def conv_at(xs_ref, taps_ref, base, lo, width):
    total = taps_ref[0:1, lo : lo + width] * xs_ref[base - 3 : base - 3 + ROWS, lo : lo + width]
    for i in range(1, 4):
        total = total + taps_ref[i : i + 1, lo : lo + width] * (
            xs_ref[base - 3 + i : base - 3 + i + ROWS, lo : lo + width]
        )
    return total


def forward_kernel(heads, proj_ref, edge_ref, taps_ref, ab_ref, par_ref,
                   value_ref, ident_ref, inv_ref, state_ref, final_ref, xs_ref, s_ref):
    step = pl.program_id(0)
    keys = heads * KEY

    @pl.when(step == 0)
    def _():
        xs_ref[0:HALO, :] = edge_ref[...].astype(f32)
        r, c = positions()
        for h in range(heads):
            s_ref[h, :, 0:VAL] = jnp.zeros((KEY, VAL), f32)
            s_ref[h, :, VAL:] = (r == c).astype(f32)

    span = proj_ref.shape[0]
    subs = range(span // ROWS)

    @pl.when(step > 0)
    def _():
        xs_ref[0:HALO, :] = xs_ref[span : span + HALO, :]

    xs_ref[HALO : HALO + span, :] = proj_ref[...].astype(f32)
    rows, cols = positions()
    every = [(s, h) for s in subs for h in range(heads)]
    running, running_rows, strength = [], [], []
    for s in subs:
        terms = decay_terms(heads, ab_ref[s * ROWS : (s + 1) * ROWS, :], par_ref[...])
        running.append(terms[1])
        running_rows.append(terms[2])
        strength.append(terms[3])
    q, k, v, a, p, t, beta, grow = {}, {}, {}, {}, {}, {}, {}, {}
    for s, h in every:
        base = HALO + s * ROWS
        u = conv_at(xs_ref, taps_ref, base, h * KEY, KEY)
        u = u * sigmoid(u)
        q[s, h] = u * (lax.rsqrt(jnp.sum(u * u, axis=1, keepdims=True) + eps_norm) * KEY**-0.5)
        w = conv_at(xs_ref, taps_ref, base, keys + h * KEY, KEY)
        w = w * sigmoid(w)
        k[s, h] = w * lax.rsqrt(jnp.sum(w * w, axis=1, keepdims=True) + eps_norm)
        x = conv_at(xs_ref, taps_ref, base, 2 * keys + h * VAL, VAL)
        v[s, h] = x * sigmoid(x)
        beta[s, h] = strength[s][:, heads + h : heads + h + 1]
        grow[s, h] = jnp.exp(running[s][:, h : h + 1])
    for s, h in every:
        ratio = ratio_of(running[s], running_rows[s], h, rows, cols)
        gram = mm_nt(k[s, h], k[s, h])
        a[s, h] = jnp.where(rows > cols, ratio * gram, 0.0) * beta[s, h]
        p[s, h] = ratio * mm_nt(q[s, h], k[s, h])
    first = (rows // 2 == cols // 2) & (rows > cols)
    for e in every:
        t[e] = (rows == cols).astype(f32) - jnp.where(first, a[e], 0.0)
    b = 2
    while b < ROWS:
        low = (rows // (2 * b) == cols // (2 * b)) & ((rows // b) % 2 == 1) & ((cols // b) % 2 == 0)
        inner = {e: mm(jnp.where(low, a[e], 0.0), t[e]) for e in every}
        t = {e: t[e] - mm(t[e], inner[e]) for e in every}
        b *= 2
    uw = {
        e: mm(t[e], jnp.concatenate([beta[e] * v[e], (beta[e] * grow[e]) * k[e]], axis=1))
        for e in every
    }
    for s, h in every:
        inv_ref[s * ROWS : (s + 1) * ROWS, h * KEY : (h + 1) * KEY] = t[s, h].astype(bf16)
    for s, h in every:
        at = slice(s * ROWS, (s + 1) * ROWS)
        state = s_ref[h]
        state_ref[s, h] = state.astype(bf16)
        pred = mm(uw[s, h][:, VAL:], state)
        err = jnp.concatenate([uw[s, h][:, :VAL] - pred[:, :VAL], -pred[:, VAL:]], axis=1)
        out = grow[s, h] * mm(q[s, h], state) + mm(p[s, h], err)
        value_ref[at, h * VAL : (h + 1) * VAL] = out[:, :VAL]
        ident_ref[at, h * KEY : (h + 1) * KEY] = out[:, VAL:].astype(bf16)
        end = running[s][ROWS - 1 : ROWS, h : h + 1]
        tail = jnp.exp(end - running[s][:, h : h + 1]) * k[s, h]
        s_ref[h] = jnp.exp(end) * state + mm_tn(tail, err)

    @pl.when(step == pl.num_programs(0) - 1)
    def _():
        final_ref[...] = s_ref[...]


def sub_blocks(heads):
    return 2


def delta_forward(proj, edge, taps, ab, par):
    tokens = proj.shape[0]
    heads = proj.shape[1] // (2 * KEY + VAL)
    keys, vals = heads * KEY, heads * VAL
    subs = sub_blocks(heads)
    span = subs * ROWS
    blocks = tokens // span
    width = proj.shape[1]
    whole = lambda *shape: pl.BlockSpec(shape, lambda c: (0,) * len(shape))
    return pl.pallas_call(
        functools.partial(forward_kernel, heads),
        grid=(blocks,),
        in_specs=[
            pl.BlockSpec((span, width), lambda c: (c, 0)),
            whole(HALO, width),
            whole(8, width),
            pl.BlockSpec((span, 128), lambda c: (c, 0)),
            whole(8, 128),
        ],
        out_specs=[
            pl.BlockSpec((span, vals), lambda c: (c, 0)),
            pl.BlockSpec((span, keys), lambda c: (c, 0)),
            pl.BlockSpec((span, keys), lambda c: (c, 0)),
            pl.BlockSpec((subs, heads, KEY, VAL + KEY), lambda c: (c, 0, 0, 0)),
            whole(heads, KEY, VAL + KEY),
        ],
        out_shape=[
            jax.ShapeDtypeStruct((tokens, vals), f32),
            jax.ShapeDtypeStruct((tokens, keys), bf16),
            jax.ShapeDtypeStruct((tokens, keys), bf16),
            jax.ShapeDtypeStruct((blocks * subs, heads, KEY, VAL + KEY), bf16),
            jax.ShapeDtypeStruct((heads, KEY, VAL + KEY), f32),
        ],
        scratch_shapes=[
            pltpu.VMEM((HALO + span, width), f32),
            pltpu.VMEM((heads, KEY, VAL + KEY), f32),
        ],
        compiler_params=pltpu.CompilerParams(
            dimension_semantics=("arbitrary",), vmem_limit_bytes=48 * 2**20
        ),
    )(proj, edge, taps, ab, par)


UNIT = 2 * ROWS


def placed_rows(order_ref, sub):
    flip = order_ref[order_ref.shape[0] - 1]
    return pl.ds(pl.multiple_of((flip + sub - 2 * flip * sub) * ROWS, ROWS), ROWS)


def reorder_kernel(order_ref, *refs):
    count = len(refs) // 2
    for in_ref, out_ref in zip(refs[:count], refs[count:]):
        for sub in range(2):
            out_ref[placed_rows(order_ref, sub), :] = in_ref[sub * ROWS : (sub + 1) * ROWS, :]


def reordered(order, *arrays):
    tokens = arrays[0].shape[0]
    return pl.pallas_call(
        reorder_kernel,
        grid_spec=pltpu.PrefetchScalarGridSpec(
            num_scalar_prefetch=1,
            grid=(tokens // UNIT,),
            in_specs=[pl.BlockSpec((UNIT, a.shape[1]), lambda c, order: (order[c], 0)) for a in arrays],
            out_specs=[pl.BlockSpec((UNIT, a.shape[1]), lambda c, order: (c, 0)) for a in arrays],
        ),
        out_shape=[jax.ShapeDtypeStruct(a.shape, a.dtype) for a in arrays],
        compiler_params=pltpu.CompilerParams(
            dimension_semantics=("arbitrary",), vmem_limit_bytes=32 * 2**20
        ),
    )(order, *arrays)


def output_kernel(heads, order_ref, value_ref, ident_ref, state_ref, gate_ref, gain_ref, out_ref, gated_ref):
    for h in range(heads):
        span = slice(h * VAL, (h + 1) * VAL)
        out = value_ref[:, span] + mm(ident_ref[:, h * KEY : (h + 1) * KEY], state_ref[h])
        out_ref[:, span] = out
        gate = gate_ref[:, span]
        unit = out * lax.rsqrt(jnp.mean(out * out, axis=1, keepdims=True) + eps_norm)
        gated = (unit * gain_ref[0:1, :] * (gate * sigmoid(gate))).astype(bf16)
        for sub in range(2):
            gated_ref[placed_rows(order_ref, sub), span] = gated[sub * ROWS : (sub + 1) * ROWS]


def gated_outputs(order, value_out, ident, state_in, gate_pre, gain):
    tokens, vals = value_out.shape
    heads = vals // VAL
    placed = lambda width: pl.BlockSpec((UNIT, width), lambda c, order: (order[c], 0))
    return pl.pallas_call(
        functools.partial(output_kernel, heads),
        grid_spec=pltpu.PrefetchScalarGridSpec(
            num_scalar_prefetch=1,
            grid=(tokens // UNIT,),
            in_specs=[
                placed(vals),
                placed(heads * KEY),
                pl.BlockSpec((heads, KEY, VAL), lambda c, order: (0, 0, 0)),
                placed(vals),
                pl.BlockSpec((1, VAL), lambda c, order: (0, 0)),
            ],
            out_specs=[placed(vals), pl.BlockSpec((UNIT, vals), lambda c, order: (c, 0))],
        ),
        out_shape=[
            jax.ShapeDtypeStruct((tokens, vals), f32),
            jax.ShapeDtypeStruct((tokens, vals), bf16),
        ],
        compiler_params=pltpu.CompilerParams(
            dimension_semantics=("arbitrary",), vmem_limit_bytes=48 * 2**20
        ),
    )(order, value_out, ident, state_in, gate_pre, gain)


def gate_back_kernel(heads, order_ref, grad_ref, out_ref, gate_ref, gain_ref, ident_ref,
                     dout_ref, dgate_ref, dgain_ref, pull_ref):
    @pl.when(pl.program_id(0) == 0)
    def _():
        dgain_ref[...] = jnp.zeros_like(dgain_ref)
        pull_ref[...] = jnp.zeros_like(pull_ref)

    gain = gain_ref[0:1, :]
    for h in range(heads):
        span = slice(h * VAL, (h + 1) * VAL)
        grad = jnp.concatenate([grad_ref[placed_rows(order_ref, sub), span] for sub in range(2)], axis=0)
        out, gate = out_ref[:, span], gate_ref[:, span]
        scale = lax.rsqrt(jnp.mean(out * out, axis=1, keepdims=True) + eps_norm)
        unit = out * scale
        sig = sigmoid(gate)
        m = grad * (gate * sig)
        mn = m * unit
        dgain_ref[...] += jnp.sum(mn.reshape(-1, 8, VAL), axis=0)
        mean = jnp.mean(mn * gain, axis=1, keepdims=True)
        dout = (scale * (m * gain - unit * mean)).astype(bf16)
        dout_ref[:, span] = dout
        dgate = (grad * unit * gain * (sig * (1.0 + gate * (1.0 - sig)))).astype(bf16)
        for sub in range(2):
            dgate_ref[placed_rows(order_ref, sub), span] = dgate[sub * ROWS : (sub + 1) * ROWS]
        pull_ref[h] += mm_tn(ident_ref[:, h * KEY : (h + 1) * KEY], dout)


def gate_backward(order, grad_gated, outputs, gate_pre, gain, ident):
    tokens, vals = outputs.shape
    heads = vals // VAL
    placed = lambda width: pl.BlockSpec((UNIT, width), lambda c, order: (order[c], 0))
    return pl.pallas_call(
        functools.partial(gate_back_kernel, heads),
        grid_spec=pltpu.PrefetchScalarGridSpec(
            num_scalar_prefetch=1,
            grid=(tokens // UNIT,),
            in_specs=[
                pl.BlockSpec((UNIT, vals), lambda c, order: (c, 0)),
                placed(vals),
                placed(vals),
                pl.BlockSpec((1, VAL), lambda c, order: (0, 0)),
                placed(heads * KEY),
            ],
            out_specs=[
                placed(vals),
                pl.BlockSpec((UNIT, vals), lambda c, order: (c, 0)),
                pl.BlockSpec((8, VAL), lambda c, order: (0, 0)),
                pl.BlockSpec((heads, KEY, VAL), lambda c, order: (0, 0, 0)),
            ],
        ),
        out_shape=[
            jax.ShapeDtypeStruct((tokens, vals), bf16),
            jax.ShapeDtypeStruct((tokens, vals), bf16),
            jax.ShapeDtypeStruct((8, VAL), f32),
            jax.ShapeDtypeStruct((heads, KEY, VAL), f32),
        ],
        compiler_params=pltpu.CompilerParams(
            dimension_semantics=("arbitrary",), vmem_limit_bytes=48 * 2**20
        ),
    )(order, grad_gated, outputs, gate_pre, gain, ident)


def backward_kernel(heads, order_ref, gate_ref, proj_ref, before_ref, edge_ref, taps_ref, ab_ref, par_ref, dout_ref,
                    inv_ref, state_ref, enter_ref, dfinal_ref,
                    dproj_ref, dtaps_ref, dpar_ref, dhead_ref,
                    xs_ref, gs_ref, ds_ref):
    step = pl.program_id(0)
    last = pl.num_programs(0) - 1
    keys = heads * KEY
    width = 2 * keys + heads * VAL
    span = proj_ref.shape[0]

    @pl.when(step == 0)
    def _():
        ds_ref[...] = dfinal_ref[...]
        dtaps_ref[...] = jnp.zeros_like(dtaps_ref)
        dpar_ref[...] = jnp.zeros_like(dpar_ref)
        gs_ref[span : span + 8, :] = jnp.zeros((8, width), f32)

    @pl.when(step > 0)
    def _():
        gs_ref[span : span + 8, :] = gs_ref[0:8, :]

    @pl.when(step == last)
    def _():
        xs_ref[0:HALO, :] = edge_ref[...].astype(f32)

    @pl.when(step < last)
    def _():
        xs_ref[0:HALO, :] = before_ref[...].astype(f32)

    xs_ref[HALO : HALO + span, :] = proj_ref[...].astype(f32)
    rows, cols = positions()
    par = par_ref[...]
    lane = lax.broadcasted_iota(jnp.int32, (ROWS, 128), 1)
    row_at = lax.broadcasted_iota(jnp.int32, (ROWS, 1), 0)
    for s in reversed(range(span // ROWS)):
        at = slice(s * ROWS, (s + 1) * ROWS)
        ab = ab_ref[at, :]
        log_decay, running, running_rows, strength = decay_terms(heads, ab, par)
        drunning = jnp.zeros((ROWS, 128), f32)
        dbeta = jnp.zeros((ROWS, 128), f32)

        for h in range(heads):
            qs, ks, vs = h * KEY, keys + h * KEY, 2 * keys + h * VAL
            u = conv_at(xs_ref, taps_ref, HALO + s * ROWS, qs, KEY)
            su = sigmoid(u)
            wu = u * su
            ru = lax.rsqrt(jnp.sum(wu * wu, axis=1, keepdims=True) + eps_norm)
            q = wu * (ru * KEY**-0.5)
            y = conv_at(xs_ref, taps_ref, HALO + s * ROWS, ks, KEY)
            sy = sigmoid(y)
            wy = y * sy
            ry = lax.rsqrt(jnp.sum(wy * wy, axis=1, keepdims=True) + eps_norm)
            k = wy * ry
            x = conv_at(xs_ref, taps_ref, HALO + s * ROWS, vs, VAL)
            sx = sigmoid(x)
            v = x * sx
            qb, kb = q.astype(bf16), k.astype(bf16)
            beta = strength[:, heads + h : heads + h + 1]
            passed = running[:, h : h + 1]
            grow = jnp.exp(passed)
            end = running[ROWS - 1 : ROWS, h : h + 1]
            tail = jnp.exp(end - passed)
            ratio = ratio_of(running, running_rows, h, rows, cols)
            p = ratio * mm_nt(qb, kb)
            t = inv_ref[at, h * KEY : (h + 1) * KEY]
            dout = dout_ref[at, h * VAL : (h + 1) * VAL]
            state = state_ref[s, h, :, :VAL].astype(f32) + mm(state_ref[s, h, :, VAL:], enter_ref[h])
            state_b = state.astype(bf16)
            dstate = ds_ref[h]
            dstate_b = dstate.astype(bf16)
            err = mm(t, beta * (v - grow * mm(kb, state_b)))
            err_b = err.astype(bf16)
            derr = mm_tn(p, dout) + mm(tail * k, dstate_b)
            dright = mm_tn(t, derr)
            dright_b = dright.astype(bf16)
            dp = mm_nt(dout, err_b) * ratio
            dp_b = dp.astype(bf16)
            da = jnp.where(rows > cols, mm_nt(dright_b, err_b) * ratio, 0.0) * (-beta)
            da_b = da.astype(bf16)
            back = (beta * grow) * dright
            back_b = back.astype(bf16)
            dq = grow * mm_nt(dout, state_b) + mm(dp_b, kb)
            dk_read = mm(da_b, kb) - mm_nt(back_b, state_b)
            dk_tail = tail * mm_nt(err_b, dstate_b)
            dk_write = mm_tn(dp_b, qb) + mm_tn(da_b, kb) + dk_tail
            dk = dk_read + dk_write
            dv = beta * dright
            to_beta = (1.0 - beta) * jnp.sum(dright * err, axis=1, keepdims=True)
            to_decay = jnp.sum(q * dq + k * (dk_read - dk_write), axis=1, keepdims=True)
            at_end = jnp.exp(end) * jnp.sum(
                jnp.sum(state * dstate, axis=1, keepdims=True), axis=0, keepdims=True
            ) + jnp.sum(jnp.sum(k * dk_tail, axis=1, keepdims=True), axis=0, keepdims=True)
            to_decay = to_decay + jnp.where(row_at == ROWS - 1, at_end, 0.0)
            drunning = jnp.where(lane == h, to_decay, drunning)
            dbeta = jnp.where(lane == heads + h, to_beta, dbeta)
            ds_ref[h] = jnp.exp(end) * dstate + mm_tn(grow * q, dout) - mm_tn(kb, back_b)
            along = jnp.sum(wu * dq, axis=1, keepdims=True)
            du = (KEY**-0.5) * (ru * dq - wu * (ru * ru * ru * along))
            gs_ref[at, qs : qs + KEY] = du * (su * (1.0 + u * (1.0 - su)))
            along = jnp.sum(wy * dk, axis=1, keepdims=True)
            dy = ry * dk - wy * (ry * ry * ry * along)
            gs_ref[at, ks : ks + KEY] = dy * (sy * (1.0 + y * (1.0 - sy)))
            gs_ref[at, vs : vs + VAL] = dv * (sx * (1.0 + x * (1.0 - sx)))

        dlog = mm_full((rows <= cols).astype(f32), drunning)
        dalpha = -dlog * par[0:1, :] * sigmoid(ab + par[1:2, :])
        dproj_ref[placed_rows(order_ref, s), width + heads * VAL :] = jnp.where(lane < heads, dalpha, dbeta).astype(bf16)
        dpar_ref[0:8, :] += jnp.sum((dlog * log_decay).reshape(-1, 8, 128), axis=0)
        dpar_ref[8:16, :] += jnp.sum(dalpha.reshape(-1, 8, 128), axis=0)

    for lo in range(0, width, 256):
        lanes = slice(lo, lo + 256)
        grad = gs_ref[0:span, lanes]
        total = taps_ref[3:4, lanes] * grad
        for i in range(4):
            moved = xs_ref[HALO - 3 + i : HALO - 3 + i + span, lanes] * grad
            dtaps_ref[8 * i : 8 * i + 8, lanes] += jnp.sum(moved.reshape(-1, 8, 256), axis=0)
            if i < 3:
                total = total + taps_ref[i : i + 1, lanes] * gs_ref[3 - i : 3 - i + span, lanes]
        total = total.astype(bf16)
        for s in range(2):
            dproj_ref[placed_rows(order_ref, s), lanes] = total[s * ROWS : (s + 1) * ROWS]

    dproj_ref[:, width : width + heads * VAL] = gate_ref[...]

    @pl.when(step == last)
    def _():
        dhead_ref[...] = gs_ref[0:8, :]


def delta_backward(order, dgate, proj, edge, taps, ab, par, dout, inverse, states, entering, dfinal):
    tokens, width = proj.shape
    heads = width // (2 * KEY + VAL)
    keys, vals = heads * KEY, heads * VAL
    subs = sub_blocks(heads)
    span = subs * ROWS
    blocks = tokens // span
    whole = lambda *shape: pl.BlockSpec(shape, lambda c, order: (0,) * len(shape))
    rev = lambda w: pl.BlockSpec((span, w), lambda c, order: (blocks - 1 - c, 0))
    sent = lambda w: pl.BlockSpec((span, w), lambda c, order: (order[blocks + blocks - 1 - c], 0))
    per = span // HALO
    return pl.pallas_call(
        functools.partial(backward_kernel, heads),
        grid_spec=pltpu.PrefetchScalarGridSpec(
            num_scalar_prefetch=1,
            grid=(blocks,),
            in_specs=[
                sent(vals),
                rev(width),
                pl.BlockSpec((HALO, width), lambda c, order: (jnp.maximum((blocks - 1 - c) * per - 1, 0), 0)),
                whole(HALO, width),
                whole(8, width),
                rev(128),
                whole(8, 128),
                rev(vals),
                rev(keys),
                pl.BlockSpec((subs, heads, KEY, VAL + KEY), lambda c, order: (blocks - 1 - c, 0, 0, 0)),
                whole(heads, KEY, VAL),
                whole(heads, KEY, VAL),
            ],
            out_specs=[
                sent(width + vals + 128),
                whole(32, width),
                whole(16, 128),
                whole(8, width),
            ],
            scratch_shapes=[
                pltpu.VMEM((HALO + span, width), f32),
                pltpu.VMEM((span + 8, width), f32),
                pltpu.VMEM((heads, KEY, VAL), f32),
            ],
        ),
        out_shape=[
            jax.ShapeDtypeStruct((tokens, width + vals + 128), bf16),
            jax.ShapeDtypeStruct((32, width), f32),
            jax.ShapeDtypeStruct((16, 128), f32),
            jax.ShapeDtypeStruct((8, width), f32),
        ],
        compiler_params=pltpu.CompilerParams(
            dimension_semantics=("arbitrary",), vmem_limit_bytes=56 * 2**20
        ),
    )(order, dgate, proj, proj, edge, taps, ab, par, dout, inverse, states, entering, dfinal)


def assemble_kernel(parts, *refs):
    out_ref, sems = refs[-2], refs[-1]
    copies, at = [], 0
    for i, (which, start, rows) in enumerate(parts):
        copies.append(pltpu.make_async_copy(
            refs[which].at[pl.ds(start, rows)], out_ref.at[pl.ds(at, rows)], sems.at[i]))
        at += rows
    for copy in copies:
        copy.start()
    for copy in copies:
        copy.wait()


def assembled(pieces, parts):
    rows = sum(p[2] for p in parts)
    return pl.pallas_call(
        functools.partial(assemble_kernel, parts),
        in_specs=[pl.BlockSpec(memory_space=pltpu.VMEM)] * len(pieces),
        out_specs=pl.BlockSpec(memory_space=pl.ANY),
        out_shape=jax.ShapeDtypeStruct((rows,) + pieces[0].shape[1:], pieces[0].dtype),
        scratch_shapes=[pltpu.SemaphoreType.DMA((len(parts),))],
        compiler_params=pltpu.CompilerParams(vmem_limit_bytes=32 * 2**20),
    )(*pieces)


def dot_rows(a, b):
    return lax.dot_general(a, b, (((1,), (0,)), ((), ())), preferred_element_type=f32)


def dot_left(a, b):
    return lax.dot_general(a, b, (((0,), (0,)), ((), ())), preferred_element_type=f32)


def dot_right(a, b):
    return lax.dot_general(a, b, (((1,), (1,)), ((), ())), preferred_element_type=f32)


def batched(a, b):
    return lax.dot_general(a, b, (((2,), (1,)), ((0,), (0,))), preferred_element_type=f32)


def batched_t(a, b):
    return lax.dot_general(a, b, (((1,), (1,)), ((0,), (0,))), preferred_element_type=f32)


def tie(first, *then):
    return lax.optimization_barrier((first, *then))[0] if then else first


def fold_of():
    return 2 if lax.axis_size("seq") == 8 and lax.axis_size("head") == 4 else 1


def lines_of():
    fold = fold_of()
    return [list(range(x, lax.axis_size("seq"), fold)) for x in range(fold)]


def side_of():
    return lax.axis_index("seq") % fold_of()


def swap_pair(v):
    return lax.ppermute(v, "seq", [(i, i ^ 1) for i in range(lax.axis_size("seq"))])


def swap_chip(v):
    return lax.ppermute(v, "head", [(i, i ^ 2) for i in range(4)])


def swap_core(v):
    return lax.ppermute(v, "head", [(i, i ^ 1) for i in range(4)])


def pick(v, at, axis=0):
    half = v.shape[axis] // 2
    return lax.dynamic_slice_in_dim(v, at * half, half, axis)


def join(at, mine, other, axis=0):
    first, second = jnp.where(at == 0, mine, other), jnp.where(at == 0, other, mine)
    return jnp.concatenate([first, second], axis=axis)


def plus(a, b):
    return (a.astype(f32) + b.astype(f32)).astype(bf16)


def place_of():
    core, chip = lax.axis_index("head") % 2, lax.axis_index("head") // 2
    return core, chip, side_of()


def unit_order(count):
    if fold_of() == 1:
        same = [jnp.int32(i) for i in range(count)]
        return same, same, jnp.int32(0)
    core, chip, side = place_of()
    bits = [(i // 4, i // 2 % 2, i % 2) for i in range(8)]
    at_place = [((s ^ side) * 4 + (c ^ core) * 2 + kind).astype(jnp.int32) for c, kind, s in bits]
    of_unit = [((c ^ core) * 4 + kind * 2 + (s ^ side)).astype(jnp.int32) for s, c, kind in bits]
    return at_place, of_unit, chip.astype(jnp.int32)


def chip_sum(away, near):
    if fold_of() == 1:
        return jnp.concatenate([near, away], axis=0).astype(bf16)
    return plus(lax.optimization_barrier(near.astype(bf16)), swap_core(away.astype(bf16)))


def together(*arrays):
    return lax.optimization_barrier(arrays)


def first_exchange(mine):
    if fold_of() == 1:
        return (mine,)
    n = mine.shape[0] // 8
    blocks = [mine[i * n : (i + 1) * n] for i in range(8)]
    keep, give = (jnp.concatenate([blocks[4 + i], blocks[6 + i]], axis=0) for i in range(2))
    by_x, by_y = together(mine[2 * n : 4 * n], give)
    return mine[: 2 * n], keep, swap_pair(by_x), swap_chip(by_y)


def first_total(parts, *beside):
    if fold_of() == 1:
        return parts
    a, b, far_a, far_b = together(*parts, *beside)[:4]
    return together(plus(a, far_a), plus(b, far_b))


def second_exchange(parts):
    if fold_of() == 1:
        return parts
    a, b = parts
    n = a.shape[0] // 2
    return a[:n], b[:n], swap_chip(a[n:]), swap_pair(b[n:])


def second_total(parts, *beside):
    if fold_of() == 1:
        return [lax.psum(parts[0], "head")]
    a, b, far_a, far_b = together(*parts, *beside)[:4]
    return list(together(plus(a, far_a), plus(b, far_b)))


def all_rows(pieces, beside=(), work=None):
    if fold_of() == 1:
        return pieces[0], () if work is None else work(pieces[0])
    a, b = together(*pieces)
    far_a, far_b = together(swap_chip(a), swap_pair(b), *beside)[:2]
    a, b = together(jnp.concatenate([a, far_a], axis=0), jnp.concatenate([b, far_b], axis=0))
    done = () if work is None else work(a)
    far_a, far_b, *done = together(swap_pair(a), swap_chip(b), *done)
    n = far_b.shape[0] // 2
    near = together(a, far_a, b, far_b)
    far = together(*(swap_core(v) for v in near))
    parts = []
    for at in (0, 4):
        parts += [(at, 0, 2 * n), (at + 1, 0, 2 * n)]
        parts += [(at + 2, 0, n), (at + 3, 0, n), (at + 2, n, n), (at + 3, n, n)]
    return assembled(near + far, tuple(parts)), tuple(done)


def chip_rows(pieces):
    if fold_of() == 1:
        return pieces
    a, b = pieces
    both_here = jnp.concatenate([a, b], axis=0)
    return both_here, swap_chip(both_here)


def own_tokens(parts, *beside):
    if fold_of() == 1:
        return parts[0]
    core, chip, _ = place_of()
    here, far = together(*parts, *beside)[:2]
    n = here.shape[0] // 2
    near = jnp.concatenate([join(chip, here[:n], far[:n]), join(chip, here[n:], far[n:])], axis=0)
    return join(core, near, swap_core(near))


def own_blocks(v):
    if fold_of() == 1:
        return [v]
    core, chip, _ = place_of()
    n = v.shape[0] // 8
    return [lax.dynamic_slice_in_dim(v, core * 4 * n + kind * 2 * n + chip * n, n) for kind in range(2)]


def line_total(v):
    fold, step = fold_of(), fold_of()
    while step < lax.axis_size("seq"):
        v = v + lax.ppermute(v, "seq", [(i, i ^ step) for i in range(lax.axis_size("seq"))])
        step *= 2
    return v


def shards_of(v):
    count, step = lax.axis_size("seq"), 1
    held = v[None]
    while step < count:
        held = jnp.concatenate(
            [held, lax.ppermute(held, "seq", [(i, i ^ step) for i in range(count)])], axis=0
        )
        step *= 2
    me = lax.axis_index("seq")
    return jnp.concatenate([lax.dynamic_slice_in_dim(held, me ^ i, 1) for i in range(count)], axis=0)


def pair_rows(v, *after):
    if fold_of() == 1:
        return v
    core = lax.axis_index("head") % 2
    got = tie(swap_pair(pick(v, core)), *after)
    return join(side_of(), v, join(core, got, swap_core(got)))


def my_part(v):
    if fold_of() == 1:
        return v, None
    half = v.shape[0] // 2
    at = side_of()
    return jnp.where(at == 0, v[:half], v[half:]), jnp.where(at == 0, v[half:], v[:half])


def side_parts(masters):
    parts = [my_part(m.astype(bf16)) for m in masters]
    mine = jnp.concatenate([p[0] for p in parts], axis=0)
    if fold_of() == 2:
        away = jnp.concatenate([p[1] for p in parts], axis=0)
        mine = join(side_of(), mine, swap_pair(away), axis=1)
    return mine


def gathered(mine):
    return lax.all_gather(mine, "seq", axis=1, tiled=True, axis_index_groups=lines_of())


def line_scatter(grad, axis=1):
    return lax.psum_scatter(grad, "seq", scatter_dimension=axis, tiled=True, axis_index_groups=lines_of())


def swapped_share(summed, axis=1):
    return swap_pair(pick(summed, 1 - side_of(), axis)) if fold_of() == 2 else None


def in_sides(summed, other, axis=1):
    if fold_of() == 1:
        return [summed.astype(f32)]
    at = side_of()
    mine = pick(summed, at, axis)
    return [jnp.where(at == 0, mine, other).astype(f32), jnp.where(at == 0, other, mine).astype(f32)]


def both(sides, lo, hi):
    return jnp.concatenate([s[lo:hi] for s in sides], axis=0)


def states_in(final):
    fold, count = fold_of(), lax.axis_size("seq")
    onward = [(i, i + fold) for i in range(count - fold)]
    bias, move = final[:, :, :VAL], final[:, :, VAL:].astype(bf16)
    state = jnp.zeros_like(bias).astype(bf16)
    for hop in range(count // fold - 1):
        sent = bias if hop == 0 else batched(move, state) + bias
        state = lax.ppermute(sent.astype(bf16), "seq", onward)
    return state, jnp.swapaxes(move, 1, 2)


def states_back(local, turned, works):
    fold, count = fold_of(), lax.axis_size("seq")
    onward = [(i + fold, i) for i in range(count - fold)]
    sent, carried = local.astype(bf16), ()
    for hop in range(count // fold - 1):
        if hop:
            sent = (batched(turned, state) + local).astype(bf16)
        state = lax.ppermute(sent, "seq", onward)
        if hop < len(works):
            carried = works[hop](sent, carried)
        state, *carried = together(state, *carried)
    return state.astype(f32), carried


def on_device(
    tokens, cotangent, norm1_gain, w_query, w_key, w_value, w_gate_out, w_alpha, w_beta,
    conv_query, conv_key, conv_value, a_log, dt_bias, out_gain, w_out, norm2_gain, w_gate, w_up, w_down,
):
    fold, side = fold_of(), side_of()
    shards = lax.axis_size("seq")
    model = tokens.shape[1]
    share = model // shards
    all_heads = w_alpha.shape[1]
    heads = all_heads // fold
    hidden = w_gate.shape[1] // fold
    keys, vals = heads * KEY, heads * VAL
    width = 2 * keys + vals
    head_at = lax.axis_index("head") * all_heads + side * heads

    proj_parts = side_parts([w_query.T, w_key.T, w_value.T])
    proj_weight = gathered(proj_parts)
    mid_weight = gathered(side_parts([w_gate_out.T, w_out]))
    gate_weight, out_weight = mid_weight[:vals], mid_weight[vals:]
    mlp_in = gathered(side_parts([w_gate.T, w_up.T]))
    mlp_down = gathered(side_parts([w_down]))

    small = [norm1_gain, norm2_gain, w_alpha, w_beta, conv_query, conv_key, conv_value, a_log, dt_bias, out_gain]
    flat = jnp.concatenate([s.astype(bf16).reshape(-1) for s in small])
    flat = shards_of(jnp.pad(flat, (0, -flat.shape[0] % 1024))).astype(f32)
    parts, at = [], 0
    for s in small:
        parts.append(flat[:, at : at + s.size].reshape((shards,) + s.shape))
        at += s.size
    gain_first, gain_second = parts[0].reshape(-1), parts[1].reshape(-1)
    of_side = lambda v, axis: lax.dynamic_slice_in_dim(v, side * heads, heads, axis)
    mix_weight = jnp.concatenate(
        [of_side(parts[2].reshape(model, all_heads), 1), of_side(parts[3].reshape(model, all_heads), 1)], axis=1
    )
    mix_weight = jnp.pad(mix_weight, ((0, 0), (0, 128 - 2 * heads))).astype(bf16)
    taps = jnp.concatenate(
        [of_side(jnp.moveaxis(p, 0, 2).reshape(4, all_heads, -1), 1).reshape(4, -1) for p in parts[4:7]], axis=1
    )
    taps = jnp.pad(taps, ((0, 4), (0, 0)))
    rate = lax.dynamic_slice_in_dim(parts[7].reshape(-1), head_at, heads)
    bias = lax.dynamic_slice_in_dim(parts[8].reshape(-1), head_at, heads)
    gain_out = parts[9].reshape(1, -1)
    par = jnp.pad(jnp.stack([jnp.exp(rate), bias]), ((0, 6), (0, 128 - heads)))

    inputs = pair_rows(tie(tokens, proj_parts)).astype(f32)
    row_count = inputs.shape[0]
    scale_first = lax.rsqrt(jnp.mean(inputs * inputs, axis=1, keepdims=True) + eps_norm)
    normed_first = (inputs * scale_first * gain_first).astype(bf16)
    proj = dot_right(normed_first, proj_weight).astype(bf16)
    mix_pre = dot_rows(normed_first, mix_weight)
    forward = [(i, i + fold) for i in range(shards - fold)]
    backward = [(i + fold, i) for i in range(shards - fold)]
    edge = lax.ppermute(proj[row_count - HALO :], "seq", forward)
    value_out, ident, inverse, states, final = delta_forward(proj, edge, taps, mix_pre, par)
    gate_pre = dot_right(normed_first, gate_weight)
    entering, move = states_in(final)
    order = unit_order(row_count // UNIT)
    places = jnp.stack(order[0] + order[1] + [order[2]])
    both_cot = pair_rows(tie(cotangent, proj), final)
    both_cot, turned_first = reordered(places, both_cot, normed_first)
    mix_turned = mix_weight.T
    side_weight = jnp.concatenate(
        [tie(proj_weight, both_cot), tie(gate_weight, both_cot), tie(mix_turned, both_cot)], axis=0
    )
    entering = tie(entering, both_cot)
    outputs, gated = gated_outputs(places, value_out, ident, entering, gate_pre, gain_out)
    half = row_count // 2
    mine = chip_sum(dot_rows(gated[half:], out_weight), dot_rows(gated[:half], out_weight))
    attention = second_total(second_exchange(first_total(first_exchange(mine), mlp_in)))
    own_inputs = own_blocks(tokens)
    hidden_state = [x.astype(f32) + v.astype(f32) for x, v in zip(own_inputs, attention)]
    scale_second = [lax.rsqrt(jnp.mean(v * v, axis=1, keepdims=True) + eps_norm) for v in hidden_state]
    hat_second = [v * r for v, r in zip(hidden_state, scale_second)]
    normed_second, (mlp_down,) = all_rows(
        [(v * gain_second).astype(bf16) for v in hat_second], (), lambda after: (mlp_down,)
    )
    act = dot_right(mlp_in, normed_second)
    gate_act, up_act = act[:hidden], act[hidden:]
    sig = jax.nn.sigmoid(gate_act)
    mixed = (gate_act * sig * up_act).astype(bf16)
    grad_mixed = dot_right(mlp_down, both_cot)
    grad_act = jnp.concatenate(
        [grad_mixed * up_act * sig * (1.0 + gate_act * (1.0 - sig)), grad_mixed * (gate_act * sig)], axis=0
    ).astype(bf16)
    mine = chip_sum(dot_left(grad_act[:, half:], mlp_in), dot_left(grad_act[:, :half], mlp_in))
    down_grad = dot_rows(tie(mixed, mine), both_cot).astype(bf16)
    in_grad = dot_rows(tie(grad_act, down_grad), normed_second).astype(bf16)
    down_sum = line_scatter(down_grad)
    in_sum = line_scatter(tie(in_grad, down_sum))
    grad_normed_second = first_total(first_exchange(mine), down_grad, in_grad)
    grad_normed_second = second_total(second_exchange(grad_normed_second))
    grad_hidden = []
    for d, v, hat, r in zip(own_blocks(cotangent), grad_normed_second, hat_second, scale_second):
        g = v.astype(f32) * gain_second
        grad_hidden.append(d.astype(f32) + r * (g - hat * jnp.mean(g * hat, axis=1, keepdims=True)))
    attention_rounded = [v.astype(bf16) for v in grad_hidden]
    gain_part = sum(
        jnp.sum(v.astype(f32) * hat, axis=0) for v, hat in zip(grad_normed_second, hat_second)
    )

    if fold == 1:
        gain_part = gain_part / lax.axis_size("head")

    def branch_beside(after):
        m = tie(mixed, after, down_sum)
        return (chip_sum(dot_left(m[:, half:], mlp_down), dot_left(m[:, :half], mlp_down)),)

    attention_rounded, (branch,) = all_rows(attention_rounded, (), branch_beside)
    branch, attention_rounded = together(branch, attention_rounded)
    branch = first_exchange(branch)
    grad_gated = dot_right(attention_rounded, out_weight)
    grad_outputs, grad_gate, grad_gain_out, local_pull = gate_backward(
        places, grad_gated, outputs, gate_pre, gain_out, ident
    )

    line_in = in_sum

    def first_work(sent, carried):
        parts = first_total(branch, sent)
        return dot_left(gated, tie(attention_rounded, parts[0])).astype(bf16), *parts

    def second_work(sent, carried):
        parts = second_exchange(tuple(carried[1:]))
        return carried[0], dot_left(tie(grad_gate, sent), turned_first).astype(bf16), *parts

    def third_work(sent, carried):
        parts = second_total(tuple(carried[2:]))
        rows = [(v + w.astype(f32)).astype(bf16) for v, w in zip(hidden_state, parts)]
        return jnp.concatenate(carried[:2], axis=0), line_in, *rows

    leaving, (mid_grad, in_sum, *result) = states_back(local_pull, move, (first_work, second_work, third_work))
    leaving, mid_grad, down_sum, *result = together(leaving, mid_grad, down_sum, *result)
    result = chip_rows(result)
    in_other, down_other = swapped_share(in_sum), swapped_share(down_sum)
    mid_sum = line_scatter(tie(mid_grad, in_sum))
    grad_side, grad_taps, grad_par, grad_head = delta_backward(
        places, grad_gate, proj, edge, taps, mix_pre, par, grad_outputs, inverse, states, entering, leaving
    )
    following = lax.ppermute(grad_head, "seq", backward)
    fixes = []
    for s in range(3):
        fixes.append(sum(taps[3 - j] * following[s - 3 + j] for j in range(3 - s, 4)))
    at_end = order[1][-1] * UNIT + (1 ^ order[2]) * ROWS + ROWS - HALO
    if fold == 2:
        grad_side, in_other, down_other, *result = together(grad_side, in_other, down_other, *result)
    ending = lax.dynamic_slice(grad_side, (at_end, 0), (HALO, width)).astype(f32)
    ending = (ending + jnp.pad(jnp.stack(fixes), ((HALO - 3, 0), (0, 0)))).astype(bf16)
    grad_side = lax.dynamic_update_slice(grad_side, ending, (at_end, 0))
    proj_grad = dot_left(turned_first, grad_side[:, :width]).astype(bf16)
    last_sum = line_scatter(proj_grad, 0)
    away = dot_rows(tie(grad_side, proj_grad, mid_sum)[half:], side_weight).astype(bf16)
    near = dot_rows(tie(grad_side, away)[:half], side_weight)
    mine = chip_sum(away, near)
    grad_normed_first = first_exchange(mine)
    in_sum, down_sum, mid_sum, grad_taps, grad_par, grad_side, proj_grad = (
        tie(v, mine) for v in (in_sum, down_sum, mid_sum, grad_taps, grad_par, grad_side, proj_grad)
    )
    taps_sum = jnp.sum(grad_taps.reshape(4, 8, width), axis=1)
    par_sum = jnp.sum(grad_par.reshape(2, 8, 128), axis=1)
    every = jnp.zeros((2, shards * a_log.shape[0]), f32)
    every = lax.dynamic_update_slice(every, par_sum[:, :heads], (0, head_at))
    mix_grad = dot_left(grad_side[:, width + vals :], turned_first)
    few = jnp.concatenate([every.reshape(1, -1), jnp.sum(grad_gain_out, axis=0).reshape(1, -1)], axis=1)
    fill = lambda v: jnp.pad(v, ((0, 0), (0, model - v.shape[1])))
    extra = jnp.concatenate([gain_part[None], fill(few), mix_grad[: 2 * heads], fill(taps_sum)], axis=0)
    extra = jnp.pad(extra, ((0, -extra.shape[0] % 8), (0, 0)))
    grad_down, grad_in = in_sides(down_sum, down_other), in_sides(in_sum, in_other)
    ready = (
        both(grad_in, 0, hidden).T, both(grad_in, hidden, 2 * hidden).T, both(grad_down, 0, hidden),
    )
    step = lambda v, by: lax.ppermute(v, "seq", [(i, i ^ by) for i in range(shards)])
    if fold == 2:
        far_a, far_b, extra, *ready = together(*grad_normed_first[2:], extra, *ready)
        grad_normed_first = first_total((*grad_normed_first[:2], far_a, far_b))
        far_extra = step(tie(extra, grad_normed_first[0]), 2)
        own_result = own_tokens([tie(v, grad_normed_first[0]) for v in result])
        grad_normed_first = second_total(second_exchange(grad_normed_first), far_extra, own_result)
        extra = extra + tie(far_extra, grad_normed_first[0])
    else:
        own_result = own_tokens(result)
        grad_normed_first, extra = second_total(grad_normed_first), line_total(extra)
    after = grad_normed_first[0]
    grad_tokens, gain_row = [], 0.0
    for x, d, v in zip(own_inputs, grad_hidden, grad_normed_first):
        x, v = x.astype(f32), v.astype(f32)
        r = lax.rsqrt(jnp.mean(x * x, axis=1, keepdims=True) + eps_norm)
        hat = x * r
        g = v * gain_first
        gain_row = gain_row + jnp.sum(v * hat, axis=0, keepdims=True)
        grad_tokens.append((d + r * (g - hat * jnp.mean(g * hat, axis=1, keepdims=True))).astype(bf16))
    grad_tokens = chip_rows(grad_tokens)
    mid_other = swapped_share(tie(mid_sum, after))
    if fold == 2:
        far_extra, far_row = step(extra, 4), step(gain_row, 2)
        *grad_tokens, far_extra, far_row, last_sum = together(*grad_tokens, far_extra, far_row, last_sum)
        extra, gain_row = extra + far_extra, gain_row + far_row
        last_other, other, far_row = swap_pair(pick(last_sum, 1 - side, 0)), swap_pair(extra), step(gain_row, 4)
        grad_tokens = own_tokens(grad_tokens).astype(f32)
        gain_row = gain_row + far_row
        gain_row = gain_row + swap_pair(gain_row)
        sides = [jnp.where(side == 0, extra, other), jnp.where(side == 0, other, extra)]
        shared = jnp.concatenate([gain_row, extra[:2] + other[:2]], axis=0)
        shared = shared + swap_core(shared)
        shared = shared + swap_chip(shared)
    else:
        last_other, sides = None, [extra]
        grad_tokens = own_tokens(grad_tokens).astype(f32)
        gain_row = line_total(gain_row) / lax.axis_size("head")
        shared = lax.psum(jnp.concatenate([gain_row, extra[:2]], axis=0), "head")
    result = own_result
    me = lax.axis_index("seq")
    take = lambda v, at, n: lax.dynamic_slice_in_dim(v, at, n, v.ndim - 1)
    grad_alpha = jnp.concatenate([take(v[2 : 2 + heads], me * share, share) for v in sides], axis=0).T
    grad_beta = jnp.concatenate([take(v[2 + heads : 2 + 2 * heads], me * share, share) for v in sides], axis=0).T
    filters = []
    for like, lo, size in ((conv_query, 0, KEY), (conv_key, keys, KEY), (conv_value, 2 * keys, VAL)):
        n = like.shape[2]
        filters.append(jnp.stack(
            [take(v[2 + 2 * heads : 6 + 2 * heads], lo + h * size + me * n, n) for v in sides for h in range(heads)],
            axis=1,
        ))
    n_rate, n_gain = a_log.shape[0], out_gain.shape[0]
    few = shared[2]
    grad_mid, grad_last = in_sides(mid_sum, mid_other), in_sides(last_sum, last_other, 0)
    channels = lambda lo, hi: jnp.concatenate([v[:, lo:hi] for v in grad_last], axis=1)

    return (
        result,
        grad_tokens,
        take(shared[0], me * share, share),
        channels(0, keys),
        channels(keys, 2 * keys),
        channels(2 * keys, width),
        both(grad_mid, vals, 2 * vals).T,
        grad_alpha,
        grad_beta,
        filters[0],
        filters[1],
        filters[2],
        take(few, me * n_rate, n_rate),
        take(few, (shards + me) * n_rate, n_rate),
        take(few, 2 * shards * n_rate + me * n_gain, n_gain),
        both(grad_mid, 0, vals),
        take(shared[1], me * share, share),
        *ready,
    )


def solution(mesh):
    P = jax.sharding.PartitionSpec
    rows, vector, filters, turned = P("seq", None), P("seq"), P(None, "head", "seq"), P("head", "seq")
    matrix = P("seq", "head")
    placed = (rows, rows, vector) + (matrix,) * 6 + (filters,) * 3 + (vector,) * 3 + (
        turned, vector, matrix, matrix, turned)
    return jax.shard_map(
        on_device, mesh=mesh, in_specs=placed, out_specs=placed, check_vma=False
    )
```

```python
import functools
import jax
import jax.numpy as jnp
from jax import lax
from jax.experimental import pallas as pl
from jax.experimental.pallas import tpu as pltpu

ROWS = 128
KEY = 128
VAL = 256
HALO = 16
eps_norm = 1e-06
f32 = jnp.float32
bf16 = jnp.bfloat16


def mm(a, b):
    return lax.dot_general(
        a.astype(bf16), b.astype(bf16), (((1,), (0,)), ((), ())), preferred_element_type=f32
    )


def mm_nt(a, b):
    return lax.dot_general(
        a.astype(bf16), b.astype(bf16), (((1,), (1,)), ((), ())), preferred_element_type=f32
    )


def mm_tn(a, b):
    return lax.dot_general(
        a.astype(bf16), b.astype(bf16), (((0,), (0,)), ((), ())), preferred_element_type=f32
    )


def mm_full(a, b):
    return lax.dot_general(
        a, b, (((1,), (0,)), ((), ())), precision=lax.Precision.HIGHEST, preferred_element_type=f32
    )


def sigmoid(x):
    return 1.0 / (1.0 + jnp.exp(-x))


def softplus(x):
    return jnp.maximum(x, 0.0) + jnp.log(1.0 + jnp.exp(-jnp.abs(x)))


def positions():
    rows = lax.broadcasted_iota(jnp.int32, (ROWS, ROWS), 0)
    cols = lax.broadcasted_iota(jnp.int32, (ROWS, ROWS), 1)
    return rows, cols


def decay_terms(heads, ab, par):
    rows, cols = positions()
    log_decay = -par[0:1, :] * softplus(ab + par[1:2, :])
    running = mm_full((rows >= cols).astype(f32), log_decay)
    return log_decay, running, running.T, sigmoid(ab)


def ratio_of(running, running_rows, h, rows, cols):
    gap = running[:, h : h + 1] - running_rows[h : h + 1, :]
    return jnp.where(rows >= cols, jnp.exp(jnp.where(rows >= cols, gap, 0.0)), 0.0)


def conv_at(xs_ref, taps_ref, base, lo, width):
    total = taps_ref[0:1, lo : lo + width] * xs_ref[base - 3 : base - 3 + ROWS, lo : lo + width]
    for i in range(1, 4):
        total = total + taps_ref[i : i + 1, lo : lo + width] * (
            xs_ref[base - 3 + i : base - 3 + i + ROWS, lo : lo + width]
        )
    return total


def forward_kernel(heads, proj_ref, edge_ref, taps_ref, ab_ref, par_ref,
                   value_ref, ident_ref, inv_ref, state_ref, final_ref, xs_ref, s_ref):
    step = pl.program_id(0)
    keys = heads * KEY

    @pl.when(step == 0)
    def _():
        xs_ref[0:HALO, :] = edge_ref[...].astype(f32)
        r, c = positions()
        for h in range(heads):
            s_ref[h, :, 0:VAL] = jnp.zeros((KEY, VAL), f32)
            s_ref[h, :, VAL:] = (r == c).astype(f32)

    span = proj_ref.shape[0]
    subs = range(span // ROWS)

    @pl.when(step > 0)
    def _():
        xs_ref[0:HALO, :] = xs_ref[span : span + HALO, :]

    xs_ref[HALO : HALO + span, :] = proj_ref[...].astype(f32)
    rows, cols = positions()
    every = [(s, h) for s in subs for h in range(heads)]
    running, running_rows, strength = [], [], []
    for s in subs:
        terms = decay_terms(heads, ab_ref[s * ROWS : (s + 1) * ROWS, :], par_ref[...])
        running.append(terms[1])
        running_rows.append(terms[2])
        strength.append(terms[3])
    q, k, v, a, p, t, beta, grow = {}, {}, {}, {}, {}, {}, {}, {}
    for s, h in every:
        base = HALO + s * ROWS
        u = conv_at(xs_ref, taps_ref, base, h * KEY, KEY)
        u = u * sigmoid(u)
        q[s, h] = u * (lax.rsqrt(jnp.sum(u * u, axis=1, keepdims=True) + eps_norm) * KEY**-0.5)
        w = conv_at(xs_ref, taps_ref, base, keys + h * KEY, KEY)
        w = w * sigmoid(w)
        k[s, h] = w * lax.rsqrt(jnp.sum(w * w, axis=1, keepdims=True) + eps_norm)
        x = conv_at(xs_ref, taps_ref, base, 2 * keys + h * VAL, VAL)
        v[s, h] = x * sigmoid(x)
        beta[s, h] = strength[s][:, heads + h : heads + h + 1]
        grow[s, h] = jnp.exp(running[s][:, h : h + 1])
    for s, h in every:
        ratio = ratio_of(running[s], running_rows[s], h, rows, cols)
        gram = mm_nt(k[s, h], k[s, h])
        a[s, h] = jnp.where(rows > cols, ratio * gram, 0.0) * beta[s, h]
        p[s, h] = ratio * mm_nt(q[s, h], k[s, h])
    first = (rows // 2 == cols // 2) & (rows > cols)
    for e in every:
        t[e] = (rows == cols).astype(f32) - jnp.where(first, a[e], 0.0)
    b = 2
    while b < ROWS:
        low = (rows // (2 * b) == cols // (2 * b)) & ((rows // b) % 2 == 1) & ((cols // b) % 2 == 0)
        inner = {e: mm(jnp.where(low, a[e], 0.0), t[e]) for e in every}
        t = {e: t[e] - mm(t[e], inner[e]) for e in every}
        b *= 2
    uw = {
        e: mm(t[e], jnp.concatenate([beta[e] * v[e], (beta[e] * grow[e]) * k[e]], axis=1))
        for e in every
    }
    for s, h in every:
        inv_ref[s * ROWS : (s + 1) * ROWS, h * KEY : (h + 1) * KEY] = t[s, h].astype(bf16)
    for s, h in every:
        at = slice(s * ROWS, (s + 1) * ROWS)
        state = s_ref[h]
        state_ref[s, h] = state.astype(bf16)
        pred = mm(uw[s, h][:, VAL:], state)
        err = jnp.concatenate([uw[s, h][:, :VAL] - pred[:, :VAL], -pred[:, VAL:]], axis=1)
        out = grow[s, h] * mm(q[s, h], state) + mm(p[s, h], err)
        value_ref[at, h * VAL : (h + 1) * VAL] = out[:, :VAL]
        ident_ref[at, h * KEY : (h + 1) * KEY] = out[:, VAL:].astype(bf16)
        end = running[s][ROWS - 1 : ROWS, h : h + 1]
        tail = jnp.exp(end - running[s][:, h : h + 1]) * k[s, h]
        s_ref[h] = jnp.exp(end) * state + mm_tn(tail, err)

    @pl.when(step == pl.num_programs(0) - 1)
    def _():
        final_ref[...] = s_ref[...]


def sub_blocks(heads):
    return 2


def delta_forward(proj, edge, taps, ab, par):
    tokens = proj.shape[0]
    heads = proj.shape[1] // (2 * KEY + VAL)
    keys, vals = heads * KEY, heads * VAL
    subs = sub_blocks(heads)
    span = subs * ROWS
    blocks = tokens // span
    width = proj.shape[1]
    whole = lambda *shape: pl.BlockSpec(shape, lambda c: (0,) * len(shape))
    return pl.pallas_call(
        functools.partial(forward_kernel, heads),
        grid=(blocks,),
        in_specs=[
            pl.BlockSpec((span, width), lambda c: (c, 0)),
            whole(HALO, width),
            whole(8, width),
            pl.BlockSpec((span, 128), lambda c: (c, 0)),
            whole(8, 128),
        ],
        out_specs=[
            pl.BlockSpec((span, vals), lambda c: (c, 0)),
            pl.BlockSpec((span, keys), lambda c: (c, 0)),
            pl.BlockSpec((span, keys), lambda c: (c, 0)),
            pl.BlockSpec((subs, heads, KEY, VAL + KEY), lambda c: (c, 0, 0, 0)),
            whole(heads, KEY, VAL + KEY),
        ],
        out_shape=[
            jax.ShapeDtypeStruct((tokens, vals), f32),
            jax.ShapeDtypeStruct((tokens, keys), bf16),
            jax.ShapeDtypeStruct((tokens, keys), bf16),
            jax.ShapeDtypeStruct((blocks * subs, heads, KEY, VAL + KEY), bf16),
            jax.ShapeDtypeStruct((heads, KEY, VAL + KEY), f32),
        ],
        scratch_shapes=[
            pltpu.VMEM((HALO + span, width), f32),
            pltpu.VMEM((heads, KEY, VAL + KEY), f32),
        ],
        compiler_params=pltpu.CompilerParams(
            dimension_semantics=("arbitrary",), vmem_limit_bytes=48 * 2**20
        ),
    )(proj, edge, taps, ab, par)


UNIT = 2 * ROWS


def placed_rows(order_ref, sub):
    flip = order_ref[order_ref.shape[0] - 1]
    return pl.ds(pl.multiple_of((flip + sub - 2 * flip * sub) * ROWS, ROWS), ROWS)


def reorder_kernel(order_ref, *refs):
    count = len(refs) // 2
    for in_ref, out_ref in zip(refs[:count], refs[count:]):
        for sub in range(2):
            out_ref[placed_rows(order_ref, sub), :] = in_ref[sub * ROWS : (sub + 1) * ROWS, :]


def reordered(order, *arrays):
    tokens = arrays[0].shape[0]
    return pl.pallas_call(
        reorder_kernel,
        grid_spec=pltpu.PrefetchScalarGridSpec(
            num_scalar_prefetch=1,
            grid=(tokens // UNIT,),
            in_specs=[pl.BlockSpec((UNIT, a.shape[1]), lambda c, order: (order[c], 0)) for a in arrays],
            out_specs=[pl.BlockSpec((UNIT, a.shape[1]), lambda c, order: (c, 0)) for a in arrays],
        ),
        out_shape=[jax.ShapeDtypeStruct(a.shape, a.dtype) for a in arrays],
        compiler_params=pltpu.CompilerParams(
            dimension_semantics=("arbitrary",), vmem_limit_bytes=32 * 2**20
        ),
    )(order, *arrays)


def output_kernel(heads, order_ref, value_ref, ident_ref, state_ref, gate_ref, gain_ref, out_ref, gated_ref):
    for h in range(heads):
        span = slice(h * VAL, (h + 1) * VAL)
        out = value_ref[:, span] + mm(ident_ref[:, h * KEY : (h + 1) * KEY], state_ref[h])
        out_ref[:, span] = out
        gate = gate_ref[:, span]
        unit = out * lax.rsqrt(jnp.mean(out * out, axis=1, keepdims=True) + eps_norm)
        gated = (unit * gain_ref[0:1, :] * (gate * sigmoid(gate))).astype(bf16)
        for sub in range(2):
            gated_ref[placed_rows(order_ref, sub), span] = gated[sub * ROWS : (sub + 1) * ROWS]


def gated_outputs(order, value_out, ident, state_in, gate_pre, gain):
    tokens, vals = value_out.shape
    heads = vals // VAL
    placed = lambda width: pl.BlockSpec((UNIT, width), lambda c, order: (order[c], 0))
    return pl.pallas_call(
        functools.partial(output_kernel, heads),
        grid_spec=pltpu.PrefetchScalarGridSpec(
            num_scalar_prefetch=1,
            grid=(tokens // UNIT,),
            in_specs=[
                placed(vals),
                placed(heads * KEY),
                pl.BlockSpec((heads, KEY, VAL), lambda c, order: (0, 0, 0)),
                placed(vals),
                pl.BlockSpec((1, VAL), lambda c, order: (0, 0)),
            ],
            out_specs=[placed(vals), pl.BlockSpec((UNIT, vals), lambda c, order: (c, 0))],
        ),
        out_shape=[
            jax.ShapeDtypeStruct((tokens, vals), f32),
            jax.ShapeDtypeStruct((tokens, vals), bf16),
        ],
        compiler_params=pltpu.CompilerParams(
            dimension_semantics=("arbitrary",), vmem_limit_bytes=48 * 2**20
        ),
    )(order, value_out, ident, state_in, gate_pre, gain)


def gate_back_kernel(heads, order_ref, grad_ref, out_ref, gate_ref, gain_ref, ident_ref,
                     dout_ref, dgate_ref, dgain_ref, pull_ref):
    @pl.when(pl.program_id(0) == 0)
    def _():
        dgain_ref[...] = jnp.zeros_like(dgain_ref)
        pull_ref[...] = jnp.zeros_like(pull_ref)

    gain = gain_ref[0:1, :]
    for h in range(heads):
        span = slice(h * VAL, (h + 1) * VAL)
        grad = jnp.concatenate([grad_ref[placed_rows(order_ref, sub), span] for sub in range(2)], axis=0)
        out, gate = out_ref[:, span], gate_ref[:, span]
        scale = lax.rsqrt(jnp.mean(out * out, axis=1, keepdims=True) + eps_norm)
        unit = out * scale
        sig = sigmoid(gate)
        m = grad * (gate * sig)
        mn = m * unit
        dgain_ref[...] += jnp.sum(mn.reshape(-1, 8, VAL), axis=0)
        mean = jnp.mean(mn * gain, axis=1, keepdims=True)
        dout = (scale * (m * gain - unit * mean)).astype(bf16)
        dout_ref[:, span] = dout
        dgate = (grad * unit * gain * (sig * (1.0 + gate * (1.0 - sig)))).astype(bf16)
        for sub in range(2):
            dgate_ref[placed_rows(order_ref, sub), span] = dgate[sub * ROWS : (sub + 1) * ROWS]
        pull_ref[h] += mm_tn(ident_ref[:, h * KEY : (h + 1) * KEY], dout)


def gate_backward(order, grad_gated, outputs, gate_pre, gain, ident):
    tokens, vals = outputs.shape
    heads = vals // VAL
    placed = lambda width: pl.BlockSpec((UNIT, width), lambda c, order: (order[c], 0))
    return pl.pallas_call(
        functools.partial(gate_back_kernel, heads),
        grid_spec=pltpu.PrefetchScalarGridSpec(
            num_scalar_prefetch=1,
            grid=(tokens // UNIT,),
            in_specs=[
                pl.BlockSpec((UNIT, vals), lambda c, order: (c, 0)),
                placed(vals),
                placed(vals),
                pl.BlockSpec((1, VAL), lambda c, order: (0, 0)),
                placed(heads * KEY),
            ],
            out_specs=[
                placed(vals),
                pl.BlockSpec((UNIT, vals), lambda c, order: (c, 0)),
                pl.BlockSpec((8, VAL), lambda c, order: (0, 0)),
                pl.BlockSpec((heads, KEY, VAL), lambda c, order: (0, 0, 0)),
            ],
        ),
        out_shape=[
            jax.ShapeDtypeStruct((tokens, vals), bf16),
            jax.ShapeDtypeStruct((tokens, vals), bf16),
            jax.ShapeDtypeStruct((8, VAL), f32),
            jax.ShapeDtypeStruct((heads, KEY, VAL), f32),
        ],
        compiler_params=pltpu.CompilerParams(
            dimension_semantics=("arbitrary",), vmem_limit_bytes=48 * 2**20
        ),
    )(order, grad_gated, outputs, gate_pre, gain, ident)


def backward_kernel(heads, order_ref, gate_ref, proj_ref, before_ref, edge_ref, taps_ref, ab_ref, par_ref, dout_ref,
                    inv_ref, state_ref, enter_ref, dfinal_ref,
                    dproj_ref, dtaps_ref, dpar_ref, dhead_ref,
                    xs_ref, gs_ref, ds_ref):
    step = pl.program_id(0)
    last = pl.num_programs(0) - 1
    keys = heads * KEY
    width = 2 * keys + heads * VAL
    span = proj_ref.shape[0]

    @pl.when(step == 0)
    def _():
        ds_ref[...] = dfinal_ref[...]
        dtaps_ref[...] = jnp.zeros_like(dtaps_ref)
        dpar_ref[...] = jnp.zeros_like(dpar_ref)
        gs_ref[span : span + 8, :] = jnp.zeros((8, width), f32)

    @pl.when(step > 0)
    def _():
        gs_ref[span : span + 8, :] = gs_ref[0:8, :]

    @pl.when(step == last)
    def _():
        xs_ref[0:HALO, :] = edge_ref[...].astype(f32)

    @pl.when(step < last)
    def _():
        xs_ref[0:HALO, :] = before_ref[...].astype(f32)

    xs_ref[HALO : HALO + span, :] = proj_ref[...].astype(f32)
    rows, cols = positions()
    par = par_ref[...]
    lane = lax.broadcasted_iota(jnp.int32, (ROWS, 128), 1)
    row_at = lax.broadcasted_iota(jnp.int32, (ROWS, 1), 0)
    terms, found = {}, {}
    for s in range(span // ROWS):
        terms[s] = decay_terms(heads, ab_ref[s * ROWS : (s + 1) * ROWS, :], par)

    def tokens_of(s, h):
        at = slice(s * ROWS, (s + 1) * ROWS)
        log_decay, running, running_rows, strength = terms[s]
        qs, ks, vs = h * KEY, keys + h * KEY, 2 * keys + h * VAL
        u = conv_at(xs_ref, taps_ref, HALO + s * ROWS, qs, KEY)
        su = sigmoid(u)
        wu = u * su
        ru = lax.rsqrt(jnp.sum(wu * wu, axis=1, keepdims=True) + eps_norm)
        q = wu * (ru * KEY**-0.5)
        y = conv_at(xs_ref, taps_ref, HALO + s * ROWS, ks, KEY)
        sy = sigmoid(y)
        wy = y * sy
        ry = lax.rsqrt(jnp.sum(wy * wy, axis=1, keepdims=True) + eps_norm)
        k = wy * ry
        x = conv_at(xs_ref, taps_ref, HALO + s * ROWS, vs, VAL)
        sx = sigmoid(x)
        v = x * sx
        yield
        qb, kb = q.astype(bf16), k.astype(bf16)
        beta = strength[:, heads + h : heads + h + 1]
        passed = running[:, h : h + 1]
        grow = jnp.exp(passed)
        end = running[ROWS - 1 : ROWS, h : h + 1]
        tail = jnp.exp(end - passed)
        ratio = ratio_of(running, running_rows, h, rows, cols)
        p = ratio * mm_nt(qb, kb)
        t = inv_ref[at, h * KEY : (h + 1) * KEY]
        dout = dout_ref[at, h * VAL : (h + 1) * VAL]
        state = state_ref[s, h, :, :VAL].astype(f32) + mm(state_ref[s, h, :, VAL:], enter_ref[h])
        state_b = state.astype(bf16)
        yield
        held = mm(kb, state_b)
        yield
        err = mm(t, beta * (v - grow * held))
        err_b = err.astype(bf16)
        yield
        dp = mm_nt(dout, err_b) * ratio
        dp_b = dp.astype(bf16)
        from_out = mm_tn(p, dout)
        dq = grow * mm_nt(dout, state_b) + mm(dp_b, kb)
        yield
        dstate = ds_ref[h]
        dstate_b = dstate.astype(bf16)
        derr = from_out + mm(tail * k, dstate_b)
        yield
        dright = mm_tn(t, derr)
        yield
        dright_b = dright.astype(bf16)
        da = jnp.where(rows > cols, mm_nt(dright_b, err_b) * ratio, 0.0) * (-beta)
        da_b = da.astype(bf16)
        back = (beta * grow) * dright
        back_b = back.astype(bf16)
        ds_ref[h] = jnp.exp(end) * dstate + mm_tn(grow * q, dout) - mm_tn(kb, back_b)
        yield
        dk_read = mm(da_b, kb) - mm_nt(back_b, state_b)
        dk_tail = tail * mm_nt(err_b, dstate_b)
        dk_write = mm_tn(dp_b, qb) + mm_tn(da_b, kb) + dk_tail
        dk = dk_read + dk_write
        dv = beta * dright
        to_beta = (1.0 - beta) * jnp.sum(dright * err, axis=1, keepdims=True)
        to_decay = jnp.sum(q * dq + k * (dk_read - dk_write), axis=1, keepdims=True)
        at_end = jnp.exp(end) * jnp.sum(
            jnp.sum(state * dstate, axis=1, keepdims=True), axis=0, keepdims=True
        ) + jnp.sum(jnp.sum(k * dk_tail, axis=1, keepdims=True), axis=0, keepdims=True)
        to_decay = to_decay + jnp.where(row_at == ROWS - 1, at_end, 0.0)
        found[s, h] = (to_decay, to_beta)
        yield
        along = jnp.sum(wu * dq, axis=1, keepdims=True)
        du = (KEY**-0.5) * (ru * dq - wu * (ru * ru * ru * along))
        gs_ref[at, qs : qs + KEY] = du * (su * (1.0 + u * (1.0 - su)))
        along = jnp.sum(wy * dk, axis=1, keepdims=True)
        dy = ry * dk - wy * (ry * ry * ry * along)
        gs_ref[at, ks : ks + KEY] = dy * (sy * (1.0 + y * (1.0 - sy)))
        gs_ref[at, vs : vs + VAL] = dv * (sx * (1.0 + x * (1.0 - sx)))

    def in_step(steps, count=None):
        while steps and count != 0:
            steps = [one for one in steps if next(one, steps) is not steps]
            count = None if count is None else count - 1
        return steps

    every = [tokens_of(s, h) for s in reversed(range(span // ROWS)) for h in range(heads)]
    every = in_step(every, 5)
    started = {s: every[i * heads : (i + 1) * heads] for i, s in enumerate(reversed(range(span // ROWS)))}
    for s in reversed(range(span // ROWS)):
        at = slice(s * ROWS, (s + 1) * ROWS)
        ab, log_decay = ab_ref[at, :], terms[s][0]
        drunning = jnp.zeros((ROWS, 128), f32)
        dbeta = jnp.zeros((ROWS, 128), f32)
        in_step(started[s])
        for h in range(heads):
            drunning = jnp.where(lane == h, found[s, h][0], drunning)
            dbeta = jnp.where(lane == heads + h, found[s, h][1], dbeta)
        dlog = mm_full((rows <= cols).astype(f32), drunning)
        dalpha = -dlog * par[0:1, :] * sigmoid(ab + par[1:2, :])
        dproj_ref[placed_rows(order_ref, s), width + heads * VAL :] = jnp.where(lane < heads, dalpha, dbeta).astype(bf16)
        dpar_ref[0:8, :] += jnp.sum((dlog * log_decay).reshape(-1, 8, 128), axis=0)
        dpar_ref[8:16, :] += jnp.sum(dalpha.reshape(-1, 8, 128), axis=0)

    for lo in range(0, width, 256):
        lanes = slice(lo, lo + 256)
        here = xs_ref[HALO : HALO + span, lanes]
        total = jnp.zeros((span, 256), f32)
        for i in range(4):
            grad = gs_ref[3 - i : 3 - i + span, lanes]
            dtaps_ref[8 * i : 8 * i + 8, lanes] += jnp.sum((here * grad).reshape(-1, 8, 256), axis=0)
            total = total + taps_ref[i : i + 1, lanes] * grad
        total = total.astype(bf16)
        for s in range(2):
            dproj_ref[placed_rows(order_ref, s), lanes] = total[s * ROWS : (s + 1) * ROWS]

    @pl.when(step == last)
    def _():
        head_row = lax.broadcasted_iota(jnp.int32, (8, width), 0)
        for i in range(3):
            moved = gs_ref[0:8, :] * xs_ref[HALO - 3 + i : HALO + 5 + i, :]
            dtaps_ref[8 * i : 8 * i + 8, :] += jnp.where(head_row < 3 - i, moved, 0.0)

    dproj_ref[:, width : width + heads * VAL] = gate_ref[...]

    @pl.when(step == last)
    def _():
        dhead_ref[...] = gs_ref[0:8, :]


def delta_backward(order, dgate, proj, edge, taps, ab, par, dout, inverse, states, entering, dfinal):
    tokens, width = proj.shape
    heads = width // (2 * KEY + VAL)
    keys, vals = heads * KEY, heads * VAL
    subs = sub_blocks(heads)
    span = subs * ROWS
    blocks = tokens // span
    whole = lambda *shape: pl.BlockSpec(shape, lambda c, order: (0,) * len(shape))
    rev = lambda w: pl.BlockSpec((span, w), lambda c, order: (blocks - 1 - c, 0))
    sent = lambda w: pl.BlockSpec((span, w), lambda c, order: (order[blocks + blocks - 1 - c], 0))
    per = span // HALO
    return pl.pallas_call(
        functools.partial(backward_kernel, heads),
        grid_spec=pltpu.PrefetchScalarGridSpec(
            num_scalar_prefetch=1,
            grid=(blocks,),
            in_specs=[
                sent(vals),
                rev(width),
                pl.BlockSpec((HALO, width), lambda c, order: (jnp.maximum((blocks - 1 - c) * per - 1, 0), 0)),
                whole(HALO, width),
                whole(8, width),
                rev(128),
                whole(8, 128),
                rev(vals),
                rev(keys),
                pl.BlockSpec((subs, heads, KEY, VAL + KEY), lambda c, order: (blocks - 1 - c, 0, 0, 0)),
                whole(heads, KEY, VAL),
                whole(heads, KEY, VAL),
            ],
            out_specs=[
                sent(width + vals + 128),
                whole(32, width),
                whole(16, 128),
                whole(8, width),
            ],
            scratch_shapes=[
                pltpu.VMEM((HALO + span, width), f32),
                pltpu.VMEM((span + 8, width), f32),
                pltpu.VMEM((heads, KEY, VAL), f32),
            ],
        ),
        out_shape=[
            jax.ShapeDtypeStruct((tokens, width + vals + 128), bf16),
            jax.ShapeDtypeStruct((32, width), f32),
            jax.ShapeDtypeStruct((16, 128), f32),
            jax.ShapeDtypeStruct((8, width), f32),
        ],
        compiler_params=pltpu.CompilerParams(
            dimension_semantics=("arbitrary",), vmem_limit_bytes=56 * 2**20
        ),
    )(order, dgate, proj, proj, edge, taps, ab, par, dout, inverse, states, entering, dfinal)


def assemble_kernel(parts, *refs):
    out_ref, sems = refs[-2], refs[-1]
    copies, at = [], 0
    for i, (which, start, rows) in enumerate(parts):
        copies.append(pltpu.make_async_copy(
            refs[which].at[pl.ds(start, rows)], out_ref.at[pl.ds(at, rows)], sems.at[i]))
        at += rows
    for copy in copies:
        copy.start()
    for copy in copies:
        copy.wait()


def assembled(pieces, parts):
    rows = sum(p[2] for p in parts)
    return pl.pallas_call(
        functools.partial(assemble_kernel, parts),
        in_specs=[pl.BlockSpec(memory_space=pltpu.VMEM)] * len(pieces),
        out_specs=pl.BlockSpec(memory_space=pl.ANY),
        out_shape=jax.ShapeDtypeStruct((rows,) + pieces[0].shape[1:], pieces[0].dtype),
        scratch_shapes=[pltpu.SemaphoreType.DMA((len(parts),))],
        compiler_params=pltpu.CompilerParams(vmem_limit_bytes=32 * 2**20),
    )(*pieces)


def dot_rows(a, b):
    return lax.dot_general(a, b, (((1,), (0,)), ((), ())), preferred_element_type=f32)


def dot_left(a, b):
    return lax.dot_general(a, b, (((0,), (0,)), ((), ())), preferred_element_type=f32)


def dot_right(a, b):
    return lax.dot_general(a, b, (((1,), (1,)), ((), ())), preferred_element_type=f32)


def batched(a, b):
    return lax.dot_general(a, b, (((2,), (1,)), ((0,), (0,))), preferred_element_type=f32)


def batched_t(a, b):
    return lax.dot_general(a, b, (((1,), (1,)), ((0,), (0,))), preferred_element_type=f32)


def tie(first, *then):
    return lax.optimization_barrier((first, *then))[0] if then else first


def fold_of():
    return 2 if lax.axis_size("seq") == 8 and lax.axis_size("head") == 4 else 1


def lines_of():
    fold = fold_of()
    return [list(range(x, lax.axis_size("seq"), fold)) for x in range(fold)]


def side_of():
    return lax.axis_index("seq") % fold_of()


def swap_pair(v):
    return lax.ppermute(v, "seq", [(i, i ^ 1) for i in range(lax.axis_size("seq"))])


def swap_chip(v):
    return lax.ppermute(v, "head", [(i, i ^ 2) for i in range(4)])


def swap_core(v):
    return lax.ppermute(v, "head", [(i, i ^ 1) for i in range(4)])


def pick(v, at, axis=0):
    half = v.shape[axis] // 2
    return lax.dynamic_slice_in_dim(v, at * half, half, axis)


def join(at, mine, other, axis=0):
    first, second = jnp.where(at == 0, mine, other), jnp.where(at == 0, other, mine)
    return jnp.concatenate([first, second], axis=axis)


def plus(a, b):
    return (a.astype(f32) + b.astype(f32)).astype(bf16)


def place_of():
    core, chip = lax.axis_index("head") % 2, lax.axis_index("head") // 2
    return core, chip, side_of()


def unit_order(count):
    if fold_of() == 1:
        same = [jnp.int32(i) for i in range(count)]
        return same, same, jnp.int32(0)
    core, chip, side = place_of()
    bits = [(i // 4, i // 2 % 2, i % 2) for i in range(8)]
    at_place = [((s ^ side) * 4 + (c ^ core) * 2 + kind).astype(jnp.int32) for c, kind, s in bits]
    of_unit = [((c ^ core) * 4 + kind * 2 + (s ^ side)).astype(jnp.int32) for s, c, kind in bits]
    return at_place, of_unit, chip.astype(jnp.int32)


def chip_sum(away, near):
    if fold_of() == 1:
        return jnp.concatenate([near, away], axis=0).astype(bf16)
    return plus(lax.optimization_barrier(near.astype(bf16)), swap_core(away.astype(bf16)))


def together(*arrays):
    return lax.optimization_barrier(arrays)


def first_exchange(mine):
    if fold_of() == 1:
        return (mine,)
    n = mine.shape[0] // 8
    blocks = [mine[i * n : (i + 1) * n] for i in range(8)]
    keep, give = (jnp.concatenate([blocks[4 + i], blocks[6 + i]], axis=0) for i in range(2))
    by_x, by_y = together(mine[2 * n : 4 * n], give)
    return mine[: 2 * n], keep, swap_pair(by_x), swap_chip(by_y)


def first_total(parts, *beside):
    if fold_of() == 1:
        return parts
    a, b, far_a, far_b = together(*parts, *beside)[:4]
    return together(plus(a, far_a), plus(b, far_b))


def second_exchange(parts):
    if fold_of() == 1:
        return parts
    a, b = parts
    n = a.shape[0] // 2
    return a[:n], b[:n], swap_chip(a[n:]), swap_pair(b[n:])


def second_total(parts, *beside):
    if fold_of() == 1:
        return [lax.psum(parts[0], "head")]
    a, b, far_a, far_b = together(*parts, *beside)[:4]
    return list(together(plus(a, far_a), plus(b, far_b)))


def all_rows(pieces, beside=(), work=None):
    if fold_of() == 1:
        return pieces[0], () if work is None else work(pieces[0])
    a, b = together(*pieces)
    far_a, far_b = together(swap_chip(a), swap_pair(b), *beside)[:2]
    a, b = together(jnp.concatenate([a, far_a], axis=0), jnp.concatenate([b, far_b], axis=0))
    done = () if work is None else work(a)
    far_a, far_b, *done = together(swap_pair(a), swap_chip(b), *done)
    n = far_b.shape[0] // 2
    near = together(a, far_a, b, far_b)
    far = together(*(swap_core(v) for v in near))
    parts = []
    for at in (0, 4):
        parts += [(at, 0, 2 * n), (at + 1, 0, 2 * n)]
        parts += [(at + 2, 0, n), (at + 3, 0, n), (at + 2, n, n), (at + 3, n, n)]
    return assembled(near + far, tuple(parts)), tuple(done)


def chip_rows(pieces):
    if fold_of() == 1:
        return pieces
    a, b = pieces
    both_here = jnp.concatenate([a, b], axis=0)
    return both_here, swap_chip(both_here)


def own_tokens(parts, *beside):
    if fold_of() == 1:
        return parts[0]
    core, chip, _ = place_of()
    here, far = together(*parts, *beside)[:2]
    n = here.shape[0] // 2
    near = jnp.concatenate([join(chip, here[:n], far[:n]), join(chip, here[n:], far[n:])], axis=0)
    return join(core, near, swap_core(near))


def own_blocks(v):
    if fold_of() == 1:
        return [v]
    core, chip, _ = place_of()
    n = v.shape[0] // 8
    return [lax.dynamic_slice_in_dim(v, core * 4 * n + kind * 2 * n + chip * n, n) for kind in range(2)]


def line_total(v):
    fold, step = fold_of(), fold_of()
    while step < lax.axis_size("seq"):
        v = v + lax.ppermute(v, "seq", [(i, i ^ step) for i in range(lax.axis_size("seq"))])
        step *= 2
    return v


def shards_of(v):
    count, step = lax.axis_size("seq"), 1
    held = v[None]
    while step < count:
        held = jnp.concatenate(
            [held, lax.ppermute(held, "seq", [(i, i ^ step) for i in range(count)])], axis=0
        )
        step *= 2
    me = lax.axis_index("seq")
    return jnp.concatenate([lax.dynamic_slice_in_dim(held, me ^ i, 1) for i in range(count)], axis=0)


def pair_rows(v, *after):
    if fold_of() == 1:
        return v
    core = lax.axis_index("head") % 2
    got = tie(swap_pair(pick(v, core)), *after)
    return join(side_of(), v, join(core, got, swap_core(got)))


def my_part(v):
    if fold_of() == 1:
        return v, None
    half = v.shape[0] // 2
    at = side_of()
    return jnp.where(at == 0, v[:half], v[half:]), jnp.where(at == 0, v[half:], v[:half])


def side_parts(masters):
    parts = [my_part(m.astype(bf16)) for m in masters]
    mine = jnp.concatenate([p[0] for p in parts], axis=0)
    if fold_of() == 2:
        away = jnp.concatenate([p[1] for p in parts], axis=0)
        mine = join(side_of(), mine, swap_pair(away), axis=1)
    return mine


def gathered(mine):
    return lax.all_gather(mine, "seq", axis=1, tiled=True, axis_index_groups=lines_of())


def line_scatter(grad, axis=1):
    return lax.psum_scatter(grad, "seq", scatter_dimension=axis, tiled=True, axis_index_groups=lines_of())


def swapped_share(summed, axis=1):
    return swap_pair(pick(summed, 1 - side_of(), axis)) if fold_of() == 2 else None


def in_sides(summed, other, axis=1):
    if fold_of() == 1:
        return [summed.astype(f32)]
    at = side_of()
    mine = pick(summed, at, axis)
    return [jnp.where(at == 0, mine, other).astype(f32), jnp.where(at == 0, other, mine).astype(f32)]


def both(sides, lo, hi):
    return jnp.concatenate([s[lo:hi] for s in sides], axis=0)


def states_in(final):
    fold, count = fold_of(), lax.axis_size("seq")
    onward = [(i, i + fold) for i in range(count - fold)]
    bias, move = final[:, :, :VAL], final[:, :, VAL:].astype(bf16)
    state = jnp.zeros_like(bias).astype(bf16)
    for hop in range(count // fold - 1):
        sent = bias if hop == 0 else batched(move, state) + bias
        state = lax.ppermute(sent.astype(bf16), "seq", onward)
    return state, jnp.swapaxes(move, 1, 2)


def states_back(local, turned, works):
    fold, count = fold_of(), lax.axis_size("seq")
    onward = [(i + fold, i) for i in range(count - fold)]
    sent, carried = local.astype(bf16), ()
    for hop in range(count // fold - 1):
        if hop:
            sent = (batched(turned, state) + local).astype(bf16)
        state = lax.ppermute(sent, "seq", onward)
        if hop < len(works):
            carried = works[hop](sent, carried)
        state, *carried = together(state, *carried)
    return state.astype(f32), carried


def on_device(
    tokens, cotangent, norm1_gain, w_query, w_key, w_value, w_gate_out, w_alpha, w_beta,
    conv_query, conv_key, conv_value, a_log, dt_bias, out_gain, w_out, norm2_gain, w_gate, w_up, w_down,
):
    fold, side = fold_of(), side_of()
    shards = lax.axis_size("seq")
    model = tokens.shape[1]
    share = model // shards
    all_heads = w_alpha.shape[1]
    heads = all_heads // fold
    hidden = w_gate.shape[1] // fold
    keys, vals = heads * KEY, heads * VAL
    width = 2 * keys + vals
    head_at = lax.axis_index("head") * all_heads + side * heads

    proj_parts = side_parts([w_query.T, w_key.T, w_value.T])
    proj_weight = gathered(proj_parts)
    mid_weight = gathered(side_parts([w_gate_out.T, w_out]))
    gate_weight, out_weight = mid_weight[:vals], mid_weight[vals:]
    mlp_in = gathered(side_parts([w_gate.T, w_up.T]))
    mlp_down = gathered(side_parts([w_down]))

    small = [norm1_gain, norm2_gain, w_alpha, w_beta, conv_query, conv_key, conv_value, a_log, dt_bias, out_gain]
    flat = jnp.concatenate([s.astype(bf16).reshape(-1) for s in small])
    flat = shards_of(jnp.pad(flat, (0, -flat.shape[0] % 1024))).astype(f32)
    parts, at = [], 0
    for s in small:
        parts.append(flat[:, at : at + s.size].reshape((shards,) + s.shape))
        at += s.size
    gain_first, gain_second = parts[0].reshape(-1), parts[1].reshape(-1)
    of_side = lambda v, axis: lax.dynamic_slice_in_dim(v, side * heads, heads, axis)
    mix_weight = jnp.concatenate(
        [of_side(parts[2].reshape(model, all_heads), 1), of_side(parts[3].reshape(model, all_heads), 1)], axis=1
    )
    mix_weight = jnp.pad(mix_weight, ((0, 0), (0, 128 - 2 * heads))).astype(bf16)
    taps = jnp.concatenate(
        [of_side(jnp.moveaxis(p, 0, 2).reshape(4, all_heads, -1), 1).reshape(4, -1) for p in parts[4:7]], axis=1
    )
    taps = jnp.pad(taps, ((0, 4), (0, 0)))
    rate = lax.dynamic_slice_in_dim(parts[7].reshape(-1), head_at, heads)
    bias = lax.dynamic_slice_in_dim(parts[8].reshape(-1), head_at, heads)
    gain_out = parts[9].reshape(1, -1)
    par = jnp.pad(jnp.stack([jnp.exp(rate), bias]), ((0, 6), (0, 128 - heads)))

    inputs = pair_rows(tie(tokens, proj_parts)).astype(f32)
    row_count = inputs.shape[0]
    scale_first = lax.rsqrt(jnp.mean(inputs * inputs, axis=1, keepdims=True) + eps_norm)
    normed_first = (inputs * scale_first * gain_first).astype(bf16)
    proj = dot_right(normed_first, proj_weight).astype(bf16)
    mix_pre = dot_rows(normed_first, mix_weight)
    forward = [(i, i + fold) for i in range(shards - fold)]
    backward = [(i + fold, i) for i in range(shards - fold)]
    edge = lax.ppermute(proj[row_count - HALO :], "seq", forward)
    value_out, ident, inverse, states, final = delta_forward(proj, edge, taps, mix_pre, par)
    gate_pre = dot_right(normed_first, gate_weight)
    entering, move = states_in(final)
    order = unit_order(row_count // UNIT)
    places = jnp.stack(order[0] + order[1] + [order[2]])
    both_cot = pair_rows(tie(cotangent, proj), final)
    both_cot, turned_first = reordered(places, both_cot, normed_first)
    mix_turned = mix_weight.T
    side_weight = jnp.concatenate(
        [tie(proj_weight, both_cot), tie(gate_weight, both_cot), tie(mix_turned, both_cot)], axis=0
    )
    entering = tie(entering, both_cot)
    outputs, gated = gated_outputs(places, value_out, ident, entering, gate_pre, gain_out)
    half = row_count // 2
    mine = chip_sum(dot_rows(gated[half:], out_weight), dot_rows(gated[:half], out_weight))
    attention = second_total(second_exchange(first_total(first_exchange(mine), mlp_in)))
    own_inputs = own_blocks(tokens)
    hidden_state = [x.astype(f32) + v.astype(f32) for x, v in zip(own_inputs, attention)]
    scale_second = [lax.rsqrt(jnp.mean(v * v, axis=1, keepdims=True) + eps_norm) for v in hidden_state]
    hat_second = [v * r for v, r in zip(hidden_state, scale_second)]
    normed_second, (mlp_down,) = all_rows(
        [(v * gain_second).astype(bf16) for v in hat_second], (), lambda after: (mlp_down,)
    )
    act = dot_right(mlp_in, normed_second)
    gate_act, up_act = act[:hidden], act[hidden:]
    sig = jax.nn.sigmoid(gate_act)
    mixed = (gate_act * sig * up_act).astype(bf16)
    grad_mixed = dot_right(mlp_down, both_cot)
    grad_act = jnp.concatenate(
        [grad_mixed * up_act * sig * (1.0 + gate_act * (1.0 - sig)), grad_mixed * (gate_act * sig)], axis=0
    ).astype(bf16)
    mine = chip_sum(dot_left(grad_act[:, half:], mlp_in), dot_left(grad_act[:, :half], mlp_in))
    down_grad = dot_rows(tie(mixed, mine), both_cot).astype(bf16)
    in_grad = dot_rows(tie(grad_act, down_grad), normed_second).astype(bf16)
    down_sum = line_scatter(down_grad)
    in_sum = line_scatter(tie(in_grad, down_sum))
    grad_normed_second = first_total(first_exchange(mine), down_grad, in_grad)
    grad_normed_second = second_total(second_exchange(grad_normed_second))
    grad_hidden = []
    for d, v, hat, r in zip(own_blocks(cotangent), grad_normed_second, hat_second, scale_second):
        g = v.astype(f32) * gain_second
        grad_hidden.append(d.astype(f32) + r * (g - hat * jnp.mean(g * hat, axis=1, keepdims=True)))
    attention_rounded = [v.astype(bf16) for v in grad_hidden]
    gain_part = sum(
        jnp.sum(v.astype(f32) * hat, axis=0) for v, hat in zip(grad_normed_second, hat_second)
    )

    if fold == 1:
        gain_part = gain_part / lax.axis_size("head")

    def branch_beside(after):
        m = tie(mixed, after, down_sum)
        return (chip_sum(dot_left(m[:, half:], mlp_down), dot_left(m[:, :half], mlp_down)),)

    attention_rounded, (branch,) = all_rows(attention_rounded, (), branch_beside)
    branch, attention_rounded = together(branch, attention_rounded)
    branch = first_exchange(branch)
    grad_gated = dot_right(attention_rounded, out_weight)
    grad_outputs, grad_gate, grad_gain_out, local_pull = gate_backward(
        places, grad_gated, outputs, gate_pre, gain_out, ident
    )

    line_in = in_sum

    def first_work(sent, carried):
        parts = first_total(branch, sent)
        return dot_left(gated, tie(attention_rounded, parts[0])).astype(bf16), *parts

    def second_work(sent, carried):
        parts = second_exchange(tuple(carried[1:]))
        return carried[0], dot_left(tie(grad_gate, sent), turned_first).astype(bf16), *parts

    def third_work(sent, carried):
        parts = second_total(tuple(carried[2:]))
        rows = [(v + w.astype(f32)).astype(bf16) for v, w in zip(hidden_state, parts)]
        return jnp.concatenate(carried[:2], axis=0), line_in, *rows

    leaving, (mid_grad, in_sum, *result) = states_back(local_pull, move, (first_work, second_work, third_work))
    leaving, mid_grad, down_sum, *result = together(leaving, mid_grad, down_sum, *result)
    result = chip_rows(result)
    in_other, down_other = swapped_share(in_sum), swapped_share(down_sum)
    mid_sum = line_scatter(tie(mid_grad, in_sum))
    grad_side, grad_taps, grad_par, grad_head = delta_backward(
        places, grad_gate, proj, edge, taps, mix_pre, par, grad_outputs, inverse, states, entering, leaving
    )
    following = lax.ppermute(grad_head, "seq", backward)
    fixes = []
    for s in range(3):
        fixes.append(sum(taps[3 - j] * following[s - 3 + j] for j in range(3 - s, 4)))
    at_end = order[1][-1] * UNIT + (1 ^ order[2]) * ROWS + ROWS - HALO
    if fold == 2:
        grad_side, in_other, down_other, *result = together(grad_side, in_other, down_other, *result)
    ending = lax.dynamic_slice(grad_side, (at_end, 0), (HALO, width)).astype(f32)
    ending = (ending + jnp.pad(jnp.stack(fixes), ((HALO - 3, 0), (0, 0)))).astype(bf16)
    grad_side = lax.dynamic_update_slice(grad_side, ending, (at_end, 0))
    proj_grad = dot_left(turned_first, grad_side[:, :width]).astype(bf16)
    last_sum = line_scatter(proj_grad, 0)
    away = dot_rows(tie(grad_side, proj_grad, mid_sum)[half:], side_weight).astype(bf16)
    near = dot_rows(tie(grad_side, away)[:half], side_weight)
    mine = chip_sum(away, near)
    grad_normed_first = first_exchange(mine)
    in_sum, down_sum, mid_sum, grad_taps, grad_par, grad_side, proj_grad = (
        tie(v, mine) for v in (in_sum, down_sum, mid_sum, grad_taps, grad_par, grad_side, proj_grad)
    )
    taps_sum = jnp.sum(grad_taps.reshape(4, 8, width), axis=1)
    par_sum = jnp.sum(grad_par.reshape(2, 8, 128), axis=1)
    every = jnp.zeros((2, shards * a_log.shape[0]), f32)
    every = lax.dynamic_update_slice(every, par_sum[:, :heads], (0, head_at))
    mix_grad = dot_left(grad_side[:, width + vals :], turned_first)
    few = jnp.concatenate([every.reshape(1, -1), jnp.sum(grad_gain_out, axis=0).reshape(1, -1)], axis=1)
    fill = lambda v: jnp.pad(v, ((0, 0), (0, model - v.shape[1])))
    extra = jnp.concatenate([gain_part[None], fill(few), mix_grad[: 2 * heads], fill(taps_sum)], axis=0)
    extra = jnp.pad(extra, ((0, -extra.shape[0] % 8), (0, 0)))
    grad_down, grad_in = in_sides(down_sum, down_other), in_sides(in_sum, in_other)
    ready = (
        both(grad_in, 0, hidden).T, both(grad_in, hidden, 2 * hidden).T, both(grad_down, 0, hidden),
    )
    step = lambda v, by: lax.ppermute(v, "seq", [(i, i ^ by) for i in range(shards)])
    if fold == 2:
        far_a, far_b, extra, *ready = together(*grad_normed_first[2:], extra, *ready)
        grad_normed_first = first_total((*grad_normed_first[:2], far_a, far_b))
        far_extra = step(tie(extra, grad_normed_first[0]), 2)
        own_result = own_tokens([tie(v, grad_normed_first[0]) for v in result])
        grad_normed_first = second_total(second_exchange(grad_normed_first), far_extra, own_result)
        extra = extra + tie(far_extra, grad_normed_first[0])
    else:
        own_result = own_tokens(result)
        grad_normed_first, extra = second_total(grad_normed_first), line_total(extra)
    after = grad_normed_first[0]
    grad_tokens, gain_row = [], 0.0
    for x, d, v in zip(own_inputs, grad_hidden, grad_normed_first):
        x, v = x.astype(f32), v.astype(f32)
        r = lax.rsqrt(jnp.mean(x * x, axis=1, keepdims=True) + eps_norm)
        hat = x * r
        g = v * gain_first
        gain_row = gain_row + jnp.sum(v * hat, axis=0, keepdims=True)
        grad_tokens.append((d + r * (g - hat * jnp.mean(g * hat, axis=1, keepdims=True))).astype(bf16))
    grad_tokens = chip_rows(grad_tokens)
    mid_other = swapped_share(tie(mid_sum, after))
    if fold == 2:
        far_extra, far_row = step(extra, 4), step(gain_row, 2)
        *grad_tokens, far_extra, far_row, last_sum = together(*grad_tokens, far_extra, far_row, last_sum)
        extra, gain_row = extra + far_extra, gain_row + far_row
        last_other, other, far_row = swap_pair(pick(last_sum, 1 - side, 0)), swap_pair(extra), step(gain_row, 4)
        grad_tokens = own_tokens(grad_tokens).astype(f32)
        gain_row = gain_row + far_row
        gain_row = gain_row + swap_pair(gain_row)
        sides = [jnp.where(side == 0, extra, other), jnp.where(side == 0, other, extra)]
        shared = jnp.concatenate([gain_row, extra[:2] + other[:2]], axis=0)
        shared = shared + swap_core(shared)
        shared = shared + swap_chip(shared)
    else:
        last_other, sides = None, [extra]
        grad_tokens = own_tokens(grad_tokens).astype(f32)
        gain_row = line_total(gain_row) / lax.axis_size("head")
        shared = lax.psum(jnp.concatenate([gain_row, extra[:2]], axis=0), "head")
    result = own_result
    me = lax.axis_index("seq")
    take = lambda v, at, n: lax.dynamic_slice_in_dim(v, at, n, v.ndim - 1)
    grad_alpha = jnp.concatenate([take(v[2 : 2 + heads], me * share, share) for v in sides], axis=0).T
    grad_beta = jnp.concatenate([take(v[2 + heads : 2 + 2 * heads], me * share, share) for v in sides], axis=0).T
    filters = []
    for like, lo, size in ((conv_query, 0, KEY), (conv_key, keys, KEY), (conv_value, 2 * keys, VAL)):
        n = like.shape[2]
        filters.append(jnp.stack(
            [take(v[2 + 2 * heads : 6 + 2 * heads], lo + h * size + me * n, n) for v in sides for h in range(heads)],
            axis=1,
        ))
    n_rate, n_gain = a_log.shape[0], out_gain.shape[0]
    few = shared[2]
    grad_mid, grad_last = in_sides(mid_sum, mid_other), in_sides(last_sum, last_other, 0)
    channels = lambda lo, hi: jnp.concatenate([v[:, lo:hi] for v in grad_last], axis=1)

    return (
        result,
        grad_tokens,
        take(shared[0], me * share, share),
        channels(0, keys),
        channels(keys, 2 * keys),
        channels(2 * keys, width),
        both(grad_mid, vals, 2 * vals).T,
        grad_alpha,
        grad_beta,
        filters[0],
        filters[1],
        filters[2],
        take(few, me * n_rate, n_rate),
        take(few, (shards + me) * n_rate, n_rate),
        take(few, 2 * shards * n_rate + me * n_gain, n_gain),
        both(grad_mid, 0, vals),
        take(shared[1], me * share, share),
        *ready,
    )


def solution(mesh):
    P = jax.sharding.PartitionSpec
    rows, vector, filters, turned = P("seq", None), P("seq"), P(None, "head", "seq"), P("head", "seq")
    matrix = P("seq", "head")
    placed = (rows, rows, vector) + (matrix,) * 6 + (filters,) * 3 + (vector,) * 3 + (
        turned, vector, matrix, matrix, turned)
    return jax.shard_map(
        on_device, mesh=mesh, in_specs=placed, out_specs=placed, check_vma=False
    )
```

```python
import functools
import jax
import jax.numpy as jnp
from jax import lax
from jax.experimental import pallas as pl
from jax.experimental.pallas import tpu as pltpu

ROWS = 128
KEY = 128
VAL = 256
HALO = 16
eps_norm = 1e-06
f32 = jnp.float32
bf16 = jnp.bfloat16


def mm(a, b):
    return lax.dot_general(
        a.astype(bf16), b.astype(bf16), (((1,), (0,)), ((), ())), preferred_element_type=f32
    )


def mm_nt(a, b):
    return lax.dot_general(
        a.astype(bf16), b.astype(bf16), (((1,), (1,)), ((), ())), preferred_element_type=f32
    )


def mm_tn(a, b):
    return lax.dot_general(
        a.astype(bf16), b.astype(bf16), (((0,), (0,)), ((), ())), preferred_element_type=f32
    )


def mm_full(a, b):
    return lax.dot_general(
        a, b, (((1,), (0,)), ((), ())), precision=lax.Precision.HIGHEST, preferred_element_type=f32
    )


def sigmoid(x):
    return 1.0 / (1.0 + jnp.exp(-x))


def softplus(x):
    return jnp.maximum(x, 0.0) + jnp.log(1.0 + jnp.exp(-jnp.abs(x)))


def positions():
    rows = lax.broadcasted_iota(jnp.int32, (ROWS, ROWS), 0)
    cols = lax.broadcasted_iota(jnp.int32, (ROWS, ROWS), 1)
    return rows, cols


def decay_terms(heads, ab, par):
    rows, cols = positions()
    log_decay = -par[0:1, :] * softplus(ab + par[1:2, :])
    running = mm_full((rows >= cols).astype(f32), log_decay)
    return log_decay, running, running.T, sigmoid(ab)


def ratio_of(running, running_rows, h, rows, cols):
    gap = running[:, h : h + 1] - running_rows[h : h + 1, :]
    return jnp.where(rows >= cols, jnp.exp(jnp.where(rows >= cols, gap, 0.0)), 0.0)


def conv_at(xs_ref, taps_ref, base, lo, width):
    total = taps_ref[0:1, lo : lo + width] * xs_ref[base - 3 : base - 3 + ROWS, lo : lo + width]
    for i in range(1, 4):
        total = total + taps_ref[i : i + 1, lo : lo + width] * (
            xs_ref[base - 3 + i : base - 3 + i + ROWS, lo : lo + width]
        )
    return total


def forward_kernel(heads, proj_ref, edge_ref, taps_ref, ab_ref, par_ref,
                   value_ref, ident_ref, inv_ref, state_ref, final_ref, xs_ref, s_ref):
    step = pl.program_id(0)
    keys = heads * KEY

    @pl.when(step == 0)
    def _():
        xs_ref[0:HALO, :] = edge_ref[...].astype(f32)
        r, c = positions()
        for h in range(heads):
            s_ref[h, :, 0:VAL] = jnp.zeros((KEY, VAL), f32)
            s_ref[h, :, VAL:] = (r == c).astype(f32)

    span = proj_ref.shape[0]
    subs = range(span // ROWS)

    @pl.when(step > 0)
    def _():
        xs_ref[0:HALO, :] = xs_ref[span : span + HALO, :]

    xs_ref[HALO : HALO + span, :] = proj_ref[...].astype(f32)
    rows, cols = positions()
    every = [(s, h) for s in subs for h in range(heads)]
    running, running_rows, strength = [], [], []
    for s in subs:
        terms = decay_terms(heads, ab_ref[s * ROWS : (s + 1) * ROWS, :], par_ref[...])
        running.append(terms[1])
        running_rows.append(terms[2])
        strength.append(terms[3])
    q, k, v, a, p, t, beta, grow = {}, {}, {}, {}, {}, {}, {}, {}
    for s, h in every:
        base = HALO + s * ROWS
        u = conv_at(xs_ref, taps_ref, base, h * KEY, KEY)
        u = u * sigmoid(u)
        q[s, h] = u * (lax.rsqrt(jnp.sum(u * u, axis=1, keepdims=True) + eps_norm) * KEY**-0.5)
        w = conv_at(xs_ref, taps_ref, base, keys + h * KEY, KEY)
        w = w * sigmoid(w)
        k[s, h] = w * lax.rsqrt(jnp.sum(w * w, axis=1, keepdims=True) + eps_norm)
        x = conv_at(xs_ref, taps_ref, base, 2 * keys + h * VAL, VAL)
        v[s, h] = x * sigmoid(x)
        beta[s, h] = strength[s][:, heads + h : heads + h + 1]
        grow[s, h] = jnp.exp(running[s][:, h : h + 1])
    for s, h in every:
        ratio = ratio_of(running[s], running_rows[s], h, rows, cols)
        gram = mm_nt(k[s, h], k[s, h])
        a[s, h] = jnp.where(rows > cols, ratio * gram, 0.0) * beta[s, h]
        p[s, h] = ratio * mm_nt(q[s, h], k[s, h])
    first = (rows // 2 == cols // 2) & (rows > cols)
    for e in every:
        t[e] = (rows == cols).astype(f32) - jnp.where(first, a[e], 0.0)
    b = 2
    while b < ROWS:
        low = (rows // (2 * b) == cols // (2 * b)) & ((rows // b) % 2 == 1) & ((cols // b) % 2 == 0)
        inner = {e: mm(jnp.where(low, a[e], 0.0), t[e]) for e in every}
        t = {e: t[e] - mm(t[e], inner[e]) for e in every}
        b *= 2
    uw = {
        e: mm(t[e], jnp.concatenate([beta[e] * v[e], (beta[e] * grow[e]) * k[e]], axis=1))
        for e in every
    }
    for s, h in every:
        inv_ref[s * ROWS : (s + 1) * ROWS, h * KEY : (h + 1) * KEY] = t[s, h].astype(bf16)
    for s, h in every:
        at = slice(s * ROWS, (s + 1) * ROWS)
        state = s_ref[h]
        state_ref[s, h] = state.astype(bf16)
        pred = mm(uw[s, h][:, VAL:], state)
        err = jnp.concatenate([uw[s, h][:, :VAL] - pred[:, :VAL], -pred[:, VAL:]], axis=1)
        out = grow[s, h] * mm(q[s, h], state) + mm(p[s, h], err)
        value_ref[at, h * VAL : (h + 1) * VAL] = out[:, :VAL]
        ident_ref[at, h * KEY : (h + 1) * KEY] = out[:, VAL:].astype(bf16)
        end = running[s][ROWS - 1 : ROWS, h : h + 1]
        tail = jnp.exp(end - running[s][:, h : h + 1]) * k[s, h]
        s_ref[h] = jnp.exp(end) * state + mm_tn(tail, err)

    @pl.when(step == pl.num_programs(0) - 1)
    def _():
        final_ref[...] = s_ref[...]


def sub_blocks(heads):
    return 2


def delta_forward(proj, edge, taps, ab, par):
    tokens = proj.shape[0]
    heads = proj.shape[1] // (2 * KEY + VAL)
    keys, vals = heads * KEY, heads * VAL
    subs = sub_blocks(heads)
    span = subs * ROWS
    blocks = tokens // span
    width = proj.shape[1]
    whole = lambda *shape: pl.BlockSpec(shape, lambda c: (0,) * len(shape))
    return pl.pallas_call(
        functools.partial(forward_kernel, heads),
        grid=(blocks,),
        in_specs=[
            pl.BlockSpec((span, width), lambda c: (c, 0)),
            whole(HALO, width),
            whole(8, width),
            pl.BlockSpec((span, 128), lambda c: (c, 0)),
            whole(8, 128),
        ],
        out_specs=[
            pl.BlockSpec((span, vals), lambda c: (c, 0)),
            pl.BlockSpec((span, keys), lambda c: (c, 0)),
            pl.BlockSpec((span, keys), lambda c: (c, 0)),
            pl.BlockSpec((subs, heads, KEY, VAL + KEY), lambda c: (c, 0, 0, 0)),
            whole(heads, KEY, VAL + KEY),
        ],
        out_shape=[
            jax.ShapeDtypeStruct((tokens, vals), f32),
            jax.ShapeDtypeStruct((tokens, keys), bf16),
            jax.ShapeDtypeStruct((tokens, keys), bf16),
            jax.ShapeDtypeStruct((blocks * subs, heads, KEY, VAL + KEY), bf16),
            jax.ShapeDtypeStruct((heads, KEY, VAL + KEY), f32),
        ],
        scratch_shapes=[
            pltpu.VMEM((HALO + span, width), f32),
            pltpu.VMEM((heads, KEY, VAL + KEY), f32),
        ],
        compiler_params=pltpu.CompilerParams(
            dimension_semantics=("arbitrary",), vmem_limit_bytes=48 * 2**20
        ),
    )(proj, edge, taps, ab, par)


UNIT = 2 * ROWS


def placed_rows(order_ref, sub):
    flip = order_ref[order_ref.shape[0] - 1]
    return pl.ds(pl.multiple_of((flip + sub - 2 * flip * sub) * ROWS, ROWS), ROWS)


def reorder_kernel(order_ref, *refs):
    count = len(refs) // 2
    for in_ref, out_ref in zip(refs[:count], refs[count:]):
        for sub in range(2):
            out_ref[placed_rows(order_ref, sub), :] = in_ref[sub * ROWS : (sub + 1) * ROWS, :]


def reordered(order, *arrays):
    tokens = arrays[0].shape[0]
    return pl.pallas_call(
        reorder_kernel,
        grid_spec=pltpu.PrefetchScalarGridSpec(
            num_scalar_prefetch=1,
            grid=(tokens // UNIT,),
            in_specs=[pl.BlockSpec((UNIT, a.shape[1]), lambda c, order: (order[c], 0)) for a in arrays],
            out_specs=[pl.BlockSpec((UNIT, a.shape[1]), lambda c, order: (c, 0)) for a in arrays],
        ),
        out_shape=[jax.ShapeDtypeStruct(a.shape, a.dtype) for a in arrays],
        compiler_params=pltpu.CompilerParams(
            dimension_semantics=("arbitrary",), vmem_limit_bytes=32 * 2**20
        ),
    )(order, *arrays)


def output_kernel(heads, order_ref, value_ref, ident_ref, state_ref, gate_ref, gain_ref, out_ref, gated_ref):
    for h in range(heads):
        span = slice(h * VAL, (h + 1) * VAL)
        out = value_ref[:, span] + mm(ident_ref[:, h * KEY : (h + 1) * KEY], state_ref[h])
        out_ref[:, span] = out
        gate = gate_ref[:, span]
        unit = out * lax.rsqrt(jnp.mean(out * out, axis=1, keepdims=True) + eps_norm)
        gated = (unit * gain_ref[0:1, :] * (gate * sigmoid(gate))).astype(bf16)
        for sub in range(2):
            gated_ref[placed_rows(order_ref, sub), span] = gated[sub * ROWS : (sub + 1) * ROWS]


def gated_outputs(order, value_out, ident, state_in, gate_pre, gain):
    tokens, vals = value_out.shape
    heads = vals // VAL
    placed = lambda width: pl.BlockSpec((UNIT, width), lambda c, order: (order[c], 0))
    return pl.pallas_call(
        functools.partial(output_kernel, heads),
        grid_spec=pltpu.PrefetchScalarGridSpec(
            num_scalar_prefetch=1,
            grid=(tokens // UNIT,),
            in_specs=[
                placed(vals),
                placed(heads * KEY),
                pl.BlockSpec((heads, KEY, VAL), lambda c, order: (0, 0, 0)),
                placed(vals),
                pl.BlockSpec((1, VAL), lambda c, order: (0, 0)),
            ],
            out_specs=[placed(vals), pl.BlockSpec((UNIT, vals), lambda c, order: (c, 0))],
        ),
        out_shape=[
            jax.ShapeDtypeStruct((tokens, vals), f32),
            jax.ShapeDtypeStruct((tokens, vals), bf16),
        ],
        compiler_params=pltpu.CompilerParams(
            dimension_semantics=("arbitrary",), vmem_limit_bytes=48 * 2**20
        ),
    )(order, value_out, ident, state_in, gate_pre, gain)


def gate_back_kernel(heads, order_ref, grad_ref, out_ref, gate_ref, gain_ref, ident_ref,
                     dout_ref, dgate_ref, dgain_ref, pull_ref):
    @pl.when(pl.program_id(0) == 0)
    def _():
        dgain_ref[...] = jnp.zeros_like(dgain_ref)
        pull_ref[...] = jnp.zeros_like(pull_ref)

    gain = gain_ref[0:1, :]
    for h in range(heads):
        span = slice(h * VAL, (h + 1) * VAL)
        grad = jnp.concatenate([grad_ref[placed_rows(order_ref, sub), span] for sub in range(2)], axis=0).astype(f32)
        out, gate = out_ref[:, span], gate_ref[:, span]
        scale = lax.rsqrt(jnp.mean(out * out, axis=1, keepdims=True) + eps_norm)
        unit = out * scale
        sig = sigmoid(gate)
        m = grad * (gate * sig)
        mn = m * unit
        dgain_ref[...] += jnp.sum(mn.reshape(-1, 8, VAL), axis=0)
        mean = jnp.mean(mn * gain, axis=1, keepdims=True)
        dout = (scale * (m * gain - unit * mean)).astype(bf16)
        dout_ref[:, span] = dout
        dgate = (grad * unit * gain * (sig * (1.0 + gate * (1.0 - sig)))).astype(bf16)
        for sub in range(2):
            dgate_ref[placed_rows(order_ref, sub), span] = dgate[sub * ROWS : (sub + 1) * ROWS]
        pull_ref[h] += mm_tn(ident_ref[:, h * KEY : (h + 1) * KEY], dout)


def gate_backward(order, grad_gated, outputs, gate_pre, gain, ident):
    tokens, vals = outputs.shape
    heads = vals // VAL
    placed = lambda width: pl.BlockSpec((UNIT, width), lambda c, order: (order[c], 0))
    return pl.pallas_call(
        functools.partial(gate_back_kernel, heads),
        grid_spec=pltpu.PrefetchScalarGridSpec(
            num_scalar_prefetch=1,
            grid=(tokens // UNIT,),
            in_specs=[
                pl.BlockSpec((UNIT, vals), lambda c, order: (c, 0)),
                placed(vals),
                placed(vals),
                pl.BlockSpec((1, VAL), lambda c, order: (0, 0)),
                placed(heads * KEY),
            ],
            out_specs=[
                placed(vals),
                pl.BlockSpec((UNIT, vals), lambda c, order: (c, 0)),
                pl.BlockSpec((8, VAL), lambda c, order: (0, 0)),
                pl.BlockSpec((heads, KEY, VAL), lambda c, order: (0, 0, 0)),
            ],
        ),
        out_shape=[
            jax.ShapeDtypeStruct((tokens, vals), bf16),
            jax.ShapeDtypeStruct((tokens, vals), bf16),
            jax.ShapeDtypeStruct((8, VAL), f32),
            jax.ShapeDtypeStruct((heads, KEY, VAL), f32),
        ],
        compiler_params=pltpu.CompilerParams(
            dimension_semantics=("arbitrary",), vmem_limit_bytes=48 * 2**20
        ),
    )(order, grad_gated, outputs, gate_pre, gain, ident)


def backward_kernel(heads, order_ref, gate_ref, proj_ref, before_ref, edge_ref, taps_ref, ab_ref, par_ref, dout_ref,
                    inv_ref, state_ref, enter_ref, dfinal_ref,
                    dproj_ref, dtaps_ref, dpar_ref, dhead_ref,
                    xs_ref, gs_ref, ds_ref):
    step = pl.program_id(0)
    last = pl.num_programs(0) - 1
    keys = heads * KEY
    width = 2 * keys + heads * VAL
    span = proj_ref.shape[0]

    @pl.when(step == 0)
    def _():
        ds_ref[...] = dfinal_ref[...]
        dtaps_ref[...] = jnp.zeros_like(dtaps_ref)
        dpar_ref[...] = jnp.zeros_like(dpar_ref)
        gs_ref[span : span + 8, :] = jnp.zeros((8, width), f32)

    @pl.when(step > 0)
    def _():
        gs_ref[span : span + 8, :] = gs_ref[0:8, :]

    @pl.when(step == last)
    def _():
        xs_ref[0:HALO, :] = edge_ref[...].astype(f32)

    @pl.when(step < last)
    def _():
        xs_ref[0:HALO, :] = before_ref[...].astype(f32)

    xs_ref[HALO : HALO + span, :] = proj_ref[...].astype(f32)
    rows, cols = positions()
    par = par_ref[...]
    lane = lax.broadcasted_iota(jnp.int32, (ROWS, 128), 1)
    row_at = lax.broadcasted_iota(jnp.int32, (ROWS, 1), 0)
    terms, found = {}, {}
    for s in range(span // ROWS):
        terms[s] = decay_terms(heads, ab_ref[s * ROWS : (s + 1) * ROWS, :], par)

    def tokens_of(s, h):
        at = slice(s * ROWS, (s + 1) * ROWS)
        log_decay, running, running_rows, strength = terms[s]
        qs, ks, vs = h * KEY, keys + h * KEY, 2 * keys + h * VAL
        u = conv_at(xs_ref, taps_ref, HALO + s * ROWS, qs, KEY)
        su = sigmoid(u)
        wu = u * su
        ru = lax.rsqrt(jnp.sum(wu * wu, axis=1, keepdims=True) + eps_norm)
        q = wu * (ru * KEY**-0.5)
        y = conv_at(xs_ref, taps_ref, HALO + s * ROWS, ks, KEY)
        sy = sigmoid(y)
        wy = y * sy
        ry = lax.rsqrt(jnp.sum(wy * wy, axis=1, keepdims=True) + eps_norm)
        k = wy * ry
        x = conv_at(xs_ref, taps_ref, HALO + s * ROWS, vs, VAL)
        sx = sigmoid(x)
        v = x * sx
        yield
        qb, kb = q.astype(bf16), k.astype(bf16)
        beta = strength[:, heads + h : heads + h + 1]
        passed = running[:, h : h + 1]
        grow = jnp.exp(passed)
        end = running[ROWS - 1 : ROWS, h : h + 1]
        tail = jnp.exp(end - passed)
        ratio = ratio_of(running, running_rows, h, rows, cols)
        p = ratio * mm_nt(qb, kb)
        t = inv_ref[at, h * KEY : (h + 1) * KEY]
        dout = dout_ref[at, h * VAL : (h + 1) * VAL]
        state = state_ref[s, h, :, :VAL].astype(f32) + mm(state_ref[s, h, :, VAL:], enter_ref[h])
        state_b = state.astype(bf16)
        yield
        held = mm(kb, state_b)
        yield
        err = mm(t, beta * (v - grow * held))
        err_b = err.astype(bf16)
        yield
        dp = mm_nt(dout, err_b) * ratio
        dp_b = dp.astype(bf16)
        from_out = mm_tn(p, dout)
        dq = grow * mm_nt(dout, state_b) + mm(dp_b, kb)
        yield
        dstate = ds_ref[h]
        dstate_b = dstate.astype(bf16)
        derr = from_out + mm(tail * k, dstate_b)
        yield
        dright = mm_tn(t, derr)
        yield
        dright_b = dright.astype(bf16)
        da = jnp.where(rows > cols, mm_nt(dright_b, err_b) * ratio, 0.0) * (-beta)
        da_b = da.astype(bf16)
        back = (beta * grow) * dright
        back_b = back.astype(bf16)
        ds_ref[h] = jnp.exp(end) * dstate + mm_tn(grow * q, dout) - mm_tn(kb, back_b)
        yield
        dk_read = mm(da_b, kb) - mm_nt(back_b, state_b)
        dk_tail = tail * mm_nt(err_b, dstate_b)
        dk_write = mm_tn(dp_b, qb) + mm_tn(da_b, kb) + dk_tail
        dk = dk_read + dk_write
        dv = beta * dright
        to_beta = (1.0 - beta) * jnp.sum(dright * err, axis=1, keepdims=True)
        to_decay = jnp.sum(q * dq + k * (dk_read - dk_write), axis=1, keepdims=True)
        at_end = jnp.exp(end) * jnp.sum(
            jnp.sum(state * dstate, axis=1, keepdims=True), axis=0, keepdims=True
        ) + jnp.sum(jnp.sum(k * dk_tail, axis=1, keepdims=True), axis=0, keepdims=True)
        to_decay = to_decay + jnp.where(row_at == ROWS - 1, at_end, 0.0)
        found[s, h] = (to_decay, to_beta)
        yield
        along = jnp.sum(wu * dq, axis=1, keepdims=True)
        du = (KEY**-0.5) * (ru * dq - wu * (ru * ru * ru * along))
        gs_ref[at, qs : qs + KEY] = du * (su * (1.0 + u * (1.0 - su)))
        along = jnp.sum(wy * dk, axis=1, keepdims=True)
        dy = ry * dk - wy * (ry * ry * ry * along)
        gs_ref[at, ks : ks + KEY] = dy * (sy * (1.0 + y * (1.0 - sy)))
        gs_ref[at, vs : vs + VAL] = dv * (sx * (1.0 + x * (1.0 - sx)))

    def in_step(steps, count=None):
        while steps and count != 0:
            steps = [one for one in steps if next(one, steps) is not steps]
            count = None if count is None else count - 1
        return steps

    every = [tokens_of(s, h) for s in reversed(range(span // ROWS)) for h in range(heads)]
    every = in_step(every, 5)
    started = {s: every[i * heads : (i + 1) * heads] for i, s in enumerate(reversed(range(span // ROWS)))}
    for s in reversed(range(span // ROWS)):
        at = slice(s * ROWS, (s + 1) * ROWS)
        ab, log_decay = ab_ref[at, :], terms[s][0]
        drunning = jnp.zeros((ROWS, 128), f32)
        dbeta = jnp.zeros((ROWS, 128), f32)
        in_step(started[s])
        for h in range(heads):
            drunning = jnp.where(lane == h, found[s, h][0], drunning)
            dbeta = jnp.where(lane == heads + h, found[s, h][1], dbeta)
        dlog = mm_full((rows <= cols).astype(f32), drunning)
        dalpha = -dlog * par[0:1, :] * sigmoid(ab + par[1:2, :])
        dproj_ref[placed_rows(order_ref, s), width + heads * VAL :] = jnp.where(lane < heads, dalpha, dbeta).astype(bf16)
        dpar_ref[0:8, :] += jnp.sum((dlog * log_decay).reshape(-1, 8, 128), axis=0)
        dpar_ref[8:16, :] += jnp.sum(dalpha.reshape(-1, 8, 128), axis=0)

    for lo in range(0, width, 256):
        lanes = slice(lo, lo + 256)
        here = xs_ref[HALO : HALO + span, lanes]
        total = jnp.zeros((span, 256), f32)
        for i in range(4):
            grad = gs_ref[3 - i : 3 - i + span, lanes]
            dtaps_ref[8 * i : 8 * i + 8, lanes] += jnp.sum((here * grad).reshape(-1, 8, 256), axis=0)
            total = total + taps_ref[i : i + 1, lanes] * grad
        total = total.astype(bf16)
        for s in range(2):
            dproj_ref[placed_rows(order_ref, s), lanes] = total[s * ROWS : (s + 1) * ROWS]

    @pl.when(step == last)
    def _():
        head_row = lax.broadcasted_iota(jnp.int32, (8, width), 0)
        for i in range(3):
            moved = gs_ref[0:8, :] * xs_ref[HALO - 3 + i : HALO + 5 + i, :]
            dtaps_ref[8 * i : 8 * i + 8, :] += jnp.where(head_row < 3 - i, moved, 0.0)

    dproj_ref[:, width : width + heads * VAL] = gate_ref[...]

    @pl.when(step == last)
    def _():
        dhead_ref[...] = gs_ref[0:8, :]


def delta_backward(order, dgate, proj, edge, taps, ab, par, dout, inverse, states, entering, dfinal):
    tokens, width = proj.shape
    heads = width // (2 * KEY + VAL)
    keys, vals = heads * KEY, heads * VAL
    subs = sub_blocks(heads)
    span = subs * ROWS
    blocks = tokens // span
    whole = lambda *shape: pl.BlockSpec(shape, lambda c, order: (0,) * len(shape))
    rev = lambda w: pl.BlockSpec((span, w), lambda c, order: (blocks - 1 - c, 0))
    sent = lambda w: pl.BlockSpec((span, w), lambda c, order: (order[blocks + blocks - 1 - c], 0))
    per = span // HALO
    return pl.pallas_call(
        functools.partial(backward_kernel, heads),
        grid_spec=pltpu.PrefetchScalarGridSpec(
            num_scalar_prefetch=1,
            grid=(blocks,),
            in_specs=[
                sent(vals),
                rev(width),
                pl.BlockSpec((HALO, width), lambda c, order: (jnp.maximum((blocks - 1 - c) * per - 1, 0), 0)),
                whole(HALO, width),
                whole(8, width),
                rev(128),
                whole(8, 128),
                rev(vals),
                rev(keys),
                pl.BlockSpec((subs, heads, KEY, VAL + KEY), lambda c, order: (blocks - 1 - c, 0, 0, 0)),
                whole(heads, KEY, VAL),
                whole(heads, KEY, VAL),
            ],
            out_specs=[
                sent(width + vals + 128),
                whole(32, width),
                whole(16, 128),
                whole(8, width),
            ],
            scratch_shapes=[
                pltpu.VMEM((HALO + span, width), f32),
                pltpu.VMEM((span + 8, width), f32),
                pltpu.VMEM((heads, KEY, VAL), f32),
            ],
        ),
        out_shape=[
            jax.ShapeDtypeStruct((tokens, width + vals + 128), bf16),
            jax.ShapeDtypeStruct((32, width), f32),
            jax.ShapeDtypeStruct((16, 128), f32),
            jax.ShapeDtypeStruct((8, width), f32),
        ],
        compiler_params=pltpu.CompilerParams(
            dimension_semantics=("arbitrary",), vmem_limit_bytes=56 * 2**20
        ),
    )(order, dgate, proj, proj, edge, taps, ab, par, dout, inverse, states, entering, dfinal)


def assemble_kernel(parts, *refs):
    out_ref, sems = refs[-2], refs[-1]
    copies, at = [], 0
    for i, (which, start, rows) in enumerate(parts):
        copies.append(pltpu.make_async_copy(
            refs[which].at[pl.ds(start, rows)], out_ref.at[pl.ds(at, rows)], sems.at[i]))
        at += rows
    for copy in copies:
        copy.start()
    for copy in copies:
        copy.wait()


def assembled(pieces, parts):
    rows = sum(p[2] for p in parts)
    return pl.pallas_call(
        functools.partial(assemble_kernel, parts),
        in_specs=[pl.BlockSpec(memory_space=pltpu.VMEM)] * len(pieces),
        out_specs=pl.BlockSpec(memory_space=pl.ANY),
        out_shape=jax.ShapeDtypeStruct((rows,) + pieces[0].shape[1:], pieces[0].dtype),
        scratch_shapes=[pltpu.SemaphoreType.DMA((len(parts),))],
        compiler_params=pltpu.CompilerParams(vmem_limit_bytes=32 * 2**20),
    )(*pieces)


def dot_rows(a, b):
    return lax.dot_general(a, b, (((1,), (0,)), ((), ())), preferred_element_type=f32)


def dot_left(a, b):
    return lax.dot_general(a, b, (((0,), (0,)), ((), ())), preferred_element_type=f32)


def dot_right(a, b):
    return lax.dot_general(a, b, (((1,), (1,)), ((), ())), preferred_element_type=f32)


def batched(a, b):
    return lax.dot_general(a, b, (((2,), (1,)), ((0,), (0,))), preferred_element_type=f32)


def batched_t(a, b):
    return lax.dot_general(a, b, (((1,), (1,)), ((0,), (0,))), preferred_element_type=f32)


def tie(first, *then):
    return lax.optimization_barrier((first, *then))[0] if then else first


def fold_of():
    return 2 if lax.axis_size("seq") == 8 and lax.axis_size("head") == 4 else 1


def lines_of():
    fold = fold_of()
    return [list(range(x, lax.axis_size("seq"), fold)) for x in range(fold)]


def side_of():
    return lax.axis_index("seq") % fold_of()


def swap_pair(v):
    return lax.ppermute(v, "seq", [(i, i ^ 1) for i in range(lax.axis_size("seq"))])


def swap_chip(v):
    return lax.ppermute(v, "head", [(i, i ^ 2) for i in range(4)])


def swap_core(v):
    return lax.ppermute(v, "head", [(i, i ^ 1) for i in range(4)])


def pick(v, at, axis=0):
    half = v.shape[axis] // 2
    return lax.dynamic_slice_in_dim(v, at * half, half, axis)


def join(at, mine, other, axis=0):
    first, second = jnp.where(at == 0, mine, other), jnp.where(at == 0, other, mine)
    return jnp.concatenate([first, second], axis=axis)


def plus(a, b):
    return (a.astype(f32) + b.astype(f32)).astype(bf16)


def place_of():
    core, chip = lax.axis_index("head") % 2, lax.axis_index("head") // 2
    return core, chip, side_of()


def unit_order(count):
    if fold_of() == 1:
        same = [jnp.int32(i) for i in range(count)]
        return same, same, jnp.int32(0)
    core, chip, side = place_of()
    bits = [(i // 4, i // 2 % 2, i % 2) for i in range(8)]
    at_place = [((s ^ side) * 4 + (c ^ core) * 2 + kind).astype(jnp.int32) for c, kind, s in bits]
    of_unit = [((c ^ core) * 4 + kind * 2 + (s ^ side)).astype(jnp.int32) for s, c, kind in bits]
    return at_place, of_unit, chip.astype(jnp.int32)


def chip_sum(away, near):
    if fold_of() == 1:
        return jnp.concatenate([near, away], axis=0).astype(bf16)
    return plus(lax.optimization_barrier(near.astype(bf16)), swap_core(away.astype(bf16)))


def together(*arrays):
    return lax.optimization_barrier(arrays)


def first_exchange(mine):
    if fold_of() == 1:
        return (mine,)
    n = mine.shape[0] // 8
    blocks = [mine[i * n : (i + 1) * n] for i in range(8)]
    keep, give = (jnp.concatenate([blocks[4 + i], blocks[6 + i]], axis=0) for i in range(2))
    by_x, by_y = together(mine[2 * n : 4 * n], give)
    return mine[: 2 * n], keep, swap_pair(by_x), swap_chip(by_y)


def first_total(parts, *beside):
    if fold_of() == 1:
        return parts
    a, b, far_a, far_b = together(*parts, *beside)[:4]
    return together(plus(a, far_a), plus(b, far_b))


def second_exchange(parts):
    if fold_of() == 1:
        return parts
    a, b = parts
    n = a.shape[0] // 2
    return a[:n], b[:n], swap_chip(a[n:]), swap_pair(b[n:])


def second_total(parts, *beside):
    if fold_of() == 1:
        return [lax.psum(parts[0], "head")]
    a, b, far_a, far_b = together(*parts, *beside)[:4]
    return list(together(plus(a, far_a), plus(b, far_b)))


def all_rows(pieces, beside=(), work=None):
    if fold_of() == 1:
        return pieces[0], () if work is None else work(pieces[0])
    a, b = together(*pieces)
    far_a, far_b = together(swap_chip(a), swap_pair(b), *beside)[:2]
    a, b = together(jnp.concatenate([a, far_a], axis=0), jnp.concatenate([b, far_b], axis=0))
    done = () if work is None else work(a)
    far_a, far_b, *done = together(swap_pair(a), swap_chip(b), *done)
    n = far_b.shape[0] // 2
    near = together(a, far_a, b, far_b)
    far = together(*(swap_core(v) for v in near))
    parts = []
    for at in (0, 4):
        parts += [(at, 0, 2 * n), (at + 1, 0, 2 * n)]
        parts += [(at + 2, 0, n), (at + 3, 0, n), (at + 2, n, n), (at + 3, n, n)]
    return assembled(near + far, tuple(parts)), tuple(done)


def chip_rows(pieces):
    if fold_of() == 1:
        return pieces
    a, b = pieces
    both_here = jnp.concatenate([a, b], axis=0)
    return both_here, swap_chip(both_here)


def own_tokens(parts, *beside):
    if fold_of() == 1:
        return parts[0]
    core, chip, _ = place_of()
    here, far = together(*parts, *beside)[:2]
    n = here.shape[0] // 2
    near = jnp.concatenate([join(chip, here[:n], far[:n]), join(chip, here[n:], far[n:])], axis=0)
    return join(core, near, swap_core(near))


def own_blocks(v):
    if fold_of() == 1:
        return [v]
    core, chip, _ = place_of()
    n = v.shape[0] // 8
    return [lax.dynamic_slice_in_dim(v, core * 4 * n + kind * 2 * n + chip * n, n) for kind in range(2)]


def line_total(v):
    fold, step = fold_of(), fold_of()
    while step < lax.axis_size("seq"):
        v = v + lax.ppermute(v, "seq", [(i, i ^ step) for i in range(lax.axis_size("seq"))])
        step *= 2
    return v


def shards_of(v):
    count, step = lax.axis_size("seq"), 1
    held = v[None]
    while step < count:
        held = jnp.concatenate(
            [held, lax.ppermute(held, "seq", [(i, i ^ step) for i in range(count)])], axis=0
        )
        step *= 2
    me = lax.axis_index("seq")
    return jnp.concatenate([lax.dynamic_slice_in_dim(held, me ^ i, 1) for i in range(count)], axis=0)


def pair_rows(v, *after):
    if fold_of() == 1:
        return v
    core = lax.axis_index("head") % 2
    got = tie(swap_pair(pick(v, core)), *after)
    return join(side_of(), v, join(core, got, swap_core(got)))


def my_part(v):
    if fold_of() == 1:
        return v, None
    half = v.shape[0] // 2
    at = side_of()
    return jnp.where(at == 0, v[:half], v[half:]), jnp.where(at == 0, v[half:], v[:half])


def side_parts(masters):
    parts = [my_part(m.astype(bf16)) for m in masters]
    mine = jnp.concatenate([p[0] for p in parts], axis=0)
    if fold_of() == 2:
        away = jnp.concatenate([p[1] for p in parts], axis=0)
        mine = join(side_of(), mine, swap_pair(away), axis=1)
    return mine


def gathered(mine):
    return lax.all_gather(mine, "seq", axis=1, tiled=True, axis_index_groups=lines_of())


def line_scatter(grad, axis=1):
    return lax.psum_scatter(grad, "seq", scatter_dimension=axis, tiled=True, axis_index_groups=lines_of())


def swapped_share(summed, axis=1):
    return swap_pair(pick(summed, 1 - side_of(), axis)) if fold_of() == 2 else None


def in_sides(summed, other, axis=1):
    if fold_of() == 1:
        return [summed.astype(f32)]
    at = side_of()
    mine = pick(summed, at, axis)
    return [jnp.where(at == 0, mine, other).astype(f32), jnp.where(at == 0, other, mine).astype(f32)]


def both(sides, lo, hi):
    return jnp.concatenate([s[lo:hi] for s in sides], axis=0)


def states_in(final):
    fold, count = fold_of(), lax.axis_size("seq")
    onward = [(i, i + fold) for i in range(count - fold)]
    bias, move = final[:, :, :VAL], final[:, :, VAL:].astype(bf16)
    state = jnp.zeros_like(bias).astype(bf16)
    for hop in range(count // fold - 1):
        sent = bias if hop == 0 else batched(move, state) + bias
        state = lax.ppermute(sent.astype(bf16), "seq", onward)
    return state, jnp.swapaxes(move, 1, 2)


def states_back(local, turned, works):
    fold, count = fold_of(), lax.axis_size("seq")
    onward = [(i + fold, i) for i in range(count - fold)]
    sent, carried = local.astype(bf16), ()
    for hop in range(count // fold - 1):
        if hop:
            sent = (batched(turned, state) + local).astype(bf16)
        state = lax.ppermute(sent, "seq", onward)
        if hop < len(works):
            carried = works[hop](sent, carried)
        state, *carried = together(state, *carried)
    return state.astype(f32), carried


def on_device(
    tokens, cotangent, norm1_gain, w_query, w_key, w_value, w_gate_out, w_alpha, w_beta,
    conv_query, conv_key, conv_value, a_log, dt_bias, out_gain, w_out, norm2_gain, w_gate, w_up, w_down,
):
    fold, side = fold_of(), side_of()
    shards = lax.axis_size("seq")
    model = tokens.shape[1]
    share = model // shards
    all_heads = w_alpha.shape[1]
    heads = all_heads // fold
    hidden = w_gate.shape[1] // fold
    keys, vals = heads * KEY, heads * VAL
    width = 2 * keys + vals
    head_at = lax.axis_index("head") * all_heads + side * heads

    proj_parts = side_parts([w_query.T, w_key.T, w_value.T])
    proj_weight = gathered(proj_parts)
    mid_weight = gathered(side_parts([w_gate_out.T, w_out]))
    gate_weight, out_weight = mid_weight[:vals], mid_weight[vals:]
    mlp_in = gathered(side_parts([w_gate.T, w_up.T]))
    mlp_down = gathered(side_parts([w_down]))

    small = [norm1_gain, norm2_gain, w_alpha, w_beta, conv_query, conv_key, conv_value, a_log, dt_bias, out_gain]
    flat = jnp.concatenate([s.astype(bf16).reshape(-1) for s in small])
    flat = shards_of(jnp.pad(flat, (0, -flat.shape[0] % 1024))).astype(f32)
    parts, at = [], 0
    for s in small:
        parts.append(flat[:, at : at + s.size].reshape((shards,) + s.shape))
        at += s.size
    gain_first, gain_second = parts[0].reshape(-1), parts[1].reshape(-1)
    of_side = lambda v, axis: lax.dynamic_slice_in_dim(v, side * heads, heads, axis)
    mix_weight = jnp.concatenate(
        [of_side(parts[2].reshape(model, all_heads), 1), of_side(parts[3].reshape(model, all_heads), 1)], axis=1
    )
    mix_weight = jnp.pad(mix_weight, ((0, 0), (0, 128 - 2 * heads))).astype(bf16)
    taps = jnp.concatenate(
        [of_side(jnp.moveaxis(p, 0, 2).reshape(4, all_heads, -1), 1).reshape(4, -1) for p in parts[4:7]], axis=1
    )
    taps = jnp.pad(taps, ((0, 4), (0, 0)))
    rate = lax.dynamic_slice_in_dim(parts[7].reshape(-1), head_at, heads)
    bias = lax.dynamic_slice_in_dim(parts[8].reshape(-1), head_at, heads)
    gain_out = parts[9].reshape(1, -1)
    par = jnp.pad(jnp.stack([jnp.exp(rate), bias]), ((0, 6), (0, 128 - heads)))

    inputs = pair_rows(tie(tokens, proj_parts)).astype(f32)
    row_count = inputs.shape[0]
    scale_first = lax.rsqrt(jnp.mean(inputs * inputs, axis=1, keepdims=True) + eps_norm)
    normed_first = (inputs * scale_first * gain_first).astype(bf16)
    proj = dot_right(normed_first, proj_weight).astype(bf16)
    mix_pre = dot_rows(normed_first, mix_weight)
    forward = [(i, i + fold) for i in range(shards - fold)]
    backward = [(i + fold, i) for i in range(shards - fold)]
    edge = lax.ppermute(proj[row_count - HALO :], "seq", forward)
    value_out, ident, inverse, states, final = delta_forward(proj, edge, taps, mix_pre, par)
    gate_pre = dot_right(normed_first, gate_weight)
    entering, move = states_in(final)
    order = unit_order(row_count // UNIT)
    places = jnp.stack(order[0] + order[1] + [order[2]])
    both_cot = pair_rows(tie(cotangent, proj), final)
    both_cot, turned_first = reordered(places, both_cot, normed_first)
    mix_turned = mix_weight.T
    side_weight = jnp.concatenate(
        [tie(proj_weight, both_cot), tie(gate_weight, both_cot), tie(mix_turned, both_cot)], axis=0
    )
    entering = tie(entering, both_cot)
    outputs, gated = gated_outputs(places, value_out, ident, entering, gate_pre, gain_out)
    half = row_count // 2
    mine = chip_sum(dot_rows(gated[half:], out_weight), dot_rows(gated[:half], out_weight))
    attention = second_total(second_exchange(first_total(first_exchange(mine), mlp_in)))
    own_inputs = own_blocks(tokens)
    hidden_state = [x.astype(f32) + v.astype(f32) for x, v in zip(own_inputs, attention)]
    scale_second = [lax.rsqrt(jnp.mean(v * v, axis=1, keepdims=True) + eps_norm) for v in hidden_state]
    hat_second = [v * r for v, r in zip(hidden_state, scale_second)]
    normed_second, (mlp_down,) = all_rows(
        [(v * gain_second).astype(bf16) for v in hat_second], (), lambda after: (mlp_down,)
    )
    act = dot_right(mlp_in, normed_second)
    gate_act, up_act = act[:hidden], act[hidden:]
    sig = jax.nn.sigmoid(gate_act)
    mixed = (gate_act * sig * up_act).astype(bf16)
    grad_mixed = dot_right(mlp_down, both_cot)
    grad_act = jnp.concatenate(
        [grad_mixed * up_act * sig * (1.0 + gate_act * (1.0 - sig)), grad_mixed * (gate_act * sig)], axis=0
    ).astype(bf16)
    mine = chip_sum(dot_left(grad_act[:, half:], mlp_in), dot_left(grad_act[:, :half], mlp_in))
    down_grad = dot_rows(tie(mixed, mine), both_cot).astype(bf16)
    in_grad = dot_rows(tie(grad_act, down_grad), normed_second).astype(bf16)
    down_sum = line_scatter(down_grad)
    in_sum = line_scatter(tie(in_grad, down_sum))
    grad_normed_second = first_total(first_exchange(mine), down_grad, in_grad)
    grad_normed_second = second_total(second_exchange(grad_normed_second))
    grad_hidden = []
    for d, v, hat, r in zip(own_blocks(cotangent), grad_normed_second, hat_second, scale_second):
        g = v.astype(f32) * gain_second
        grad_hidden.append(d.astype(f32) + r * (g - hat * jnp.mean(g * hat, axis=1, keepdims=True)))
    attention_rounded = [v.astype(bf16) for v in grad_hidden]
    gain_part = sum(
        jnp.sum(v.astype(f32) * hat, axis=0) for v, hat in zip(grad_normed_second, hat_second)
    )

    if fold == 1:
        gain_part = gain_part / lax.axis_size("head")

    def branch_beside(after):
        m = tie(mixed, after, down_sum)
        return (chip_sum(dot_left(m[:, half:], mlp_down), dot_left(m[:, :half], mlp_down)),)

    attention_rounded, (branch,) = all_rows(attention_rounded, (), branch_beside)
    branch, attention_rounded = together(branch, attention_rounded)
    branch = first_exchange(branch)
    grad_gated = dot_right(attention_rounded, out_weight).astype(bf16)
    grad_outputs, grad_gate, grad_gain_out, local_pull = gate_backward(
        places, grad_gated, outputs, gate_pre, gain_out, ident
    )

    line_in = in_sum

    def first_work(sent, carried):
        parts = first_total(branch, sent)
        return dot_left(gated, tie(attention_rounded, parts[0])).astype(bf16), *parts

    def second_work(sent, carried):
        parts = second_exchange(tuple(carried[1:]))
        return carried[0], dot_left(tie(grad_gate, sent), turned_first).astype(bf16), *parts

    def third_work(sent, carried):
        parts = second_total(tuple(carried[2:]))
        rows = [(v + w.astype(f32)).astype(bf16) for v, w in zip(hidden_state, parts)]
        return jnp.concatenate(carried[:2], axis=0), line_in, *rows

    leaving, (mid_grad, in_sum, *result) = states_back(local_pull, move, (first_work, second_work, third_work))
    leaving, mid_grad, down_sum, *result = together(leaving, mid_grad, down_sum, *result)
    result = chip_rows(result)
    in_other, down_other = swapped_share(in_sum), swapped_share(down_sum)
    mid_sum = line_scatter(tie(mid_grad, in_sum))
    grad_side, grad_taps, grad_par, grad_head = delta_backward(
        places, grad_gate, proj, edge, taps, mix_pre, par, grad_outputs, inverse, states, entering, leaving
    )
    following = lax.ppermute(grad_head, "seq", backward)
    fixes = []
    for s in range(3):
        fixes.append(sum(taps[3 - j] * following[s - 3 + j] for j in range(3 - s, 4)))
    at_end = order[1][-1] * UNIT + (1 ^ order[2]) * ROWS + ROWS - HALO
    if fold == 2:
        grad_side, in_other, down_other, *result = together(grad_side, in_other, down_other, *result)
    ending = lax.dynamic_slice(grad_side, (at_end, 0), (HALO, width)).astype(f32)
    ending = (ending + jnp.pad(jnp.stack(fixes), ((HALO - 3, 0), (0, 0)))).astype(bf16)
    grad_side = lax.dynamic_update_slice(grad_side, ending, (at_end, 0))
    proj_grad = dot_left(turned_first, grad_side[:, :width]).astype(bf16)
    last_sum = line_scatter(proj_grad, 0)
    away = dot_rows(tie(grad_side, proj_grad, mid_sum)[half:], side_weight).astype(bf16)
    near = dot_rows(tie(grad_side, away)[:half], side_weight)
    mine = chip_sum(away, near)
    grad_normed_first = first_exchange(mine)
    in_sum, down_sum, mid_sum, grad_taps, grad_par, grad_side, proj_grad = (
        tie(v, mine) for v in (in_sum, down_sum, mid_sum, grad_taps, grad_par, grad_side, proj_grad)
    )
    taps_sum = jnp.sum(grad_taps.reshape(4, 8, width), axis=1)
    par_sum = jnp.sum(grad_par.reshape(2, 8, 128), axis=1)
    every = jnp.zeros((2, shards * a_log.shape[0]), f32)
    every = lax.dynamic_update_slice(every, par_sum[:, :heads], (0, head_at))
    mix_grad = dot_left(grad_side[:, width + vals :], turned_first)
    few = jnp.concatenate([every.reshape(1, -1), jnp.sum(grad_gain_out, axis=0).reshape(1, -1)], axis=1)
    fill = lambda v: jnp.pad(v, ((0, 0), (0, model - v.shape[1])))
    extra = jnp.concatenate([gain_part[None], fill(few), mix_grad[: 2 * heads], fill(taps_sum)], axis=0)
    extra = jnp.pad(extra, ((0, -extra.shape[0] % 8), (0, 0)))
    grad_down, grad_in = in_sides(down_sum, down_other), in_sides(in_sum, in_other)
    ready = (
        both(grad_in, 0, hidden).T, both(grad_in, hidden, 2 * hidden).T, both(grad_down, 0, hidden),
    )
    step = lambda v, by: lax.ppermute(v, "seq", [(i, i ^ by) for i in range(shards)])
    if fold == 2:
        far_a, far_b, extra, *ready = together(*grad_normed_first[2:], extra, *ready)
        grad_normed_first = first_total((*grad_normed_first[:2], far_a, far_b))
        far_extra = step(tie(extra, grad_normed_first[0]), 2)
        own_result = own_tokens([tie(v, grad_normed_first[0]) for v in result])
        grad_normed_first = second_total(second_exchange(grad_normed_first), far_extra, own_result)
        extra = extra + tie(far_extra, grad_normed_first[0])
    else:
        own_result = own_tokens(result)
        grad_normed_first, extra = second_total(grad_normed_first), line_total(extra)
    after = grad_normed_first[0]
    grad_tokens, gain_row = [], 0.0
    for x, d, v in zip(own_inputs, grad_hidden, grad_normed_first):
        x, v = x.astype(f32), v.astype(f32)
        r = lax.rsqrt(jnp.mean(x * x, axis=1, keepdims=True) + eps_norm)
        hat = x * r
        g = v * gain_first
        gain_row = gain_row + jnp.sum(v * hat, axis=0, keepdims=True)
        grad_tokens.append((d + r * (g - hat * jnp.mean(g * hat, axis=1, keepdims=True))).astype(bf16))
    grad_tokens = chip_rows(grad_tokens)
    mid_other = swapped_share(tie(mid_sum, after))
    if fold == 2:
        far_extra, far_row = step(extra, 4), step(gain_row, 2)
        *grad_tokens, far_extra, far_row, last_sum = together(*grad_tokens, far_extra, far_row, last_sum)
        extra, gain_row = extra + far_extra, gain_row + far_row
        last_other, other, far_row = swap_pair(pick(last_sum, 1 - side, 0)), swap_pair(extra), step(gain_row, 4)
        grad_tokens = own_tokens(grad_tokens).astype(f32)
        gain_row = gain_row + far_row
        gain_row = gain_row + swap_pair(gain_row)
        sides = [jnp.where(side == 0, extra, other), jnp.where(side == 0, other, extra)]
        shared = jnp.concatenate([gain_row, extra[:2] + other[:2]], axis=0)
        shared = shared + swap_core(shared)
        shared = shared + swap_chip(shared)
    else:
        last_other, sides = None, [extra]
        grad_tokens = own_tokens(grad_tokens).astype(f32)
        gain_row = line_total(gain_row) / lax.axis_size("head")
        shared = lax.psum(jnp.concatenate([gain_row, extra[:2]], axis=0), "head")
    result = own_result
    me = lax.axis_index("seq")
    take = lambda v, at, n: lax.dynamic_slice_in_dim(v, at, n, v.ndim - 1)
    grad_alpha = jnp.concatenate([take(v[2 : 2 + heads], me * share, share) for v in sides], axis=0).T
    grad_beta = jnp.concatenate([take(v[2 + heads : 2 + 2 * heads], me * share, share) for v in sides], axis=0).T
    filters = []
    for like, lo, size in ((conv_query, 0, KEY), (conv_key, keys, KEY), (conv_value, 2 * keys, VAL)):
        n = like.shape[2]
        filters.append(jnp.stack(
            [take(v[2 + 2 * heads : 6 + 2 * heads], lo + h * size + me * n, n) for v in sides for h in range(heads)],
            axis=1,
        ))
    n_rate, n_gain = a_log.shape[0], out_gain.shape[0]
    few = shared[2]
    grad_mid, grad_last = in_sides(mid_sum, mid_other), in_sides(last_sum, last_other, 0)
    channels = lambda lo, hi: jnp.concatenate([v[:, lo:hi] for v in grad_last], axis=1)

    return (
        result,
        grad_tokens,
        take(shared[0], me * share, share),
        channels(0, keys),
        channels(keys, 2 * keys),
        channels(2 * keys, width),
        both(grad_mid, vals, 2 * vals).T,
        grad_alpha,
        grad_beta,
        filters[0],
        filters[1],
        filters[2],
        take(few, me * n_rate, n_rate),
        take(few, (shards + me) * n_rate, n_rate),
        take(few, 2 * shards * n_rate + me * n_gain, n_gain),
        both(grad_mid, 0, vals),
        take(shared[1], me * share, share),
        *ready,
    )


def solution(mesh):
    P = jax.sharding.PartitionSpec
    rows, vector, filters, turned = P("seq", None), P("seq"), P(None, "head", "seq"), P("head", "seq")
    matrix = P("seq", "head")
    placed = (rows, rows, vector) + (matrix,) * 6 + (filters,) * 3 + (vector,) * 3 + (
        turned, vector, matrix, matrix, turned)
    return jax.shard_map(
        on_device, mesh=mesh, in_specs=placed, out_specs=placed, check_vma=False
    )
```
